32 devices in a mesh: img: 4 (over y, x), band: 8 (over z, core).
Axes of the slice: x: 2, y: 2, z: 4, core: 2. Of those that a mesh axis runs over, the one named last changes fastest.
Arguments:
- patches: bfloat16 [16, 2048, 768], P('img', 'band'), may hold values from -6 to 6
- cotangent: bfloat16 [16, 2048, 768], P('img', 'band')
- valid_counts: int32 [16], P('img'), may hold values from 512 to 2048, as said below
- qkv_master: float32 [768, 2304], P(('img', 'band')), may hold values from -0.21875 to 0.21875
- out_master: float32 [768, 768], P(None, ('img', 'band')), may hold values from -1.75 to 1.75
- in_master: float32 [768, 4096], P(('img', 'band')), may hold values from -0.21875 to 0.21875
- down_master: float32 [2048, 768], P(None, ('img', 'band')), may hold values from -0.125 to 0.125
- gain_master: float32 [2, 768], P(None, ('img', 'band'))
- qkv_first: float32 [768, 2304], P(('img', 'band')), may hold values from -0.00024414062 to 0.00024414062
- out_first: float32 [768, 768], P(None, ('img', 'band')), may hold values from -0.00024414062 to 0.00024414062
- in_first: float32 [768, 4096], P(('img', 'band')), may hold values from -0.00024414062 to 0.00024414062
- down_first: float32 [2048, 768], P(None, ('img', 'band')), may hold values from -0.00024414062 to 0.00024414062
- gain_first: float32 [2, 768], P(None, ('img', 'band')), may hold values from -0.0007324219 to 0.0007324219
- qkv_second: float32 [768, 2304], P(('img', 'band')), may hold values from 1.4128508e-10 to 5.651403e-10
- out_second: float32 [768, 768], P(None, ('img', 'band')), may hold values from 1.4128508e-10 to 5.651403e-10
- in_second: float32 [768, 4096], P(('img', 'band')), may hold values from 1.4128508e-10 to 5.651403e-10
- down_second: float32 [2048, 768], P(None, ('img', 'band')), may hold values from 1.4128508e-10 to 5.651403e-10
- gain_second: float32 [2, 768], P(None, ('img', 'band')), may hold values from 1.2715657e-09 to 5.086263e-09
Outputs:
- output: bfloat16 [16, 2048, 768], P('img', 'band')
- back_input: bfloat16 [16, 2048, 768], P('img', 'band')
- grad_norm: float32 [], replicated
- qkv_new: float32 [768, 2304], P(('img', 'band'))
- out_new: float32 [768, 768], P(None, ('img', 'band'))
- in_new: float32 [768, 4096], P(('img', 'band'))
- down_new: float32 [2048, 768], P(None, ('img', 'band'))
- gain_new: float32 [2, 768], P(None, ('img', 'band'))
- qkv_first_new: float32 [768, 2304], P(('img', 'band'))
- out_first_new: float32 [768, 768], P(None, ('img', 'band'))
- in_first_new: float32 [768, 4096], P(('img', 'band'))
- down_first_new: float32 [2048, 768], P(None, ('img', 'band'))
- gain_first_new: float32 [2, 768], P(None, ('img', 'band'))
- qkv_second_new: float32 [768, 2304], P(('img', 'band'))
- out_second_new: float32 [768, 768], P(None, ('img', 'band'))
- in_second_new: float32 [768, 4096], P(('img', 'band'))
- down_second_new: float32 [2048, 768], P(None, ('img', 'band'))
- gain_second_new: float32 [2, 768], P(None, ('img', 'band'))
- qkv_copy: bfloat16 [768, 2304], P(('img', 'band'))
- out_copy: bfloat16 [768, 768], P(None, ('img', 'band'))
- in_copy: bfloat16 [768, 4096], P(('img', 'band'))
- down_copy: bfloat16 [2048, 768], P(None, ('img', 'band'))
- gain_copy: bfloat16 [2, 768], P(None, ('img', 'band'))
The draws below stay inside these ranges and needn't reach their ends.
Inputs may be any that keep to these rules, and one draw needn't show every extreme that they name: `valid_counts`: each image's valid patches are its first slots; in each aligned group of 4 images one image has all 2048 slots valid.
All inputs are finite; a program needn't handle non-finite values.
Results may differ from the reference program's by a relative error of at most 0.015.
The reference program's roundings to bfloat16 on the way count: a program that leaves them out, or rounds other values in their place, can miss the bound.
Values may be sent and summed in bfloat16 or wider, within the bound.
A program may use at most 256 MiB of HBM per device.

```python
import math
import jax
import jax.numpy as jnp
from jax import lax

D = 768
HEADS = 12
HEAD_DIM = 64
FF = 2048
LEN = 2048
IMG_DEV = 4
STEP = 10
IMAGES = 16
N_IMG = 4
N_BAND = 8
DEVICES = 32


def feature_ramp(rise):
    index = jnp.arange(D, dtype=jnp.int32)
    shard = index // (D // DEVICES)
    along_band = (shard % N_BAND).astype(jnp.float32) / max(N_BAND - 1, 1)
    along_img = (shard // N_BAND).astype(jnp.float32) / max(N_IMG - 1, 1)
    return (1.0 + rise * along_band) * (1.0 + rise * along_img)


def draw_cotangent(key, part):
    key = jax.random.fold_in(key, 11)
    values = jnp.clip(jax.random.normal(key, (IMAGES, LEN, D), jnp.float32), -6.0, 6.0)
    ramp = 0.6 * feature_ramp(0.732)
    return (values * ramp[None, None, :]).astype(jnp.bfloat16)


def draw_gain_master(key, part):
    key = jax.random.fold_in(key, 12)
    rough = 1.0 + 0.15 * jnp.clip(jax.random.normal(key, (2, D), jnp.float32), -2.5, 2.5)
    ramp = 0.6 * feature_ramp(0.732)
    return (rough * ramp[None, :]).astype(jnp.float32)


def draw_valid_counts(key, part):
    key = jax.random.fold_in(key, 13)
    first_key, second_key = jax.random.split(key)
    counts = jax.random.randint(first_key, (IMAGES,), LEN // 4, LEN + 1, jnp.int32)
    chosen = jax.random.randint(second_key, (IMAGES // IMG_DEV,), 0, IMG_DEV, jnp.int32)
    image_ids = jnp.arange(IMAGES, dtype=jnp.int32)
    full_one = image_ids % IMG_DEV == chosen[image_ids // IMG_DEV]
    return jnp.where(full_one, LEN, counts).astype(jnp.int32)


def block_levels(stream_key, dims, cuts, low, top_value):
    loudness, own = 1.0, jax.random.fold_in(stream_key, 6)
    for axis_at, parts in cuts:
        heights = jnp.exp(jax.random.uniform(jax.random.fold_in(own, axis_at), (parts,), jnp.float32, low / len(cuts), top_value / len(cuts)))
        loudness = loudness * jnp.repeat(heights, dims[axis_at] // parts).reshape([-1 if axis == axis_at else 1 for axis in range(len(dims))])
    return loudness


def gaussian(key, shape, scale, reach, shards=(), held_as=jnp.bfloat16):
    values = scale * jax.random.normal(key, shape, jnp.float32)
    if shards:
        values = values * block_levels(key, shape, shards, -0.22, 0.18)
    return jnp.clip(values, -reach, reach).astype(held_as)


def setup_inputs(seed: int = 0) -> dict:
    streams_of = jax.random.split(jax.random.key(seed), 19)
    return {
        "patches": gaussian(streams_of[0], (IMAGES, LEN, D), 1.0, 6.0, ((0, 4), (1, 8))),
        "cotangent": draw_cotangent(jax.random.fold_in(streams_of[18], 71), 0),
        "valid_counts": draw_valid_counts(jax.random.fold_in(streams_of[18], 71), 0),
        "qkv_master": gaussian(streams_of[3], (D, 3 * D), D ** -0.5, 0.21875, ((0, 32),), jnp.float32),
        "out_master": gaussian(streams_of[4], (D, D), (D // 64) ** -0.5, 1.75, ((1, 32),), jnp.float32),
        "in_master": gaussian(streams_of[5], (D, 2 * FF), D ** -0.5, 0.21875, ((0, 32),), jnp.float32),
        "down_master": gaussian(streams_of[6], (FF, D), FF ** -0.5, 0.125, ((1, 32),), jnp.float32),
        "gain_master": draw_gain_master(jax.random.fold_in(streams_of[18], 71), 0),
        "qkv_first": gaussian(streams_of[8], (D, 3 * D), (0.11 / (4 * D * D + 3 * D * FF) ** 0.5), 0.00024414062, ((0, 32),), jnp.float32),
        "out_first": gaussian(streams_of[9], (D, D), (0.11 / (4 * D * D + 3 * D * FF) ** 0.5), 0.00024414062, ((1, 32),), jnp.float32),
        "in_first": gaussian(streams_of[10], (D, 2 * FF), (0.11 / (4 * D * D + 3 * D * FF) ** 0.5), 0.00024414062, ((0, 32),), jnp.float32),
        "down_first": gaussian(streams_of[11], (FF, D), (0.11 / (4 * D * D + 3 * D * FF) ** 0.5), 0.00024414062, ((1, 32),), jnp.float32),
        "gain_first": gaussian(streams_of[12], (2, D), (0.33 / (4 * D * D + 3 * D * FF) ** 0.5), 0.0007324219, ((1, 32),), jnp.float32),
        "qkv_second": jnp.clip(jnp.exp(math.log(5.65140323427471e-10) - 1.3862944 * jax.random.uniform(streams_of[13], (D, 3 * D), jnp.float32) ** block_levels(streams_of[13], (D, 3 * D), ((0, 32),), -0.2, 0.2)), 1.4128508085686775e-10, 5.65140323427471e-10),
        "out_second": jnp.clip(jnp.exp(math.log(5.65140323427471e-10) - 1.3862944 * jax.random.uniform(streams_of[14], (D, D), jnp.float32) ** block_levels(streams_of[14], (D, D), ((1, 32),), -0.2, 0.2)), 1.4128508085686775e-10, 5.65140323427471e-10),
        "in_second": jnp.clip(jnp.exp(math.log(5.65140323427471e-10) - 1.3862944 * jax.random.uniform(streams_of[15], (D, 2 * FF), jnp.float32) ** block_levels(streams_of[15], (D, 2 * FF), ((0, 32),), -0.2, 0.2)), 1.4128508085686775e-10, 5.65140323427471e-10),
        "down_second": jnp.clip(jnp.exp(math.log(5.65140323427471e-10) - 1.3862944 * jax.random.uniform(streams_of[16], (FF, D), jnp.float32) ** block_levels(streams_of[16], (FF, D), ((1, 32),), -0.2, 0.2)), 1.4128508085686775e-10, 5.65140323427471e-10),
        "gain_second": jnp.clip(jnp.exp(math.log(5.08626296635839e-09) - 1.3862944 * jax.random.uniform(streams_of[17], (2, D), jnp.float32) ** block_levels(streams_of[17], (2, D), ((1, 32),), -0.2, 0.2)), 1.2715657415895976e-09, 5.08626296635839e-09),
    }


@jax.custom_vjp
def low(v):
    return lax.optimization_barrier(v.astype(jnp.bfloat16)).astype(jnp.float32)

@jax.custom_vjp
def low_back(v):
    return v

def low_keep(v):
    return (low(v), None)

def low_pass(kept, grad):
    return (grad,)

def back_keep(v):
    return (v, None)

def back_low(kept, grad):
    return (low(grad),)
low.defvjp(low_keep, low_pass)
low_back.defvjp(back_keep, back_low)
EPS = 1e-06
NEG = -1000000000.0
SCALE = 0.125
CLIP = 1.0
BETA_ONE = 0.9
BETA_TWO = 0.999
ADAM_EPS = 1e-08
RATES = (0.06, 0.5, 0.06, 0.04, 0.5)
DECAYS = (0.1, 0.1, 0.1, 0.1, 0.0)
HIGHEST = lax.Precision.HIGHEST

def rms_norm(value, gain):
    return value * lax.rsqrt(lax.optimization_barrier(jnp.mean(value * value, -1, keepdims=True)) + EPS) * gain

def gated(gate_part, up_part):
    return jax.nn.gelu(gate_part, approximate=True) * up_part

def adam_step(master, grad, first, second, factor, rate, decay):
    clipped = factor * grad
    first_new = BETA_ONE * first + (1.0 - BETA_ONE) * clipped
    second_new = BETA_TWO * second + (1.0 - BETA_TWO) * clipped * clipped
    corrected = first_new / (1.0 - BETA_ONE ** STEP)
    spread = jnp.sqrt(second_new / (1.0 - BETA_TWO ** STEP)) + ADAM_EPS
    master_new = master - rate * (corrected / spread + decay * master)
    return (master_new, first_new, second_new)

def image_layer(patch_rows, count, qkv_w, out_w, in_w, down_w, gains):
    length = patch_rows.shape[0]
    model_width = patch_rows.shape[1]
    hidden_units = down_w.shape[0]
    valid = jnp.arange(length, dtype=jnp.int32) < count
    keep = valid.astype(jnp.float32)[:, None]
    normed_a = low(rms_norm(patch_rows, gains[0]))
    project = jnp.dot(normed_a, qkv_w, precision=HIGHEST)
    queries = low_back(low(project[:, :model_width])).reshape(length, HEADS, HEAD_DIM)
    keys = low_back(low(project[:, model_width:2 * model_width])).reshape(length, HEADS, HEAD_DIM)
    values = low_back(low(project[:, 2 * model_width:])).reshape(length, HEADS, HEAD_DIM)
    scores = low_back(jnp.einsum('phd,rhd->hpr', queries, keys, precision=HIGHEST) * SCALE)
    scores = jnp.where(valid[None, None, :], scores, NEG)
    highest = lax.optimization_barrier(jnp.max(scores, -1, keepdims=True))
    powers = jnp.exp(scores - highest)
    chances = powers / lax.optimization_barrier(jnp.sum(powers, -1, keepdims=True))
    attended = jnp.einsum('hpr,rhd->phd', low(chances), values, precision=HIGHEST).reshape(length, model_width)
    attended = low_back(low(attended))
    middle = patch_rows + low_back(jnp.dot(attended, out_w, precision=HIGHEST))
    normed_b = low(rms_norm(middle, gains[1]))
    both = jnp.dot(normed_b, in_w, precision=HIGHEST)
    hidden = low(gated(low_back(both[:, :hidden_units]), low_back(both[:, hidden_units:])))
    return keep * (middle + low_back(jnp.dot(hidden, down_w, precision=HIGHEST)))

def reference(patches, cotangent, valid_counts, qkv_master, out_master, in_master, down_master, gain_master, qkv_first, out_first, in_first, down_first, gain_first, qkv_second, out_second, in_second, down_second, gain_second):

    def forward(patch_all, qkv_w, out_w, in_w, down_w, gain_w):
        copies = (low(qkv_w), low(out_w), low(in_w), low(down_w), low(gain_w))

        def one_image(item):
            return image_layer(item[0], item[1], copies[0], copies[1], copies[2], copies[3], copies[4])
        return lax.map(jax.checkpoint(one_image), (patch_all, valid_counts))
    result, back = jax.vjp(forward, patches.astype(jnp.float32), qkv_master, out_master, in_master, down_master, gain_master)
    grads = back(cotangent.astype(jnp.float32))
    weight_grads = grads[1:]
    squares = jnp.float32(0.0)
    for grad in weight_grads:
        squares = squares + jnp.sum(grad * grad)
    grad_norm = jnp.sqrt(squares)
    factor = jnp.minimum(1.0, CLIP / grad_norm)
    masters = (qkv_master, out_master, in_master, down_master, gain_master)
    firsts = (qkv_first, out_first, in_first, down_first, gain_first)
    seconds = (qkv_second, out_second, in_second, down_second, gain_second)
    updated = [adam_step(masters[j], weight_grads[j], firsts[j], seconds[j], factor, RATES[j], DECAYS[j]) for j in range(5)]
    return (result.astype(jnp.bfloat16), grads[0].astype(jnp.bfloat16), grad_norm, updated[0][0], updated[1][0], updated[2][0], updated[3][0], updated[4][0], updated[0][1], updated[1][1], updated[2][1], updated[3][1], updated[4][1], updated[0][2], updated[1][2], updated[2][2], updated[3][2], updated[4][2], updated[0][0].astype(jnp.bfloat16), updated[1][0].astype(jnp.bfloat16), updated[2][0].astype(jnp.bfloat16), updated[3][0].astype(jnp.bfloat16), updated[4][0].astype(jnp.bfloat16))
```

```python
import functools

import jax
import jax.numpy as jnp
from jax import lax
from jax.experimental import pallas as pl
from jax.experimental.pallas import tpu as pltpu
from jax.sharding import PartitionSpec as P

HEADS = 12
HEAD_DIM = 64
PAIR = 2 * HEAD_DIM
STEP = 10
EPS = 1e-06
NEG = -1000000000.0
SCALE = 0.125
CLIP = 1.0
BETA_ONE = 0.9
BETA_TWO = 0.999
ADAM_EPS = 1e-08
RATES = (0.06, 0.5, 0.06, 0.04, 0.5)
DECAYS = (0.1, 0.1, 0.1, 0.1, 0.0)
BF = jnp.bfloat16
F32 = jnp.float32
MESH = pl.DeviceIdType.MESH
ANY = pl.BlockSpec(memory_space=pl.ANY)
MIB = 2**20


class Net:
    def __init__(self, dims, send, recv, local):
        self.dims = dims
        big_y, big_x, big_z, share = dims
        img, band = lax.axis_index("img"), lax.axis_index("band")
        self.y, self.x = img // big_x, img % big_x
        self.z, self.c = band // 2, band % 2
        self.image, self.part = band // share, band % share
        self.images = 2 * big_z // share
        self.send, self.recv, self.local = send, recv, local
        self.used, self.used_local = 0, 0

    def device(self, y, x, z, c):
        return (y * self.dims[1] + x, z * 2 + c)

    def line(self, name):
        size = dict(zip("yxz", self.dims))[name] if name in "yxz" else 2
        places = []
        for d in range(1, size):
            at = dict(y=self.y, x=self.x, z=self.z, c=self.c)
            at[name] = lax.rem(at[name] + d, size)
            places.append((at[name], self.device(**at)))
        return places

    def holders(self):
        img = lax.axis_index("img")
        places = []
        for d in range(1, self.images):
            other = lax.rem(self.image + d, self.images)
            places.append((other, (img, other * self.dims[3] + self.part)))
        return places

    def sharers(self):
        img = lax.axis_index("img")
        places = []
        for d in range(1, self.dims[3]):
            other = lax.rem(self.part + d, self.dims[3])
            places.append((other, (img, self.image * self.dims[3] + other)))
        return places

    def greet(self, kinds):
        barrier = pltpu.get_barrier_semaphore()
        count = 0
        for kind in kinds:
            if kind == "image":
                places = self.holders()
            elif kind == "share":
                places = self.sharers()
            else:
                places = self.line(kind)
            for _, target in places:
                pl.semaphore_signal(barrier, inc=1, device_id=target, device_id_type=MESH)
            count += len(places)
        pl.semaphore_wait(barrier, count)

    def copy(self, source, target_ref, target):
        at = self.used
        self.used += 1
        made = pltpu.make_async_remote_copy(
            src_ref=source,
            dst_ref=target_ref,
            send_sem=self.send.at[at],
            recv_sem=self.recv.at[at],
            device_id=target,
            device_id_type=MESH,
        )
        made.start()
        return made

    def local_copy(self, source, target_ref):
        made = pltpu.make_async_copy(source, target_ref, self.local.at[self.used_local])
        self.used_local += 1
        made.start()
        return made


def drive(tasks):
    waiting = list(tasks)
    turn = 0
    while waiting:
        left = []
        for start, task in waiting:
            if start <= turn:
                try:
                    next(task)
                except StopIteration:
                    continue
            left.append((start, task))
        waiting = left
        turn += 1


def exchange_images(net, source, target):
    moves = [net.copy(source.at[other], target.at[net.image], dev) for other, dev in net.holders()]
    own = net.local_copy(source.at[net.image], target.at[net.image])
    yield
    yield
    yield
    yield
    for move in moves:
        move.wait_recv()
    own.wait()
    for move in moves:
        move.wait_send()


def exchange_shares(net, source, target):
    moves = [net.copy(source, target.at[net.part], dev) for _, dev in net.sharers()]
    own = net.local_copy(source, target.at[net.part])
    yield
    for move in moves:
        move.wait_recv()
    own.wait()
    for move in moves:
        move.wait_send()


def gather(net, source, target, columns, order):
    cols = pl.ds(*columns)
    y, x, z, c = net.y, net.x, net.z, net.c
    own = net.local_copy(source.at[:, cols], target.at[y, x, z, c, :, cols])
    sent = [net.copy(source.at[:, cols], target.at[y, x, z, c, :, cols], dev) for _, dev in net.line("z")]
    yield
    own.wait()
    for move in sent:
        move.wait_recv()
    part = target.at[y, x, :, c, :, cols]
    moves = [net.copy(part, part, dev) for _, dev in net.line(order[0])]
    sent += moves
    yield
    for move in moves:
        move.wait_recv()
    part = target.at[y, :, :, c, :, cols] if order[0] == "x" else target.at[:, x, :, c, :, cols]
    moves = [net.copy(part, part, dev) for _, dev in net.line(order[1])]
    sent += moves
    yield
    for move in moves:
        move.wait_recv()
    part = target.at[:, :, :, c, :, cols]
    moves = [net.copy(part, part, dev) for _, dev in net.line("c")]
    sent += moves
    yield
    for move in moves:
        move.wait_recv()
    for move in sent:
        move.wait_send()


def gather_copies(dims):
    return dims[0] + dims[1] + dims[2] - 3 + 1


def add_into(own, others, places):
    for at, slots in places:
        total = own[at].astype(F32)
        for slot in slots:
            total = total + others[slot].astype(F32)
        own[at] = total.astype(own.dtype)


def scatter(net, grad, held, from_core, from_first, from_second, from_z, out, columns, order):
    big_y, big_x, big_z, _ = net.dims
    cols = pl.ds(*columns)
    y, x, z, c = net.y, net.x, net.z, net.c
    sent = []
    (_, twin), = net.line("c")
    moves = [net.copy(grad.at[:, :, :, 1 - c, :, cols], from_core, twin)]
    sent += moves
    own = net.local_copy(grad.at[:, :, :, c, :, cols], held)
    yield
    own.wait()
    moves[0].wait_recv()

    def first_add(at, _):
        a, b, d = at // (big_x * big_z), (at // big_z) % big_x, at % big_z
        held[a, b, d] = (held[a, b, d].astype(F32) + from_core[a, b, d].astype(F32)).astype(BF)
        return 0

    lax.fori_loop(0, big_y * big_x * big_z, first_add, 0)
    moves = []
    for slot, (other, dev) in enumerate(net.line(order[0])):
        part = held.at[:, other] if order[0] == "x" else held.at[other]
        moves.append(net.copy(part, from_first.at[slot], dev))
    sent += moves
    yield
    for move in moves:
        move.wait_recv()
    left = big_y if order[0] == "x" else big_x

    def second_add(at, _):
        a, d = at // big_z, at % big_z
        place = (a, x, d) if order[0] == "x" else (y, a, d)
        total = held[place].astype(F32)
        for slot in range(len(moves)):
            total = total + from_first[slot, a, d].astype(F32)
        held[place] = total.astype(BF)
        return 0

    lax.fori_loop(0, left * big_z, second_add, 0)
    moves = []
    for slot, (other, dev) in enumerate(net.line(order[1])):
        part = held.at[other, x] if order[1] == "y" else held.at[y, other]
        moves.append(net.copy(part, from_second.at[slot], dev))
    sent += moves
    yield
    for move in moves:
        move.wait_recv()

    def third_add(d, _):
        total = held[y, x, d].astype(F32)
        for slot in range(len(moves)):
            total = total + from_second[slot, d].astype(F32)
        held[y, x, d] = total.astype(BF)
        return 0

    lax.fori_loop(0, big_z, third_add, 0)
    moves = []
    for slot, (other, dev) in enumerate(net.line("z")):
        moves.append(net.copy(held.at[y, x, other], from_z.at[slot], dev))
    sent += moves
    yield
    for move in moves:
        move.wait_recv()
    total = held[y, x, z].astype(F32)
    for slot in range(len(moves)):
        total = total + from_z[slot].astype(F32)
    out[:, columns[0] : columns[0] + columns[1]] = total
    for move in sent:
        move.wait_send()


def scatter_scratch(dims, rows, columns, order):
    big_y, big_x, big_z, _ = dims
    width = columns[1]
    ahead, left = (big_x, big_y) if order[0] == "x" else (big_y, big_x)
    return [
        pltpu.VMEM((big_y, big_x, big_z, rows, width), BF),
        pltpu.VMEM((big_y, big_x, big_z, rows, width), BF),
        pltpu.VMEM((ahead - 1, left, big_z, rows, width), BF),
        pltpu.VMEM((left - 1, big_z, rows, width), BF),
        pltpu.VMEM((big_z - 1, rows, width), BF),
    ]


def sum_tiles(net, tile, slots):
    first = 0
    for name in "cxyz":
        places = net.line(name)
        me = dict(y=net.y, x=net.x, z=net.z, c=net.c)[name]
        size = len(places) + 1
        slots[first + me] = tile[...]
        moves = [net.copy(tile, slots.at[first + me], dev) for _, dev in places]
        for move in moves:
            move.wait_recv()
        for move in moves:
            move.wait_send()
        total = slots[first]
        for d in range(1, size):
            total = total + slots[first + d]
        tile[...] = total
        first += size


def sems(count):
    return pltpu.SemaphoreType.DMA((max(count, 1),))


def halves(width):
    units = width // 128
    low = (units + 1) // 2 * 128
    if low == width:
        return [((0, width), "xy")]
    return [((0, low), "xy"), ((low, width - low), "yx")]


def gather_call(dims, name, number, blocks, images=None):
    big_y, big_x, big_z, share = dims
    parts = [halves(block.shape[1]) for block in blocks]
    copies = sum(len(p) for p in parts) * gather_copies(dims)
    local = sum(len(p) for p in parts)
    n = len(blocks)
    with_images = images is not None
    if with_images:
        copies += images.shape[0] - 1
        local += 1

    def body(*refs):
        ins, rest = refs[: n + with_images], refs[n + with_images :]
        outs, (send, recv, local_sem) = rest[: n + with_images], rest[n + with_images :]
        net = Net(dims, send, recv, local_sem)
        net.greet("zxyc" if not with_images else ["z", "x", "y", "c", "image"])
        tasks = []
        for j in range(n):
            for columns, order in parts[j]:
                tasks.append((0, gather(net, ins[j], outs[j], columns, order)))
        if with_images:
            tasks.append((0, exchange_images(net, ins[n], outs[n])))
        drive(tasks)

    args = list(blocks) + ([images] if with_images else [])
    shapes = [jax.ShapeDtypeStruct((big_y, big_x, big_z, 2) + b.shape, b.dtype) for b in blocks]
    if with_images:
        shapes.append(jax.ShapeDtypeStruct(images.shape, images.dtype))
    return pl.pallas_call(
        body,
        out_shape=shapes,
        in_specs=[ANY] * len(args),
        out_specs=[ANY] * len(shapes),
        scratch_shapes=[sems(copies), sems(copies), sems(local)],
        compiler_params=pltpu.CompilerParams(collective_id=number, has_side_effects=True),
        name=name,
    )(*args)


def scatter_call(dims, name, number, grads, images, squares=None):
    big_y, big_x, big_z, _ = dims
    rows = grads[0].shape[4]
    parts = [(j, columns, order) for j, g in enumerate(grads) for columns, order in halves(g.shape[5])]
    copies = len(parts) * gather_copies(dims) + images.shape[0] - 1
    with_squares = squares is not None
    if with_squares:
        copies += gather_copies(dims)
    local = len(parts) + 1
    n = len(grads)
    scratch = [sems(copies), sems(copies), sems(local)]
    for _, columns, order in parts:
        scratch += scatter_scratch(dims, rows, columns, order)
    if with_squares:
        scratch += [
            pltpu.VMEM((8, 128), F32),
            pltpu.VMEM((2 + big_x + big_y + big_z, 8, 128), F32),
        ]

    def body(*refs):
        n_in = n + 1 + with_squares
        n_out = n + 1 + with_squares
        ins, outs, rest = refs[:n_in], refs[n_in : n_in + n_out], refs[n_in + n_out :]
        net = Net(dims, *rest[:3])
        net.greet(["z", "x", "y", "c", "image"])
        tasks = []
        for k, (j, columns, order) in enumerate(parts):
            buffers = rest[3 + 5 * k : 8 + 5 * k]
            tasks.append((0, scatter(net, ins[j], *buffers, outs[j], columns, order)))
        tasks.append((0, exchange_images(net, ins[n], outs[n])))
        drive(tasks)
        if with_squares:
            tile, slots = rest[3 + 5 * len(parts) :]
            total = ins[n + 1][...]
            for j in range(n):
                value = outs[j][...]
                total = total + jnp.sum(value * value)
            tile[...] = total
            sum_tiles(net, tile, slots)
            outs[n + 1][...] = tile[...]

    vmem = pl.BlockSpec(memory_space=pltpu.VMEM)
    shapes = [jax.ShapeDtypeStruct((rows, g.shape[5]), F32) for g in grads]
    shapes.append(jax.ShapeDtypeStruct(images.shape, images.dtype))
    args = list(grads) + [images]
    in_specs, out_specs = [ANY] * (n + 1), [vmem] * n + [ANY]
    if with_squares:
        shapes.append(jax.ShapeDtypeStruct((8, 128), F32))
        args.append(jnp.broadcast_to(squares, (8, 128)))
        in_specs.append(vmem)
        out_specs.append(vmem)
    return pl.pallas_call(
        body,
        out_shape=shapes,
        in_specs=in_specs,
        out_specs=out_specs,
        scratch_shapes=scratch,
        compiler_params=pltpu.CompilerParams(
            collective_id=number, has_side_effects=True, vmem_limit_bytes=60 * MIB
        ),
        name=name,
    )(*args)


def share_call(dims, number, block):
    share = dims[3]

    def body(source, target, send, recv, local):
        net = Net(dims, send, recv, local)
        net.greet(["share"])
        drive([(0, exchange_shares(net, source, target))])

    return pl.pallas_call(
        body,
        out_shape=jax.ShapeDtypeStruct((share,) + block.shape, block.dtype),
        in_specs=[ANY],
        out_specs=ANY,
        scratch_shapes=[sems(share - 1), sems(share - 1), sems(1)],
        compiler_params=pltpu.CompilerParams(collective_id=number, has_side_effects=True),
        name="share_keys",
    )(block)


def return_call(dims, number, block):
    share = dims[3]

    def body(source, target, send, recv, local):
        net = Net(dims, send, recv, local)
        net.greet(["share"])
        moves = [
            net.copy(source.at[other], target.at[slot], dev)
            for slot, (other, dev) in enumerate(net.sharers())
        ]
        for move in moves:
            move.wait_recv()
        for move in moves:
            move.wait_send()

    return pl.pallas_call(
        body,
        out_shape=jax.ShapeDtypeStruct((share - 1,) + block.shape[1:], block.dtype),
        in_specs=[ANY],
        out_specs=ANY,
        scratch_shapes=[sems(share - 1), sems(share - 1), sems(1)],
        compiler_params=pltpu.CompilerParams(collective_id=number, has_side_effects=True),
        name="return_keys",
    )(block)


def mm(a, b, ca, cb):
    return lax.dot_general(a, b, (((ca,), (cb,)), ((), ())), preferred_element_type=F32)


def attend_kernel(q_ref, k_ref, v_ref, bias_ref, o_ref, l_ref, *, block):
    lane = lax.broadcasted_iota(jnp.int32, (1, PAIR), 1) < HEAD_DIM
    k, v, bias = k_ref[...], v_ref[...], bias_ref[...]

    def step(i, _):
        rows = pl.ds(pl.multiple_of(i * block, block), block)
        q = q_ref[rows, :] * jnp.asarray(SCALE, BF)
        mixed, logs = [], []
        for h in range(2):
            mine = lane if h == 0 else ~lane
            scores = mm(jnp.where(mine, q, jnp.zeros_like(q)), k, 1, 1) + bias
            highest = jnp.max(scores, -1, keepdims=True)
            powers = jnp.exp(scores - highest)
            total = jnp.sum(powers, -1, keepdims=True)
            mixed.append(mm(powers.astype(BF), v, 1, 0) / total)
            logs.append(highest + jnp.log(total))
        o_ref[rows, :] = jnp.where(lane, mixed[0], mixed[1]).astype(BF)
        l_ref[rows, :] = jnp.where(lane, logs[0], logs[1])
        return 0

    lax.fori_loop(0, q_ref.shape[0] // block, step, 0)


def attend(q, kv, bias, block):
    rows, width = q.shape
    keys = kv.shape[0]
    pairs = width // PAIR
    own = pl.BlockSpec((rows, PAIR), lambda h: (0, h))
    return pl.pallas_call(
        functools.partial(attend_kernel, block=block),
        grid=(pairs,),
        in_specs=[
            own,
            pl.BlockSpec((keys, PAIR), lambda h: (0, h)),
            pl.BlockSpec((keys, PAIR), lambda h: (0, h + pairs)),
            pl.BlockSpec((1, keys), lambda h: (0, 0)),
        ],
        out_specs=[own, own],
        out_shape=[jax.ShapeDtypeStruct((rows, width), BF), jax.ShapeDtypeStruct((rows, width), F32)],
        compiler_params=pltpu.CompilerParams(vmem_limit_bytes=56 * MIB),
        cost_estimate=pl.CostEstimate(
            flops=16 * rows * keys * width, bytes_accessed=2 * 4 * keys * width, transcendentals=rows * keys * HEADS
        ),
        name="attend",
    )(q, kv, kv, bias)


def attend_back_kernel(
    q_ref, k_ref, v_ref, bias_ref, o_ref, l_ref, do_ref, dq_ref, dk_ref, dv_ref, dk_sum, dv_sum, *, block
):
    lane = lax.broadcasted_iota(jnp.int32, (1, PAIR), 1) < HEAD_DIM
    k, v = k_ref[...], v_ref[...]
    bias = jnp.transpose(jnp.broadcast_to(bias_ref[...], (8, k.shape[0])))[:, :1]
    dk_sum[...] = jnp.zeros_like(dk_sum)
    dv_sum[...] = jnp.zeros_like(dv_sum)

    def step(i, _):
        rows = pl.ds(pl.multiple_of(i * block, block), block)
        q, do = q_ref[rows, :] * jnp.asarray(SCALE, BF), do_ref[rows, :]
        logs = jnp.transpose(l_ref[rows, :])
        products = jnp.transpose(do.astype(F32) * o_ref[rows, :].astype(F32))
        dqs, dks, dvs = [], [], []
        for h in range(2):
            mine = lane if h == 0 else ~lane
            low, high = h * HEAD_DIM, (h + 1) * HEAD_DIM
            q_h = jnp.where(mine, q, jnp.zeros_like(q))
            do_h = jnp.where(mine, do, jnp.zeros_like(do))
            row_dots = jnp.sum(products[low:high, :], 0, keepdims=True)
            chances = jnp.exp(mm(k, q_h, 1, 1) + bias - logs[low : low + 1, :])
            back = mm(v, do_h, 1, 1)
            scores = (chances * (back - row_dots)).astype(BF)
            dqs.append(mm(scores, k, 0, 0))
            dks.append(mm(scores, q_h, 1, 0))
            dvs.append(mm(chances.astype(BF), do_h, 1, 0))
        dq_ref[rows, :] = (jnp.where(lane, dqs[0], dqs[1]) * SCALE).astype(BF)
        dk_sum[...] += dks[0] + dks[1]
        dv_sum[...] += dvs[0] + dvs[1]
        return 0

    lax.fori_loop(0, q_ref.shape[0] // block, step, 0)
    dk_ref[...] = dk_sum[...].astype(BF)
    dv_ref[...] = dv_sum[...].astype(BF)


def attend_back(q, kv, bias, mixed, logs, back, block):
    rows, width = q.shape
    keys = kv.shape[0]
    pairs = width // PAIR
    own = pl.BlockSpec((rows, PAIR), lambda h: (0, h))
    key = pl.BlockSpec((keys, PAIR), lambda h: (0, h))
    return pl.pallas_call(
        functools.partial(attend_back_kernel, block=block),
        grid=(pairs,),
        in_specs=[
            own,
            key,
            pl.BlockSpec((keys, PAIR), lambda h: (0, h + pairs)),
            pl.BlockSpec((1, keys), lambda h: (0, 0)),
            own,
            own,
            own,
        ],
        out_specs=[own, key, key],
        out_shape=[
            jax.ShapeDtypeStruct((rows, width), BF),
            jax.ShapeDtypeStruct((keys, width), BF),
            jax.ShapeDtypeStruct((keys, width), BF),
        ],
        scratch_shapes=[pltpu.VMEM((keys, PAIR), F32), pltpu.VMEM((keys, PAIR), F32)],
        compiler_params=pltpu.CompilerParams(vmem_limit_bytes=56 * MIB),
        cost_estimate=pl.CostEstimate(
            flops=40 * rows * keys * width, bytes_accessed=2 * 8 * keys * width, transcendentals=rows * keys * HEADS
        ),
        name="attend_back",
    )(q, kv, kv, bias, mixed, logs, back)


def rms_norm(value, gain):
    return value * lax.rsqrt(jnp.mean(value * value, -1, keepdims=True) + EPS) * gain


def gated(gate_part, up_part):
    return jax.nn.gelu(gate_part, approximate=True) * up_part


def adam_step(master, grad, first, second, factor, rate, decay):
    clipped = factor * grad
    first_new = BETA_ONE * first + (1.0 - BETA_ONE) * clipped
    second_new = BETA_TWO * second + (1.0 - BETA_TWO) * clipped * clipped
    corrected = first_new / (1.0 - BETA_ONE**STEP)
    spread = jnp.sqrt(second_new / (1.0 - BETA_TWO**STEP)) + ADAM_EPS
    master_new = master - rate * (corrected / spread + decay * master)
    return (master_new, first_new, second_new)


def grid_of(n_img):
    big_y = max(d for d in range(1, n_img + 1) if n_img % d == 0 and d * d <= n_img)
    return big_y, n_img // big_y


def on_device(
    patches,
    cotangent,
    valid_counts,
    qkv_master,
    out_master,
    in_master,
    down_master,
    gain_master,
    qkv_first,
    out_first,
    in_first,
    down_first,
    gain_first,
    qkv_second,
    out_second,
    in_second,
    down_second,
    gain_second,
):
    images, band_rows, width = patches.shape
    n_img, n_band = lax.axis_size("img"), lax.axis_size("band")
    share = n_band // images
    big_y, big_x = grid_of(n_img)
    dims = (big_y, big_x, n_band // 2, share)
    rows = images * band_rows
    shard = qkv_master.shape[0]
    own_comm = shard % 8 == 0
    both = ("img", "band")

    def gather_all(number, blocks, chunks):
        if own_comm:
            got = gather_call(dims, "gather_%d" % number, number, blocks, chunks)
        else:
            got = [lax.all_gather(b, both, axis=0, tiled=True) for b in blocks]
            groups = [[s * share + r for s in range(images)] for r in range(share)]
            got.append(lax.all_to_all(chunks, "band", 0, 0, axis_index_groups=groups, tiled=True))
        return [g.reshape(width, g.shape[-1]) for g in got[:-1]] + [got[-1]]

    def scatter_all(number, grads, chunks, squares=None):
        if own_comm:
            shaped = [g.astype(BF).reshape(dims[:3] + (2, shard, g.shape[1])) for g in grads]
            return scatter_call(dims, "scatter_%d" % number, number, shaped, chunks, squares)
        sums = [lax.psum_scatter(g, both, scatter_dimension=0, tiled=True) for g in grads]
        groups = [[s * share + r for s in range(images)] for r in range(share)]
        got = sums + [lax.all_to_all(chunks, "band", 0, 0, axis_index_groups=groups, tiled=True)]
        if squares is not None:
            total = squares
            for s in sums:
                total = total + jnp.sum(s * s)
            got.append(lax.psum(jnp.broadcast_to(total, (8, 128)), both))
        return got

    gains_block = jnp.pad(jnp.transpose(gain_master).astype(BF), ((0, 0), (0, 126)))
    w_qkv, gains, tokens_low = gather_all(0, [qkv_master.astype(BF), gains_block], patches)
    w_in, w_out_t, w_down_t, cotangent_low = gather_all(
        1,
        [in_master.astype(BF), jnp.transpose(out_master).astype(BF), jnp.transpose(down_master).astype(BF)],
        cotangent,
    )
    gain_one = gains[:, 0].astype(F32)
    gain_two = gains[:, 1].astype(F32)
    hidden_units = w_down_t.shape[1]

    band = lax.axis_index("band")
    image, part = band // share, band % share
    count = lax.dynamic_index_in_dim(valid_counts, image, 0, keepdims=False)
    own_places = (
        (jnp.arange(images, dtype=jnp.int32)[:, None] * share + part) * band_rows
        + jnp.arange(band_rows, dtype=jnp.int32)[None, :]
    ).reshape(rows, 1)
    row_keep = (own_places < count).astype(F32)
    key_places = (
        (
            jnp.arange(images, dtype=jnp.int32)[None, :, None] * share
            + jnp.arange(share, dtype=jnp.int32)[:, None, None]
        )
        * band_rows
        + jnp.arange(band_rows, dtype=jnp.int32)[None, None, :]
    ).reshape(1, share * rows)
    bias = jnp.where(key_places < count, 0.0, NEG).astype(F32)

    tokens = tokens_low.reshape(rows, width).astype(F32)
    normed_a = rms_norm(tokens, gain_one).astype(BF)
    project = jnp.dot(normed_a, w_qkv, preferred_element_type=F32).astype(BF)
    queries = project[:, :width]
    kv = share_call(dims, 2, project[:, width:]).reshape(share * rows, 2 * width)
    attended, log_sums = attend(queries, kv, bias, 256)

    middle = tokens + mm(attended, w_out_t, 1, 1)
    normed_b = rms_norm(middle, gain_two).astype(BF)
    gate_up = jnp.dot(normed_b, w_in, preferred_element_type=F32)
    gate_part = gate_up[:, :hidden_units]
    up_part = gate_up[:, hidden_units:]
    hidden = gated(gate_part, up_part).astype(BF)
    result = row_keep * (middle + mm(hidden, w_down_t, 1, 1))
    result_low = result.astype(BF).reshape(images, band_rows, width)
    back_result = row_keep * cotangent_low.reshape(rows, width).astype(F32)
    back_low = back_result.astype(BF)
    grad_down_t = mm(back_low, hidden, 0, 0)
    back_hidden = jnp.dot(back_low, w_down_t, preferred_element_type=F32)
    _, gate_back = jax.vjp(gated, gate_part, up_part)
    back_gate, back_up = gate_back(back_hidden)
    back_gate_up = jnp.concatenate([back_gate, back_up], 1).astype(BF)
    grad_in = mm(normed_b, back_gate_up, 0, 0)
    back_normed_b = mm(back_gate_up, w_in, 1, 1)
    _, second_back = jax.vjp(rms_norm, middle, gain_two)
    back_middle_norm, grad_gain_two = second_back(back_normed_b)
    back_middle = back_result + back_middle_norm
    back_branch = back_middle.astype(BF)
    grad_out_t = mm(back_branch, attended, 0, 0)
    back_attended = jnp.dot(back_branch, w_out_t, preferred_element_type=F32).astype(BF)

    in_sum, out_sum, down_sum, output = scatter_all(3, [grad_in, grad_out_t, grad_down_t], result_low)
    squares = jnp.sum(in_sum * in_sum) + jnp.sum(out_sum * out_sum) + jnp.sum(down_sum * down_sum)

    back_q, part_k, part_v = attend_back(queries, kv, bias, attended, log_sums, back_attended, 256)
    part_kv = jnp.concatenate([part_k, part_v], 1).reshape(share, rows, 2 * width)
    arrived = return_call(dims, 4, part_kv)
    back_kv = lax.dynamic_index_in_dim(part_kv, part, 0, keepdims=False).astype(F32)
    for slot in range(share - 1):
        back_kv = back_kv + arrived[slot].astype(F32)
    back_project = jnp.concatenate([back_q, back_kv.astype(BF)], 1)
    grad_qkv = mm(normed_a, back_project, 0, 0)
    back_normed_a = mm(back_project, w_qkv, 1, 1)
    _, first_back = jax.vjp(rms_norm, tokens, gain_one)
    back_tokens, grad_gain_one = first_back(back_normed_a)
    back_rows = (back_middle + back_tokens).astype(BF).reshape(images, band_rows, width)
    grad_gains = jnp.pad(jnp.stack([grad_gain_one, grad_gain_two], 1), ((0, 0), (0, 126)))
    qkv_sum, gain_sum, back_input, total = scatter_all(5, [grad_qkv, grad_gains], back_rows, squares)
    grad_norm = jnp.sqrt(total[0, 0])
    factor = jnp.minimum(1.0, CLIP / grad_norm)
    shards = (
        qkv_sum,
        jnp.transpose(out_sum),
        in_sum,
        jnp.transpose(down_sum),
        jnp.transpose(gain_sum[:, :2]),
    )
    masters = (qkv_master, out_master, in_master, down_master, gain_master)
    firsts = (qkv_first, out_first, in_first, down_first, gain_first)
    seconds = (qkv_second, out_second, in_second, down_second, gain_second)
    updated = [
        adam_step(masters[j], shards[j], firsts[j], seconds[j], factor, RATES[j], DECAYS[j]) for j in range(5)
    ]
    return (
        (output, back_input, grad_norm)
        + tuple(updated[j][0] for j in range(5))
        + tuple(updated[j][1] for j in range(5))
        + tuple(updated[j][2] for j in range(5))
        + tuple(updated[j][0].astype(BF) for j in range(5))
    )


def solution(mesh):
    rows_split, columns_split = P(("img", "band"), None), P(None, ("img", "band"))
    weights = (rows_split, columns_split, rows_split, columns_split, columns_split)
    tokens = P("img", "band", None)
    return jax.shard_map(
        on_device,
        mesh=mesh,
        in_specs=(tokens, tokens, P("img")) + weights * 3,
        out_specs=(tokens, tokens, P()) + weights * 4,
        check_vma=False,
    )
```

```python
import functools

import jax
import jax.numpy as jnp
from jax import lax
from jax.experimental import pallas as pl
from jax.experimental.pallas import tpu as pltpu
from jax.sharding import PartitionSpec as P

HEADS = 12
HEAD_DIM = 64
PAIR = 2 * HEAD_DIM
STEP = 10
EPS = 1e-06
NEG = -1000000000.0
SCALE = 0.125
CLIP = 1.0
BETA_ONE = 0.9
BETA_TWO = 0.999
ADAM_EPS = 1e-08
RATES = (0.06, 0.5, 0.06, 0.04, 0.5)
DECAYS = (0.1, 0.1, 0.1, 0.1, 0.0)
BF = jnp.bfloat16
F32 = jnp.float32
MESH = pl.DeviceIdType.MESH
ANY = pl.BlockSpec(memory_space=pl.ANY)
MIB = 2**20


class Net:
    def __init__(self, dims, send, recv, local):
        self.dims = dims
        big_y, big_x, big_z, share = dims
        img, band = lax.axis_index("img"), lax.axis_index("band")
        self.y, self.x = img // big_x, img % big_x
        self.z, self.c = band // 2, band % 2
        self.twin = 1 - self.c
        image, self.part = band // share, band % share
        self.image, self.images = image, 2 * big_z // share
        self.send, self.recv, self.local = send, recv, local
        self.used, self.used_local = 0, 0
        self.lines = {}
        for name, size in zip("yxzc", (big_y, big_x, big_z, 2)):
            places = []
            for d in range(1, size):
                at = dict(y=self.y, x=self.x, z=self.z, c=self.c)
                at[name] = lax.rem(at[name] + d, size)
                places.append((at[name], (at["y"] * big_x + at["x"], at["z"] * 2 + at["c"])))
            self.lines[name] = places
        self.lines["image"] = []
        for d in range(1, self.images):
            other = lax.rem(image + d, self.images)
            self.lines["image"].append((other, (img, other * share + self.part)))
        self.lines["share"] = []
        for d in range(1, share):
            other = lax.rem(self.part + d, share)
            self.lines["share"].append((other, (img, image * share + other)))

    def line(self, name):
        return self.lines[name]

    def greet(self, kinds):
        barrier = pltpu.get_barrier_semaphore()
        count = 0
        for kind in kinds:
            for _, target in self.lines[kind]:
                pl.semaphore_signal(barrier, inc=1, device_id=target, device_id_type=MESH)
            count += len(self.lines[kind])
        pl.semaphore_wait(barrier, count)

    def copy(self, source, target_ref, target):
        made = self.plan(source, target_ref, target)
        made.start()
        return made

    def plan(self, source, target_ref, target):
        self.used += 1
        return Move(source, target_ref, self.send, self.recv, self.used - 1, target)

    def local_copy(self, source, target_ref):
        self.used_local += 1
        made = Move(source, target_ref, None, self.local, self.used_local - 1, None)
        made.start()
        return made


class Part:
    def __init__(self, ref, index=None):
        self.ref, self.index = ref, index

    def __getitem__(self, index):
        return Part(self.ref, index)

    def view(self):
        return self.ref if self.index is None else self.ref.at[self.index]


class Move:
    def __init__(self, source, target_ref, send, recv, at, target):
        self.source, self.target_ref = source, target_ref
        self.send, self.recv, self.at, self.target = send, recv, at, target

    def build(self):
        if self.target is None:
            return pltpu.make_async_copy(self.source.view(), self.target_ref.view(), self.recv.at[self.at])
        return pltpu.make_async_remote_copy(
            src_ref=self.source.view(),
            dst_ref=self.target_ref.view(),
            send_sem=self.send.at[self.at],
            recv_sem=self.recv.at[self.at],
            device_id=self.target,
            device_id_type=MESH,
        )

    def start(self):
        self.build().start()

    def wait(self):
        self.build().wait()

    def wait_recv(self):
        self.build().wait_recv()

    def wait_send(self):
        self.build().wait_send()


def drive(tasks):
    waiting = list(tasks)
    turn = 0
    while waiting:
        left = []
        for start, task in waiting:
            if start <= turn:
                try:
                    next(task)
                except StopIteration:
                    continue
            left.append((start, task))
        waiting = left
        turn += 1


def exchange_images(net, source, target):
    moves = [net.copy(Part(source)[other], Part(target)[net.image], dev) for other, dev in net.line("image")]
    own = net.local_copy(Part(source)[net.image], Part(target)[net.image])
    yield
    yield
    yield
    yield
    for move in moves:
        move.wait_recv()
    own.wait()
    for move in moves:
        move.wait_send()


def gather(net, source, target, columns, order):
    cols = pl.ds(*columns)
    y, x, z, c = net.y, net.x, net.z, net.c
    own = net.local_copy(Part(source)[:, cols], Part(target)[y, x, z, c, :, cols])
    sent = [net.copy(Part(source)[:, cols], Part(target)[y, x, z, c, :, cols], dev) for _, dev in net.line("z")]
    yield
    own.wait()
    for move in sent:
        move.wait_recv()
    part = Part(target)[y, x, :, c, :, cols]
    moves = [net.copy(part, part, dev) for _, dev in net.line(order[0])]
    sent += moves
    yield
    for move in moves:
        move.wait_recv()
    part = Part(target)[y, :, :, c, :, cols] if order[0] == "x" else Part(target)[:, x, :, c, :, cols]
    moves = [net.copy(part, part, dev) for _, dev in net.line(order[1])]
    sent += moves
    yield
    for move in moves:
        move.wait_recv()
    part = Part(target)[:, :, :, c, :, cols]
    moves = [net.copy(part, part, dev) for _, dev in net.line("c")]
    sent += moves
    yield
    for move in moves:
        move.wait_recv()
    for move in sent:
        move.wait_send()


def gather_copies(dims):
    return dims[0] + dims[1] + dims[2] - 3 + 1


def scatter(net, grad, held, from_core, from_first, from_second, from_z, out, squares, columns, order):
    big_y, big_x, big_z, _ = net.dims
    cols = pl.ds(*columns)
    y, x, z, c = net.y, net.x, net.z, net.c
    sent = []
    (_, twin), = net.line("c")
    moves = [net.copy(Part(grad)[:, :, :, net.twin, :, cols], Part(from_core), twin)]
    sent += moves
    own = net.local_copy(Part(grad)[:, :, :, c, :, cols], Part(held))
    yield
    own.wait()
    moves[0].wait_recv()

    def first_add(at, _):
        a, b, d = at // (big_x * big_z), (at // big_z) % big_x, at % big_z
        held[a, b, d] = (held[a, b, d].astype(F32) + from_core[a, b, d].astype(F32)).astype(BF)
        return 0

    lax.fori_loop(0, big_y * big_x * big_z, first_add, 0)
    moves = []
    for slot, (other, dev) in enumerate(net.line(order[0])):
        part = Part(held)[:, other] if order[0] == "x" else Part(held)[other]
        moves.append(net.copy(part, Part(from_first)[slot], dev))
    sent += moves
    yield
    for move in moves:
        move.wait_recv()
    left = big_y if order[0] == "x" else big_x

    def second_add(at, _):
        a, d = at // big_z, at % big_z
        place = (a, x, d) if order[0] == "x" else (y, a, d)
        total = held[place].astype(F32)
        for slot in range(len(moves)):
            total = total + from_first[slot, a, d].astype(F32)
        held[place] = total.astype(BF)
        return 0

    lax.fori_loop(0, left * big_z, second_add, 0)
    moves = []
    for slot, (other, dev) in enumerate(net.line(order[1])):
        part = Part(held)[other, x] if order[1] == "y" else Part(held)[y, other]
        moves.append(net.copy(part, Part(from_second)[slot], dev))
    sent += moves
    yield
    for move in moves:
        move.wait_recv()

    def third_add(d, _):
        total = held[y, x, d].astype(F32)
        for slot in range(len(moves)):
            total = total + from_second[slot, d].astype(F32)
        held[y, x, d] = total.astype(BF)
        return 0

    lax.fori_loop(0, big_z, third_add, 0)
    moves = []
    for slot, (other, dev) in enumerate(net.line("z")):
        moves.append(net.copy(Part(held)[y, x, other], Part(from_z)[slot], dev))
    sent += moves
    yield
    for move in moves:
        move.wait_recv()
    total = held[y, x, z].astype(F32)
    for slot in range(len(moves)):
        total = total + from_z[slot].astype(F32)
    out[:, columns[0] : columns[0] + columns[1]] = total
    tile = squares[...]
    for a in range(total.shape[0] // 8):
        for b in range(columns[1] // 128):
            piece = total[8 * a : 8 * a + 8, 128 * b : 128 * b + 128]
            tile = tile + piece * piece
    squares[...] = tile
    for move in sent:
        move.wait_send()


def scatter_scratch(dims, rows, columns, order):
    big_y, big_x, big_z, _ = dims
    width = columns[1]
    ahead, left = (big_x, big_y) if order[0] == "x" else (big_y, big_x)
    return [
        pltpu.VMEM((big_y, big_x, big_z, rows, width), BF),
        pltpu.VMEM((big_y, big_x, big_z, rows, width), BF),
        pltpu.VMEM((ahead - 1, left, big_z, rows, width), BF),
        pltpu.VMEM((left - 1, big_z, rows, width), BF),
        pltpu.VMEM((big_z - 1, rows, width), BF),
    ]


def sum_tiles(net, tile, slots):
    first = 0
    for name in "cxyz":
        places = net.line(name)
        me = dict(y=net.y, x=net.x, z=net.z, c=net.c)[name]
        size = len(places) + 1
        slots[first + me] = tile[...]
        moves = [net.copy(Part(tile), Part(slots)[first + me], dev) for _, dev in places]
        for move in moves:
            move.wait_recv()
        for move in moves:
            move.wait_send()
        total = slots[first]
        for d in range(1, size):
            total = total + slots[first + d]
        tile[...] = total
        first += size


def sems(count):
    return pltpu.SemaphoreType.DMA((max(count, 1),))


def halves(width):
    units = width // 128
    low = (units + 1) // 2 * 128
    if low == width:
        return [((0, width), "xy")]
    return [((0, low), "xy"), ((low, width - low), "yx")]


def gather_call(dims, name, number, blocks, images=None):
    big_y, big_x, big_z, share = dims
    parts = [halves(block.shape[1]) for block in blocks]
    copies = sum(len(p) for p in parts) * gather_copies(dims)
    local = sum(len(p) for p in parts)
    n = len(blocks)
    with_images = images is not None
    if with_images:
        copies += images.shape[0] - 1
        local += 1

    def body(*refs):
        ins, rest = refs[: n + with_images], refs[n + with_images :]
        outs, (send, recv, local_sem) = rest[: n + with_images], rest[n + with_images :]
        net = Net(dims, send, recv, local_sem)
        net.greet("zxyc" if not with_images else ["z", "x", "y", "c", "image"])
        tasks = []
        for j in range(n):
            for columns, order in parts[j]:
                tasks.append((0, gather(net, ins[j], outs[j], columns, order)))
        if with_images:
            tasks.append((0, exchange_images(net, ins[n], outs[n])))
        drive(tasks)

    args = list(blocks) + ([images] if with_images else [])
    shapes = [jax.ShapeDtypeStruct((big_y, big_x, big_z, 2) + b.shape, b.dtype) for b in blocks]
    if with_images:
        shapes.append(jax.ShapeDtypeStruct(images.shape, images.dtype))
    return pl.pallas_call(
        body,
        out_shape=shapes,
        in_specs=[ANY] * len(args),
        out_specs=[ANY] * len(shapes),
        scratch_shapes=[sems(copies), sems(copies), sems(local)],
        compiler_params=pltpu.CompilerParams(collective_id=number, has_side_effects=True),
        name=name,
    )(*args)


def scatter_call(dims, name, number, grads, images, squares):
    big_y, big_x, big_z, _ = dims
    rows = grads[0].shape[4]
    parts = [(j, columns, order) for j, g in enumerate(grads) for columns, order in halves(g.shape[5])]
    copies = (len(parts) + 1) * gather_copies(dims) + images.shape[0] - 1
    local = len(parts) + 1
    n = len(grads)
    scratch = [sems(copies), sems(copies), sems(local)]
    for _, columns, order in parts:
        scratch += scatter_scratch(dims, rows, columns, order)
    scratch += [pltpu.VMEM((8, 128), F32), pltpu.VMEM((2 + big_x + big_y + big_z, 8, 128), F32)]

    def body(*refs):
        ins, outs, rest = refs[: n + 2], refs[n + 2 : 2 * n + 4], refs[2 * n + 4 :]
        tile, slots = rest[3 + 5 * len(parts) :]
        net = Net(dims, *rest[:3])
        net.greet(["z", "x", "y", "c", "image"])
        tile[...] = ins[n + 1][...]
        tasks = []
        for k, (j, columns, order) in enumerate(parts):
            buffers = rest[3 + 5 * k : 8 + 5 * k]
            tasks.append((0, scatter(net, ins[j], *buffers, outs[j], tile, columns, order)))
        tasks.append((0, exchange_images(net, ins[n], outs[n])))
        drive(tasks)
        sum_tiles(net, tile, slots)
        outs[n + 1][...] = jnp.broadcast_to(jnp.sum(tile[...], keepdims=True), (8, 128))

    vmem = pl.BlockSpec(memory_space=pltpu.VMEM)
    shapes = [jax.ShapeDtypeStruct((rows, g.shape[5]), F32) for g in grads]
    shapes += [jax.ShapeDtypeStruct(images.shape, images.dtype), jax.ShapeDtypeStruct((8, 128), F32)]
    return pl.pallas_call(
        body,
        out_shape=shapes,
        in_specs=[ANY] * (n + 1) + [vmem],
        out_specs=[vmem] * n + [ANY, vmem],
        scratch_shapes=scratch,
        compiler_params=pltpu.CompilerParams(
            collective_id=number, has_side_effects=True, vmem_limit_bytes=60 * MIB
        ),
        name=name,
    )(*grads, images, squares)


def mm(a, b, ca, cb):
    return lax.dot_general(a, b, (((ca,), (cb,)), ((), ())), preferred_element_type=F32)


def at_turn(turn, events):
    for when in sorted(events):

        @pl.when(turn == when)
        def _(when=when):
            for task in events[when]:
                next(task, None)


def schedule(tasks, turns, last):
    events, tail = {}, []
    for task, when in zip(tasks, turns):
        for turn in when:
            if turn < last:
                events.setdefault(turn, []).append(task)
            else:
                tail.append(task)
    return events, tail


def lanes_of(h):
    lane = lax.broadcasted_iota(jnp.int32, (1, PAIR), 1) < HEAD_DIM
    return lane if h == 0 else ~lane


def attend(dims, number, project, bias, block, weights):
    big_y, big_x, big_z, share = dims
    rows, width = project.shape[0], project.shape[1] // 3
    pairs = width // PAIR
    others = share - 1
    blocks = rows // block
    n = len(weights)
    parts = [(j, columns, order) for j, w in enumerate(weights) for columns, order in halves(w.shape[1])]
    copies = len(parts) * gather_copies(dims) + others * 2 * pairs
    per_turn = max(blocks // 4, 1)

    def body(*refs):
        q_ref, k_ref, v_ref, project_ref, bias_ref = refs[:5]
        blocks_in, refs = refs[5 : 5 + n], refs[5 + n :]
        o_ref, l_ref, kv_out, refs = refs[0], refs[1], refs[2], refs[3:]
        gathered, (kv_held, send, recv, local) = refs[:n], refs[n:]
        h = pl.program_id(0)
        net = Net(dims, send, recv, local)

        def move_keys(j):
            moves = []
            for slot, (_, target) in enumerate(net.line("share")):
                source = Part(project_ref)[:, pl.ds(width + PAIR * j, PAIR)]
                moves.append(net.plan(source, Part(kv_held)[others - 1 - slot, j], target))
            return moves

        key_moves = [move_keys(j) for j in range(2 * pairs)]
        keep = Move(Part(kv_held), Part(kv_out), None, local, len(parts), None)
        tasks = [gather(net, blocks_in[j], gathered[j], columns, order) for j, columns, order in parts]
        turns = []
        for j, columns, order in parts:
            turns.append([GATHER_TURNS[j][0]] + [t for t in GATHER_TURNS[j][1:]])
        events, tail = schedule(tasks, turns, 4 * pairs)

        @pl.when(h == 0)
        def _():
            net.greet(["z", "x", "y", "c"] + (["share"] if share > 2 else []))
            for j in range(pairs):
                for move in key_moves[j] + key_moves[j + pairs]:
                    move.start()

        for j in range(pairs):

            @pl.when(h == j)
            def _(j=j):
                for move in key_moves[j] + key_moves[j + pairs]:
                    move.wait_recv()
                if j == pairs - 1:
                    keep.start()

        def step(i, _):
            at_turn(h * 4 + i // per_turn, events)
            at = pl.ds(pl.multiple_of(i * block, block), block)
            k = jnp.concatenate([k_ref[...]] + [kv_held[s, h] for s in range(others)], 0)
            v = jnp.concatenate([v_ref[...]] + [kv_held[s, h + pairs] for s in range(others)], 0)
            q = q_ref[at, :] * jnp.asarray(SCALE, BF)
            mixed, logs = [], []
            for half in range(2):
                scores = mm(jnp.where(lanes_of(half), q, jnp.zeros_like(q)), k, 1, 1) + bias_ref[...]
                highest = jnp.max(scores, -1, keepdims=True)
                powers = jnp.exp(scores - highest)
                total = jnp.sum(powers, -1, keepdims=True)
                mixed.append(mm(powers.astype(BF), v, 1, 0) / total)
                logs.append(highest + jnp.log(total))
            o_ref[at, :] = jnp.where(lanes_of(0), mixed[0], mixed[1]).astype(BF)
            l_ref[at, :] = jnp.where(lanes_of(0), logs[0], logs[1])
            return 0

        lax.fori_loop(0, blocks, step, 0)

        @pl.when(h == pairs - 1)
        def _():
            for task in tail:
                next(task, None)
            for moves in key_moves:
                for move in moves:
                    move.wait_send()
            keep.wait()

    column = lambda first: pl.BlockSpec((rows, PAIR), lambda h: (0, h + first))
    keys = rows * share
    shapes = [
        jax.ShapeDtypeStruct((rows, width), BF),
        jax.ShapeDtypeStruct((rows, width), F32),
        jax.ShapeDtypeStruct((others, 2 * pairs, rows, PAIR), BF),
    ] + [jax.ShapeDtypeStruct((big_y, big_x, big_z, 2) + w.shape, w.dtype) for w in weights]
    return pl.pallas_call(
        body,
        grid=(pairs,),
        in_specs=[column(0), column(pairs), column(2 * pairs), ANY, pl.BlockSpec((1, keys), lambda h: (0, 0))]
        + [ANY] * n,
        out_specs=[column(0), column(0), ANY] + [ANY] * n,
        out_shape=shapes,
        scratch_shapes=[
            pltpu.VMEM((others, 2 * pairs, rows, PAIR), BF),
            sems(copies),
            sems(copies),
            sems(len(parts) + 1),
        ],
        compiler_params=pltpu.CompilerParams(
            collective_id=number, has_side_effects=True, vmem_limit_bytes=56 * MIB
        ),
        cost_estimate=pl.CostEstimate(
            flops=16 * rows * keys * width, bytes_accessed=8 * keys * width, transcendentals=rows * keys * HEADS
        ),
        name="attend",
    )(project, project, project, project, bias, *weights)


GATHER_TURNS = ((0, 8, 11, 17, 21), (1, 4, 6, 9, 12), (3, 12, 15, 21, 24))
SCATTER_TURNS = ((0, 2, 8, 14, 20), (1, 3, 9, 15, 21), (1, 4, 11, 17, 24))


def attend_back(dims, number, project, kv, bias, mixed, logs, back, block, grads):
    big_y, big_x, big_z, share = dims
    rows, width = mixed.shape
    pairs = width // PAIR
    others = share - 1
    blocks = rows // block
    keys = rows * share
    n = len(grads)
    parts = [(j, columns, order) for j, g in enumerate(grads) for columns, order in halves(g.shape[5])]
    copies = len(parts) * gather_copies(dims) + others * 2 * pairs
    per_turn = max(blocks // 4, 1)

    def body(*refs):
        q_ref, k_ref, v_ref, k_other, v_other, bias_ref, mixed_ref, logs_ref, back_ref = refs[:9]
        grads_in, refs = refs[9 : 9 + n], refs[9 + n :]
        out_ref, sums, squares, refs = refs[0], refs[1 : 1 + n], refs[1 + n], refs[2 + n :]
        dk_sum, dv_sum, dk_own, dv_own, parted, arrived, bias_column = refs[:7]
        send, recv, local = refs[7:10]
        buffers = refs[10:]
        h = pl.program_id(0)
        net = Net(dims, send, recv, local)

        def move_keys(j):
            moves = []
            for slot, (_, target) in enumerate(net.line("share")):
                moves.append(net.plan(Part(parted)[slot, j], Part(arrived)[others - 1 - slot, j], target))
            return moves

        key_moves = [move_keys(j) for j in range(2 * pairs)]
        tasks = [
            scatter(net, grads_in[j], *buffers[5 * k : 5 * k + 5], sums[j], squares, columns, order)
            for k, (j, columns, order) in enumerate(parts)
        ]
        events, tail = schedule(tasks, [SCATTER_TURNS[j] for j, _, _ in parts], 4 * pairs)

        @pl.when(h == 0)
        def _():
            net.greet(["z", "x", "y", "c"] + (["share"] if share > 2 else []))
            squares[...] = jnp.zeros_like(squares)
            bias_column[...] = jnp.transpose(jnp.broadcast_to(bias_ref[...], (PAIR, keys)))

        dk_sum[...] = jnp.zeros_like(dk_sum)
        dv_sum[...] = jnp.zeros_like(dv_sum)

        def step(i, _):
            at_turn(h * 4 + i // per_turn, events)
            at = pl.ds(pl.multiple_of(i * block, block), block)
            k = jnp.concatenate([k_ref[...]] + [k_other[s, 0] for s in range(others)], 0)
            v = jnp.concatenate([v_ref[...]] + [v_other[s, 0] for s in range(others)], 0)
            q, do = q_ref[at, :] * jnp.asarray(SCALE, BF), back_ref[at, :]
            lse = jnp.transpose(logs_ref[at, :])
            products = jnp.transpose(do.astype(F32) * mixed_ref[at, :].astype(F32))
            dqs, dks, dvs = [], [], []
            for half in range(2):
                low, high = half * HEAD_DIM, (half + 1) * HEAD_DIM
                q_h = jnp.where(lanes_of(half), q, jnp.zeros_like(q))
                do_h = jnp.where(lanes_of(half), do, jnp.zeros_like(do))
                row_dots = jnp.sum(products[low:high, :], 0, keepdims=True)
                chances = jnp.exp(mm(k, q_h, 1, 1) + bias_column[:, :1] - lse[low : low + 1, :])
                slopes = mm(v, do_h, 1, 1)
                scores = (chances * (slopes - row_dots)).astype(BF)
                dqs.append(mm(scores, k, 0, 0))
                dks.append(mm(scores, q_h, 1, 0))
                dvs.append(mm(chances.astype(BF), do_h, 1, 0))
            dq = (jnp.where(lanes_of(0), dqs[0], dqs[1]) * SCALE).astype(BF)
            out_ref[at, pl.ds(pl.multiple_of(h * PAIR, PAIR), PAIR)] = dq
            dk_sum[...] += dks[0] + dks[1]
            dv_sum[...] += dvs[0] + dvs[1]
            return 0

        lax.fori_loop(0, blocks, step, 0)

        def finish(j):
            for move in key_moves[j] + key_moves[j + pairs]:
                move.wait_recv()
            for first, kept, total in ((0, j, dk_own), (pairs, j + pairs, dv_own)):
                value = total[...]
                for slot in range(others):
                    value = value + arrived[slot, kept].astype(F32)
                out_ref[:, width + PAIR * kept : width + PAIR * (kept + 1)] = value.astype(BF)

        for j in range(pairs):

            @pl.when(h == j)
            def _(j=j):
                if j > 0:
                    finish(j - 1)
                dk_own[...] = dk_sum[0:rows, :]
                dv_own[...] = dv_sum[0:rows, :]
                for slot in range(others):
                    away = slice(rows * (slot + 1), rows * (slot + 2))
                    parted[slot, j] = dk_sum[away, :].astype(BF)
                    parted[slot, j + pairs] = dv_sum[away, :].astype(BF)
                for move in key_moves[j] + key_moves[j + pairs]:
                    move.start()
                if j == pairs - 1:
                    for task in tail:
                        next(task, None)
                    finish(j)
                    for moves in key_moves:
                        for move in moves:
                            move.wait_send()

    column = lambda first: pl.BlockSpec((rows, PAIR), lambda h: (0, h + first))
    other = lambda first: pl.BlockSpec((others, 1, rows, PAIR), lambda h: (0, h + first, 0, 0))
    whole = lambda shape: pl.BlockSpec(shape, lambda h: (0,) * len(shape))
    shard = grads[0].shape[4] if n else 0
    shapes = (
        [jax.ShapeDtypeStruct((rows, 3 * width), BF)]
        + [jax.ShapeDtypeStruct((shard, g.shape[5]), F32) for g in grads]
        + [jax.ShapeDtypeStruct((8, 128), F32)]
    )
    scratch = [
        pltpu.VMEM((keys, PAIR), F32),
        pltpu.VMEM((keys, PAIR), F32),
        pltpu.VMEM((rows, PAIR), F32),
        pltpu.VMEM((rows, PAIR), F32),
        pltpu.VMEM((others, 2 * pairs, rows, PAIR), BF),
        pltpu.VMEM((others, 2 * pairs, rows, PAIR), BF),
        pltpu.VMEM((keys, PAIR), F32),
        sems(copies),
        sems(copies),
        sems(len(parts)),
    ]
    for j, columns, order in parts:
        scratch += scatter_scratch(dims, shard, columns, order)
    return pl.pallas_call(
        body,
        grid=(pairs,),
        in_specs=[
            column(0),
            column(pairs),
            column(2 * pairs),
            other(0),
            other(pairs),
            whole((1, keys)),
            column(0),
            column(0),
            column(0),
        ]
        + [ANY] * n,
        out_specs=[whole(s.shape) for s in shapes],
        out_shape=shapes,
        scratch_shapes=scratch,
        compiler_params=pltpu.CompilerParams(
            collective_id=number, has_side_effects=True, vmem_limit_bytes=60 * MIB
        ),
        cost_estimate=pl.CostEstimate(
            flops=40 * rows * keys * width, bytes_accessed=16 * keys * width, transcendentals=rows * keys * HEADS
        ),
        name="attend_back",
    )(project, project, project, kv, kv, bias, mixed, logs, back, *grads)


def rms_norm(value, gain):
    return value * lax.rsqrt(jnp.mean(value * value, -1, keepdims=True) + EPS) * gain


def gated(gate_part, up_part):
    return jax.nn.gelu(gate_part, approximate=True) * up_part


def adam_step(master, grad, first, second, factor, rate, decay):
    clipped = factor * grad
    first_new = BETA_ONE * first + (1.0 - BETA_ONE) * clipped
    second_new = BETA_TWO * second + (1.0 - BETA_TWO) * clipped * clipped
    corrected = first_new / (1.0 - BETA_ONE**STEP)
    spread = jnp.sqrt(second_new / (1.0 - BETA_TWO**STEP)) + ADAM_EPS
    master_new = master - rate * (corrected / spread + decay * master)
    return (master_new, first_new, second_new)


def grid_of(n_img):
    big_y = max(d for d in range(1, n_img + 1) if n_img % d == 0 and d * d <= n_img)
    return big_y, n_img // big_y


def on_device(
    patches,
    cotangent,
    valid_counts,
    qkv_master,
    out_master,
    in_master,
    down_master,
    gain_master,
    qkv_first,
    out_first,
    in_first,
    down_first,
    gain_first,
    qkv_second,
    out_second,
    in_second,
    down_second,
    gain_second,
):
    images, band_rows, width = patches.shape
    n_img, n_band = lax.axis_size("img"), lax.axis_size("band")
    share = n_band // images
    big_y, big_x = grid_of(n_img)
    dims = (big_y, big_x, n_band // 2, share)
    rows = images * band_rows
    shard = qkv_master.shape[0]
    own_comm = shard % 8 == 0
    both = ("img", "band")

    places = [[s * share + r for s in range(images)] for r in range(share)]

    def exchange(chunks):
        return lax.all_to_all(chunks, "band", 0, 0, axis_index_groups=places, tiled=True)

    def flat(got):
        return [g.reshape(width, g.shape[-1]) for g in got]

    def blocks_of(grads):
        return [g.astype(BF).reshape(dims[:3] + (2, shard, g.shape[1])) for g in grads]

    gains_block = jnp.pad(jnp.transpose(gain_master).astype(BF), ((0, 0), (0, 126)))
    early = [qkv_master.astype(BF), gains_block]
    late = [
        jnp.transpose(out_master).astype(BF),
        in_master.astype(BF),
        jnp.transpose(down_master).astype(BF),
    ]
    if own_comm:
        w_qkv, gains, tokens_low = gather_call(dims, "gather", 0, early, patches)
        w_qkv, gains = flat([w_qkv, gains])
    else:
        w_qkv, gains = [lax.all_gather(b, both, axis=0, tiled=True) for b in early]
        tokens_low = exchange(patches)
    gain_one = gains[:, 0].astype(F32)
    gain_two = gains[:, 1].astype(F32)

    band = lax.axis_index("band")
    image, part = band // share, band % share
    count = lax.dynamic_index_in_dim(valid_counts, image, 0, keepdims=False)
    own_places = (
        (jnp.arange(images, dtype=jnp.int32)[:, None] * share + part) * band_rows
        + jnp.arange(band_rows, dtype=jnp.int32)[None, :]
    ).reshape(rows, 1)
    row_keep = (own_places < count).astype(F32)
    key_places = (
        (
            jnp.arange(images, dtype=jnp.int32)[None, :, None] * share
            + lax.rem(part + jnp.arange(share, dtype=jnp.int32), share)[:, None, None]
        )
        * band_rows
        + jnp.arange(band_rows, dtype=jnp.int32)[None, None, :]
    ).reshape(1, share * rows)
    bias = jnp.where(key_places < count, 0.0, NEG).astype(F32)

    tokens = tokens_low.reshape(rows, width).astype(F32)
    normed_a = rms_norm(tokens, gain_one).astype(BF)
    project = jnp.dot(normed_a, w_qkv, preferred_element_type=F32).astype(BF)
    attended, log_sums, kv, *late_all = attend(dims, 1, project, bias, 256, late if own_comm else [])
    if own_comm:
        w_out_t, w_in, w_down_t = flat(late_all)
    else:
        w_out_t, w_in, w_down_t = [lax.all_gather(b, both, axis=0, tiled=True) for b in late]
    hidden_units = w_down_t.shape[1]
    cotangent_later, attended = lax.optimization_barrier((cotangent, attended))
    cotangent_low = exchange(cotangent_later)

    middle = tokens + mm(attended, w_out_t, 1, 1)
    normed_b = rms_norm(middle, gain_two).astype(BF)
    gate_up = jnp.dot(normed_b, w_in, preferred_element_type=F32)
    gate_part = gate_up[:, :hidden_units]
    up_part = gate_up[:, hidden_units:]
    hidden = gated(gate_part, up_part).astype(BF)
    result = row_keep * (middle + mm(hidden, w_down_t, 1, 1))
    result_low = result.astype(BF).reshape(images, band_rows, width)
    back_result = row_keep * cotangent_low.reshape(rows, width).astype(F32)
    back_low = back_result.astype(BF)
    grad_down_t = mm(back_low, hidden, 0, 0)
    back_hidden = jnp.dot(back_low, w_down_t, preferred_element_type=F32)
    _, gate_back = jax.vjp(gated, gate_part, up_part)
    back_gate, back_up = gate_back(back_hidden)
    back_gate_up = jnp.concatenate([back_gate, back_up], 1).astype(BF)
    grad_in = mm(normed_b, back_gate_up, 0, 0)
    back_normed_b = mm(back_gate_up, w_in, 1, 1)
    _, second_back = jax.vjp(rms_norm, middle, gain_two)
    back_middle_norm, grad_gain_two = second_back(back_normed_b)
    back_middle = back_result + back_middle_norm
    back_branch = back_middle.astype(BF)
    grad_out_t = mm(back_branch, attended, 0, 0)
    back_attended = jnp.dot(back_branch, w_out_t, preferred_element_type=F32).astype(BF)

    output = exchange(result_low)
    late_grads = [grad_out_t, grad_in, grad_down_t]
    back_project, *late_sums, squares = attend_back(
        dims,
        2,
        project,
        kv,
        bias,
        attended,
        log_sums,
        back_attended,
        256,
        blocks_of(late_grads) if own_comm else [],
    )
    if not own_comm:
        late_sums = [lax.psum_scatter(g, both, scatter_dimension=0, tiled=True) for g in late_grads]
    out_sum, in_sum, down_sum = late_sums
    back_project, output = lax.optimization_barrier((back_project, output))
    grad_qkv = mm(normed_a, back_project, 0, 0)
    back_normed_a = mm(back_project, w_qkv, 1, 1)
    _, first_back = jax.vjp(rms_norm, tokens, gain_one)
    back_tokens, grad_gain_one = first_back(back_normed_a)
    back_rows = (back_middle + back_tokens).astype(BF).reshape(images, band_rows, width)
    grad_gains = jnp.pad(jnp.stack([grad_gain_one, grad_gain_two], 1), ((0, 0), (0, 126)))
    early_grads = [grad_qkv, grad_gains]
    if own_comm:
        qkv_sum, gain_sum, back_input, total = scatter_call(
            dims, "scatter", 3, blocks_of(early_grads), back_rows, squares
        )
    else:
        qkv_sum, gain_sum = [lax.psum_scatter(g, both, scatter_dimension=0, tiled=True) for g in early_grads]
        back_input = exchange(back_rows)
        squares = sum(jnp.sum(g * g) for g in late_sums + [qkv_sum, gain_sum])
        total = lax.psum(jnp.broadcast_to(squares, (8, 128)), both)
    grad_norm = jnp.sqrt(total[0, 0])
    factor = jnp.minimum(1.0, CLIP / grad_norm)
    shards = (
        qkv_sum,
        jnp.transpose(out_sum),
        in_sum,
        jnp.transpose(down_sum),
        jnp.transpose(gain_sum[:, :2]),
    )
    masters = (qkv_master, out_master, in_master, down_master, gain_master)
    firsts = (qkv_first, out_first, in_first, down_first, gain_first)
    seconds = (qkv_second, out_second, in_second, down_second, gain_second)
    updated = [
        adam_step(masters[j], shards[j], firsts[j], seconds[j], factor, RATES[j], DECAYS[j]) for j in range(5)
    ]
    return (
        (output, back_input, grad_norm)
        + tuple(updated[j][0] for j in range(5))
        + tuple(updated[j][1] for j in range(5))
        + tuple(updated[j][2] for j in range(5))
        + tuple(updated[j][0].astype(BF) for j in range(5))
    )


def solution(mesh):
    rows_split, columns_split = P(("img", "band"), None), P(None, ("img", "band"))
    weights = (rows_split, columns_split, rows_split, columns_split, columns_split)
    tokens = P("img", "band", None)
    return jax.shard_map(
        on_device,
        mesh=mesh,
        in_specs=(tokens, tokens, P("img")) + weights * 3,
        out_specs=(tokens, tokens, P()) + weights * 4,
        check_vma=False,
    )
```

```python
import functools

import jax
import jax.numpy as jnp
from jax import lax
from jax.experimental import pallas as pl
from jax.experimental.pallas import tpu as pltpu
from jax.sharding import PartitionSpec as P

HEADS = 12
HEAD_DIM = 64
PAIR = 2 * HEAD_DIM
STEP = 10
EPS = 1e-06
NEG = -1000000000.0
SCALE = 0.125
CLIP = 1.0
BETA_ONE = 0.9
BETA_TWO = 0.999
ADAM_EPS = 1e-08
RATES = (0.06, 0.5, 0.06, 0.04, 0.5)
DECAYS = (0.1, 0.1, 0.1, 0.1, 0.0)
BF = jnp.bfloat16
F32 = jnp.float32
MESH = pl.DeviceIdType.MESH
ANY = pl.BlockSpec(memory_space=pl.ANY)
MIB = 2**20


class Net:
    def __init__(self, dims, send, recv, local):
        self.dims = dims
        big_y, big_x, big_z, share = dims
        img, band = lax.axis_index("img"), lax.axis_index("band")
        self.y, self.x = img // big_x, img % big_x
        self.z, self.c = band // 2, band % 2
        self.twin = 1 - self.c
        image, self.part = band // share, band % share
        self.image, self.images = image, 2 * big_z // share
        self.send, self.recv, self.local = send, recv, local
        self.used, self.used_local = 0, 0
        self.lines = {}
        for name, size in zip("yxzc", (big_y, big_x, big_z, 2)):
            places = []
            for d in range(1, size):
                at = dict(y=self.y, x=self.x, z=self.z, c=self.c)
                at[name] = lax.rem(at[name] + d, size)
                places.append((at[name], (at["y"] * big_x + at["x"], at["z"] * 2 + at["c"])))
            self.lines[name] = places
        self.lines["image"] = []
        for d in range(1, self.images):
            other = lax.rem(image + d, self.images)
            self.lines["image"].append((other, (img, other * share + self.part)))
        self.lines["share"] = []
        for d in range(1, share):
            other = lax.rem(self.part + d, share)
            self.lines["share"].append((other, (img, image * share + other)))

    def line(self, name):
        return self.lines[name]

    def greet(self, kinds):
        barrier = pltpu.get_barrier_semaphore()
        count = 0
        for kind in kinds:
            for _, target in self.lines[kind]:
                pl.semaphore_signal(barrier, inc=1, device_id=target, device_id_type=MESH)
            count += len(self.lines[kind])
        pl.semaphore_wait(barrier, count)

    def copy(self, source, target_ref, target):
        made = self.plan(source, target_ref, target)
        made.start()
        return made

    def plan(self, source, target_ref, target):
        self.used += 1
        return Move(source, target_ref, self.send, self.recv, self.used - 1, target)

    def local_copy(self, source, target_ref):
        self.used_local += 1
        made = Move(source, target_ref, None, self.local, self.used_local - 1, None)
        made.start()
        return made


class Part:
    def __init__(self, ref, index=None):
        self.ref, self.index = ref, index

    def __getitem__(self, index):
        return Part(self.ref, index)

    def view(self):
        return self.ref if self.index is None else self.ref.at[self.index]


class Move:
    def __init__(self, source, target_ref, send, recv, at, target):
        self.source, self.target_ref = source, target_ref
        self.send, self.recv, self.at, self.target = send, recv, at, target

    def build(self):
        if self.target is None:
            return pltpu.make_async_copy(self.source.view(), self.target_ref.view(), self.recv.at[self.at])
        return pltpu.make_async_remote_copy(
            src_ref=self.source.view(),
            dst_ref=self.target_ref.view(),
            send_sem=self.send.at[self.at],
            recv_sem=self.recv.at[self.at],
            device_id=self.target,
            device_id_type=MESH,
        )

    def start(self):
        self.build().start()

    def wait(self):
        self.build().wait()

    def wait_recv(self):
        self.build().wait_recv()

    def wait_send(self):
        self.build().wait_send()


def drive(tasks):
    waiting = list(tasks)
    turn = 0
    while waiting:
        left = []
        for start, task in waiting:
            if start <= turn:
                try:
                    next(task)
                except StopIteration:
                    continue
            left.append((start, task))
        waiting = left
        turn += 1


def exchange_images(net, source, target, idle=1):
    moves = [net.copy(Part(source)[other], Part(target)[net.image], dev) for other, dev in net.line("image")]
    own = net.local_copy(Part(source)[net.image], Part(target)[net.image])
    for _ in range(idle):
        yield
    for move in moves:
        move.wait_recv()
    own.wait()
    for move in moves:
        move.wait_send()


def gather(net, source, target, columns, order):
    cols = pl.ds(*columns)
    y, x, z, c = net.y, net.x, net.z, net.c
    own = net.local_copy(Part(source)[:, cols], Part(target)[y, x, z, c, :, cols])
    sent = [net.copy(Part(source)[:, cols], Part(target)[y, x, z, c, :, cols], dev) for _, dev in net.line("z")]
    yield
    own.wait()
    for move in sent:
        move.wait_recv()
    part = Part(target)[y, x, :, c, :, cols]
    moves = [net.copy(part, part, dev) for _, dev in net.line(order[0])]
    sent += moves
    yield
    for move in moves:
        move.wait_recv()
    part = Part(target)[y, :, :, c, :, cols] if order[0] == "x" else Part(target)[:, x, :, c, :, cols]
    moves = [net.copy(part, part, dev) for _, dev in net.line(order[1])]
    sent += moves
    yield
    for move in moves:
        move.wait_recv()
    part = Part(target)[:, :, :, c, :, cols]
    moves = [net.copy(part, part, dev) for _, dev in net.line("c")]
    sent += moves
    yield
    for move in moves:
        move.wait_recv()
    for move in sent:
        move.wait_send()


def gather_copies(dims):
    return dims[0] + dims[1] + dims[2] - 3 + 1


def scatter(net, grad, held, from_core, from_first, from_second, from_z, out, squares, columns, order):
    big_y, big_x, big_z, _ = net.dims
    cols = pl.ds(*columns)
    y, x, z, c = net.y, net.x, net.z, net.c
    sent = []
    (_, twin), = net.line("c")
    moves = [net.copy(Part(grad)[:, :, :, net.twin, :, cols], Part(from_core), twin)]
    sent += moves
    own = net.local_copy(Part(grad)[:, :, :, c, :, cols], Part(held))
    yield
    own.wait()
    moves[0].wait_recv()

    def first_add(at, _):
        a, b, d = at // (big_x * big_z), (at // big_z) % big_x, at % big_z
        held[a, b, d] = (held[a, b, d].astype(F32) + from_core[a, b, d].astype(F32)).astype(BF)
        return 0

    lax.fori_loop(0, big_y * big_x * big_z, first_add, 0)
    moves = []
    for slot, (other, dev) in enumerate(net.line(order[0])):
        part = Part(held)[:, other] if order[0] == "x" else Part(held)[other]
        moves.append(net.copy(part, Part(from_first)[slot], dev))
    sent += moves
    yield
    for move in moves:
        move.wait_recv()
    left = big_y if order[0] == "x" else big_x

    def second_add(at, _):
        a, d = at // big_z, at % big_z
        place = (a, x, d) if order[0] == "x" else (y, a, d)
        total = held[place].astype(F32)
        for slot in range(len(moves)):
            total = total + from_first[slot, a, d].astype(F32)
        held[place] = total.astype(BF)
        return 0

    lax.fori_loop(0, left * big_z, second_add, 0)
    moves = []
    for slot, (other, dev) in enumerate(net.line(order[1])):
        part = Part(held)[other, x] if order[1] == "y" else Part(held)[y, other]
        moves.append(net.copy(part, Part(from_second)[slot], dev))
    sent += moves
    yield
    for move in moves:
        move.wait_recv()

    def third_add(d, _):
        total = held[y, x, d].astype(F32)
        for slot in range(len(moves)):
            total = total + from_second[slot, d].astype(F32)
        held[y, x, d] = total.astype(BF)
        return 0

    lax.fori_loop(0, big_z, third_add, 0)
    moves = []
    for slot, (other, dev) in enumerate(net.line("z")):
        moves.append(net.copy(Part(held)[y, x, other], Part(from_z)[slot], dev))
    sent += moves
    yield
    for move in moves:
        move.wait_recv()
    total = held[y, x, z].astype(F32)
    for slot in range(len(moves)):
        total = total + from_z[slot].astype(F32)
    out[:, columns[0] : columns[0] + columns[1]] = total
    tile = squares[...]
    for a in range(total.shape[0] // 8):
        for b in range(columns[1] // 128):
            piece = total[8 * a : 8 * a + 8, 128 * b : 128 * b + 128]
            tile = tile + piece * piece
    squares[...] = tile
    for move in sent:
        move.wait_send()


def scatter_scratch(dims, rows, columns, order):
    big_y, big_x, big_z, _ = dims
    width = columns[1]
    ahead, left = (big_x, big_y) if order[0] == "x" else (big_y, big_x)
    return [
        pltpu.VMEM((big_y, big_x, big_z, rows, width), BF),
        pltpu.VMEM((big_y, big_x, big_z, rows, width), BF),
        pltpu.VMEM((ahead - 1, left, big_z, rows, width), BF),
        pltpu.VMEM((left - 1, big_z, rows, width), BF),
        pltpu.VMEM((big_z - 1, rows, width), BF),
    ]


def sum_tiles(net, tile, slots):
    first = 0
    for name in "cxyz":
        places = net.line(name)
        me = dict(y=net.y, x=net.x, z=net.z, c=net.c)[name]
        size = len(places) + 1
        slots[first + me] = tile[...]
        moves = [net.copy(Part(tile), Part(slots)[first + me], dev) for _, dev in places]
        for move in moves:
            move.wait_recv()
        for move in moves:
            move.wait_send()
        total = slots[first]
        for d in range(1, size):
            total = total + slots[first + d]
        tile[...] = total
        first += size


def sems(count):
    return pltpu.SemaphoreType.DMA((max(count, 1),))


def halves(width):
    units = width // 128
    low = (units + 1) // 2 * 128
    if low == width:
        return [((0, width), "xy")]
    return [((0, low), "xy"), ((low, width - low), "yx")]


def pieces(width, groups):
    found = []
    for group in range(groups):
        for columns, order in halves(width // groups):
            found.append((group, (columns[0] + group * (width // groups), columns[1]), order))
    return found


def gather_call(dims, name, number, blocks, images=None):
    big_y, big_x, big_z, share = dims
    parts = [halves(block.shape[1]) for block in blocks]
    copies = sum(len(p) for p in parts) * gather_copies(dims)
    local = sum(len(p) for p in parts)
    n = len(blocks)
    with_images = images is not None
    if with_images:
        copies += images.shape[0] - 1
        local += 1

    def body(*refs):
        ins, rest = refs[: n + with_images], refs[n + with_images :]
        outs, (send, recv, local_sem) = rest[: n + with_images], rest[n + with_images :]
        net = Net(dims, send, recv, local_sem)
        net.greet("zxyc" if not with_images else ["z", "x", "y", "c", "image"])
        tasks = []
        for j in range(n):
            for columns, order in parts[j]:
                tasks.append((0, gather(net, ins[j], outs[j], columns, order)))
        if with_images:
            tasks.append((1, exchange_images(net, ins[n], outs[n], 3)))
        drive(tasks)

    args = list(blocks) + ([images] if with_images else [])
    shapes = [jax.ShapeDtypeStruct((big_y, big_x, big_z, 2) + b.shape, b.dtype) for b in blocks]
    if with_images:
        shapes.append(jax.ShapeDtypeStruct(images.shape, images.dtype))
    return pl.pallas_call(
        body,
        out_shape=shapes,
        in_specs=[ANY] * len(args),
        out_specs=[ANY] * len(shapes),
        scratch_shapes=[sems(copies), sems(copies), sems(local)],
        compiler_params=pltpu.CompilerParams(collective_id=number, has_side_effects=True),
        name=name,
    )(*args)


def scatter_call(dims, name, number, grads, images, squares):
    big_y, big_x, big_z, _ = dims
    rows = grads[0].shape[4]
    parts = [(j, columns, order) for j, g in enumerate(grads) for columns, order in halves(g.shape[5])]
    copies = (len(parts) + 1) * gather_copies(dims) + images.shape[0] - 1
    local = len(parts) + 1
    n = len(grads)
    scratch = [sems(copies), sems(copies), sems(local)]
    for _, columns, order in parts:
        scratch += scatter_scratch(dims, rows, columns, order)
    scratch += [pltpu.VMEM((8, 128), F32), pltpu.VMEM((2 + big_x + big_y + big_z, 8, 128), F32)]

    def body(*refs):
        ins, outs, rest = refs[: n + 2], refs[n + 2 : 2 * n + 4], refs[2 * n + 4 :]
        tile, slots = rest[3 + 5 * len(parts) :]
        net = Net(dims, *rest[:3])
        net.greet(["z", "x", "y", "c", "image"])
        tile[...] = ins[n + 1][...]
        tasks = []
        for k, (j, columns, order) in enumerate(parts):
            buffers = rest[3 + 5 * k : 8 + 5 * k]
            tasks.append((0, scatter(net, ins[j], *buffers, outs[j], tile, columns, order)))
        tasks.append((0, exchange_images(net, ins[n], outs[n], 4)))
        drive(tasks)
        sum_tiles(net, tile, slots)
        outs[n + 1][...] = jnp.broadcast_to(jnp.sum(tile[...], keepdims=True), (8, 128))

    vmem = pl.BlockSpec(memory_space=pltpu.VMEM)
    shapes = [jax.ShapeDtypeStruct((rows, g.shape[5]), F32) for g in grads]
    shapes += [jax.ShapeDtypeStruct(images.shape, images.dtype), jax.ShapeDtypeStruct((8, 128), F32)]
    return pl.pallas_call(
        body,
        out_shape=shapes,
        in_specs=[ANY] * (n + 1) + [vmem],
        out_specs=[vmem] * n + [ANY, vmem],
        scratch_shapes=scratch,
        compiler_params=pltpu.CompilerParams(
            collective_id=number, has_side_effects=True, vmem_limit_bytes=60 * MIB
        ),
        name=name,
    )(*grads, images, squares)


def mm(a, b, ca, cb):
    return lax.dot_general(a, b, (((ca,), (cb,)), ((), ())), preferred_element_type=F32)


def at_turn(turn, events):
    for when in sorted(events):

        @pl.when(turn == when)
        def _(when=when):
            for task in events[when]:
                next(task, None)


def schedule(tasks, turns, last):
    events, tail = {}, []
    for task, when in zip(tasks, turns):
        for turn in when:
            if turn < last:
                events.setdefault(turn, []).append(task)
            else:
                tail.append(task)
    return events, tail


def lanes_of(h):
    lane = lax.broadcasted_iota(jnp.int32, (1, PAIR), 1) < HEAD_DIM
    return lane if h == 0 else ~lane


def attend(dims, number, project, bias, block, weights, chunks):
    big_y, big_x, big_z, share = dims
    rows, width = project.shape[0], project.shape[1] // 3
    pairs = width // PAIR
    others = share - 1
    blocks = rows // block
    n = len(weights)
    parts = [
        (j, columns, order, GATHER_TURNS[j][group])
        for j, w in enumerate(weights)
        for group, columns, order in pieces(w.shape[1], len(GATHER_TURNS[j]))
    ]
    copies = len(parts) * gather_copies(dims) + others * 2 * pairs + chunks.shape[0] - 1
    per_turn = max(blocks // 4, 1)

    def body(*refs):
        q_ref, k_ref, v_ref, project_ref, bias_ref, chunks_in = refs[:6]
        blocks_in, refs = refs[6 : 6 + n], refs[6 + n :]
        o_ref, l_ref, kv_out, chunks_out, refs = refs[0], refs[1], refs[2], refs[3], refs[4:]
        gathered, (kv_held, send, recv, local) = refs[:n], refs[n:]
        h = pl.program_id(0)
        net = Net(dims, send, recv, local)

        def move_keys(j):
            moves = []
            for slot, (_, target) in enumerate(net.line("share")):
                source = Part(project_ref)[:, pl.ds(width + PAIR * j, PAIR)]
                moves.append(net.plan(source, Part(kv_held)[others - 1 - slot, j], target))
            return moves

        key_moves = [move_keys(j) for j in range(2 * pairs)]
        keep = Move(Part(kv_held), Part(kv_out), None, local, len(parts) + 1, None)
        tasks = [gather(net, blocks_in[j], gathered[j], columns, order) for j, columns, order, _ in parts]
        tasks.append(exchange_images(net, chunks_in, chunks_out))
        turns = [turn for _, _, _, turn in parts] + [CHUNK_TURNS]
        events, tail = schedule(tasks, turns, 4 * pairs)

        @pl.when(h == 0)
        def _():
            net.greet(["z", "x", "y", "c", "image"] + (["share"] if share > 2 else []))
            for j in range(pairs):
                for move in key_moves[j] + key_moves[j + pairs]:
                    move.start()

        for j in range(pairs):

            @pl.when(h == j)
            def _(j=j):
                for move in key_moves[j] + key_moves[j + pairs]:
                    move.wait_recv()
                if j == pairs - 1:
                    keep.start()

        def step(i, _):
            at_turn(h * 4 + i // per_turn, events)
            at = pl.ds(pl.multiple_of(i * block, block), block)
            k = jnp.concatenate([k_ref[...]] + [kv_held[s, h] for s in range(others)], 0)
            v = jnp.concatenate([v_ref[...]] + [kv_held[s, h + pairs] for s in range(others)], 0)
            q = q_ref[at, :] * jnp.asarray(SCALE, BF)
            mixed, logs = [], []
            for half in range(2):
                scores = mm(jnp.where(lanes_of(half), q, jnp.zeros_like(q)), k, 1, 1) + bias_ref[...]
                highest = jnp.max(scores, -1, keepdims=True)
                powers = jnp.exp(scores - highest)
                total = jnp.sum(powers, -1, keepdims=True)
                mixed.append(mm(powers.astype(BF), v, 1, 0) / total)
                logs.append(highest + jnp.log(total))
            o_ref[at, :] = jnp.where(lanes_of(0), mixed[0], mixed[1]).astype(BF)
            l_ref[at, :] = jnp.where(lanes_of(0), logs[0], logs[1])
            return 0

        lax.fori_loop(0, blocks, step, 0)

        @pl.when(h == pairs - 1)
        def _():
            for task in tail:
                next(task, None)
            for moves in key_moves:
                for move in moves:
                    move.wait_send()
            keep.wait()

    column = lambda first: pl.BlockSpec((rows, PAIR), lambda h: (0, h + first))
    keys = rows * share
    shapes = [
        jax.ShapeDtypeStruct((rows, width), BF),
        jax.ShapeDtypeStruct((rows, width), F32),
        jax.ShapeDtypeStruct((others, 2 * pairs, rows, PAIR), BF),
        jax.ShapeDtypeStruct(chunks.shape, chunks.dtype),
    ] + [jax.ShapeDtypeStruct((big_y, big_x, big_z, 2) + w.shape, w.dtype) for w in weights]
    return pl.pallas_call(
        body,
        grid=(pairs,),
        in_specs=[column(0), column(pairs), column(2 * pairs), ANY, pl.BlockSpec((1, keys), lambda h: (0, 0))]
        + [ANY] * (1 + n),
        out_specs=[column(0), column(0), ANY, ANY] + [ANY] * n,
        out_shape=shapes,
        scratch_shapes=[
            pltpu.VMEM((others, 2 * pairs, rows, PAIR), BF),
            sems(copies),
            sems(copies),
            sems(len(parts) + 2),
        ],
        compiler_params=pltpu.CompilerParams(
            collective_id=number, has_side_effects=True, vmem_limit_bytes=56 * MIB
        ),
        cost_estimate=pl.CostEstimate(
            flops=16 * rows * keys * width, bytes_accessed=8 * keys * width, transcendentals=rows * keys * HEADS
        ),
        name="attend",
    )(project, project, project, project, bias, chunks, *weights)


GATHER_TURNS = (
    ((0, 1, 2, 4, 6),),
    ((0, 3, 6, 11, 13), (1, 7, 13, 18, 20)),
    ((2, 10, 17, 22, 24),),
)
CHUNK_TURNS = (8, 24)
SCATTER_TURNS = ((1, 4, 11, 17, 24), (0, 2, 8, 14, 20), (1, 3, 9, 15, 21))
RESULT_TURNS = (0, 24)


def attend_back(dims, number, project, kv, bias, mixed, logs, back, block, grads, chunks):
    big_y, big_x, big_z, share = dims
    rows, width = mixed.shape
    pairs = width // PAIR
    others = share - 1
    blocks = rows // block
    keys = rows * share
    n = len(grads)
    parts = [(j, columns, order) for j, g in enumerate(grads) for columns, order in halves(g.shape[5])]
    copies = len(parts) * gather_copies(dims) + others * 2 * pairs + chunks.shape[0] - 1
    per_turn = max(blocks // 4, 1)

    def body(*refs):
        q_ref, k_ref, v_ref, k_other, v_other, bias_ref, mixed_ref, logs_ref, back_ref = refs[:9]
        grads_in, chunks_in, refs = refs[9 : 9 + n], refs[9 + n], refs[10 + n :]
        out_ref, sums, squares, chunks_out, refs = refs[0], refs[1 : 1 + n], refs[1 + n], refs[2 + n], refs[3 + n :]
        dk_sum, dv_sum, dk_own, dv_own, parted, arrived, bias_column = refs[:7]
        send, recv, local = refs[7:10]
        buffers = refs[10:]
        h = pl.program_id(0)
        net = Net(dims, send, recv, local)

        def move_keys(j):
            moves = []
            for slot, (_, target) in enumerate(net.line("share")):
                moves.append(net.plan(Part(parted)[slot, j], Part(arrived)[others - 1 - slot, j], target))
            return moves

        key_moves = [move_keys(j) for j in range(2 * pairs)]
        tasks = [
            scatter(net, grads_in[j], *buffers[5 * k : 5 * k + 5], sums[j], squares, columns, order)
            for k, (j, columns, order) in enumerate(parts)
        ]
        tasks.append(exchange_images(net, chunks_in, chunks_out))
        turns = [SCATTER_TURNS[j] for j, _, _ in parts] + [RESULT_TURNS]
        events, tail = schedule(tasks, turns, 4 * pairs)

        @pl.when(h == 0)
        def _():
            net.greet(["z", "x", "y", "c", "image"] + (["share"] if share > 2 else []))
            squares[...] = jnp.zeros_like(squares)
            bias_column[...] = jnp.transpose(jnp.broadcast_to(bias_ref[...], (PAIR, keys)))

        dk_sum[...] = jnp.zeros_like(dk_sum)
        dv_sum[...] = jnp.zeros_like(dv_sum)

        def step(i, _):
            at_turn(h * 4 + i // per_turn, events)
            at = pl.ds(pl.multiple_of(i * block, block), block)
            k = jnp.concatenate([k_ref[...]] + [k_other[s, 0] for s in range(others)], 0)
            v = jnp.concatenate([v_ref[...]] + [v_other[s, 0] for s in range(others)], 0)
            q, do = q_ref[at, :] * jnp.asarray(SCALE, BF), back_ref[at, :]
            lse = jnp.transpose(logs_ref[at, :])
            products = jnp.transpose(do.astype(F32) * mixed_ref[at, :].astype(F32))
            dqs, dks, dvs = [], [], []
            for half in range(2):
                low, high = half * HEAD_DIM, (half + 1) * HEAD_DIM
                q_h = jnp.where(lanes_of(half), q, jnp.zeros_like(q))
                do_h = jnp.where(lanes_of(half), do, jnp.zeros_like(do))
                row_dots = jnp.sum(products[low:high, :], 0, keepdims=True)
                chances = jnp.exp(mm(k, q_h, 1, 1) + bias_column[:, :1] - lse[low : low + 1, :])
                slopes = mm(v, do_h, 1, 1)
                scores = (chances * (slopes - row_dots)).astype(BF)
                dqs.append(mm(scores, k, 0, 0))
                dks.append(mm(scores, q_h, 1, 0))
                dvs.append(mm(chances.astype(BF), do_h, 1, 0))
            dq = (jnp.where(lanes_of(0), dqs[0], dqs[1]) * SCALE).astype(BF)
            out_ref[at, pl.ds(pl.multiple_of(h * PAIR, PAIR), PAIR)] = dq
            dk_sum[...] += dks[0] + dks[1]
            dv_sum[...] += dvs[0] + dvs[1]
            return 0

        lax.fori_loop(0, blocks, step, 0)

        def finish(j):
            for move in key_moves[j] + key_moves[j + pairs]:
                move.wait_recv()
            for first, kept, total in ((0, j, dk_own), (pairs, j + pairs, dv_own)):
                value = total[...]
                for slot in range(others):
                    value = value + arrived[slot, kept].astype(F32)
                out_ref[:, width + PAIR * kept : width + PAIR * (kept + 1)] = value.astype(BF)

        for j in range(pairs):

            @pl.when(h == j)
            def _(j=j):
                if j > 0:
                    finish(j - 1)
                dk_own[...] = dk_sum[0:rows, :]
                dv_own[...] = dv_sum[0:rows, :]
                for slot in range(others):
                    away = slice(rows * (slot + 1), rows * (slot + 2))
                    parted[slot, j] = dk_sum[away, :].astype(BF)
                    parted[slot, j + pairs] = dv_sum[away, :].astype(BF)
                for move in key_moves[j] + key_moves[j + pairs]:
                    move.start()
                if j == pairs - 1:
                    for task in tail:
                        next(task, None)
                    finish(j)
                    for moves in key_moves:
                        for move in moves:
                            move.wait_send()

    column = lambda first: pl.BlockSpec((rows, PAIR), lambda h: (0, h + first))
    other = lambda first: pl.BlockSpec((others, 1, rows, PAIR), lambda h: (0, h + first, 0, 0))
    whole = lambda shape: pl.BlockSpec(shape, lambda h: (0,) * len(shape))
    shard = grads[0].shape[4] if n else 0
    shapes = (
        [jax.ShapeDtypeStruct((rows, 3 * width), BF)]
        + [jax.ShapeDtypeStruct((shard, g.shape[5]), F32) for g in grads]
        + [jax.ShapeDtypeStruct((8, 128), F32)]
    )
    moved = jax.ShapeDtypeStruct(chunks.shape, chunks.dtype)
    scratch = [
        pltpu.VMEM((keys, PAIR), F32),
        pltpu.VMEM((keys, PAIR), F32),
        pltpu.VMEM((rows, PAIR), F32),
        pltpu.VMEM((rows, PAIR), F32),
        pltpu.VMEM((others, 2 * pairs, rows, PAIR), BF),
        pltpu.VMEM((others, 2 * pairs, rows, PAIR), BF),
        pltpu.VMEM((keys, PAIR), F32),
        sems(copies),
        sems(copies),
        sems(len(parts) + 1),
    ]
    for j, columns, order in parts:
        scratch += scatter_scratch(dims, shard, columns, order)
    return pl.pallas_call(
        body,
        grid=(pairs,),
        in_specs=[
            column(0),
            column(pairs),
            column(2 * pairs),
            other(0),
            other(pairs),
            whole((1, keys)),
            column(0),
            column(0),
            column(0),
        ]
        + [ANY] * (n + 1),
        out_specs=[whole(s.shape) for s in shapes] + [ANY],
        out_shape=shapes + [moved],
        scratch_shapes=scratch,
        compiler_params=pltpu.CompilerParams(
            collective_id=number, has_side_effects=True, vmem_limit_bytes=60 * MIB
        ),
        cost_estimate=pl.CostEstimate(
            flops=40 * rows * keys * width, bytes_accessed=16 * keys * width, transcendentals=rows * keys * HEADS
        ),
        name="attend_back",
    )(project, project, project, kv, kv, bias, mixed, logs, back, *grads, chunks)


def whole(shape):
    return pl.BlockSpec(shape, lambda i: (0,) * len(shape))


def kept(shape):
    return pl.BlockSpec(shape, lambda i: (0,) * len(shape), pipeline_mode=pl.Buffered(1))


def inverse_rms(value):
    return lax.rsqrt(jnp.mean(value * value, -1, keepdims=True) + EPS)


def norm_back(back, value, scale, gain):
    scaled = back * gain
    inner = jnp.mean(scaled * value, -1, keepdims=True)
    return scale * scaled - value * (scale * scale * scale * inner), back * (value * scale)


def project_call(tokens, weight, gains, block):
    rows, width = tokens.shape

    def body(x_ref, w_ref, g_ref, out_ref, gains_ref):
        gain_rows = jnp.transpose(g_ref[...].astype(F32))
        gains_ref[...] = gain_rows[:8]
        x = x_ref[...].astype(F32)
        normed = (x * inverse_rms(x) * gain_rows[0:1]).astype(BF)
        out_ref[...] = mm(normed, w_ref[...], 1, 0).astype(BF)

    return pl.pallas_call(
        body,
        grid=(rows // block,),
        in_specs=[pl.BlockSpec((block, width), lambda i: (i, 0)), kept(weight.shape), kept(gains.shape)],
        out_specs=[pl.BlockSpec((block, 3 * width), lambda i: (i, 0)), whole((8, width))],
        out_shape=[jax.ShapeDtypeStruct((rows, 3 * width), BF), jax.ShapeDtypeStruct((8, width), F32)],
        compiler_params=pltpu.CompilerParams(vmem_limit_bytes=40 * MIB),
        cost_estimate=pl.CostEstimate(
            flops=6 * rows * width * width, bytes_accessed=14 * width * width, transcendentals=rows
        ),
        name="project",
    )(tokens, weight, gains)


GELU_A = 0.7978845608028654
GELU_B = 0.044715


def mlp_call(tokens, attended, cotangent, keep, w_out_t, w_in, w_down_t, gains, block):
    rows, width = tokens.shape
    hidden_units = w_down_t.shape[1]
    steps = rows // block
    tile = 512
    in_tiles, down_tiles = 2 * hidden_units // tile, hidden_units // tile
    part = 512

    def body(
        x_ref, a_ref, c_ref, keep_ref, wo_ref, wi_ref, wd_ref, g_ref,
        result_ref, middle_ref, back_ref, gain_ref, g_out_ref, g_in_ref, g_down_ref,
        normed_t, low_t, branch_t, mixed, hidden, back_gu,
    ):
        i = pl.program_id(0)

        @pl.when(i == 0)
        def _():
            gain_ref[...] = jnp.zeros_like(gain_ref)

        @pl.when(i < steps)
        def _():
            at = pl.ds(pl.multiple_of(i * block, block), block)
            gain = g_ref[1:2, :]
            a = a_ref[...]
            mixed[at, :] = a
            middle = x_ref[...].astype(F32) + mm(a, wo_ref[...], 1, 1)
            scale = inverse_rms(middle)
            normed = (middle * scale * gain).astype(BF)
            normed_t[:, at] = jnp.transpose(normed)
            back_result = keep_ref[...] * c_ref[...].astype(F32)
            low = back_result.astype(BF)
            low_t[:, at] = jnp.transpose(low)
            result, back = middle, jnp.zeros_like(middle)
            for p in range(hidden_units // part):
                one = slice(p * part, (p + 1) * part)
                two = slice(hidden_units + p * part, hidden_units + (p + 1) * part)
                gate = mm(normed, wi_ref[:, one], 1, 0)
                up = mm(normed, wi_ref[:, two], 1, 0)
                back_hidden = mm(low, wd_ref[:, one], 1, 0)
                square = gate * gate
                bend = jnp.tanh(GELU_A * (gate + GELU_B * (gate * square)))
                half = 0.5 + 0.5 * bend
                curve = gate * half
                slope = half + (0.5 * GELU_A) * gate * (1.0 - bend * bend) * (1.0 + (3.0 * GELU_B) * square)
                hid = (curve * up).astype(BF)
                back_gate = (back_hidden * up * slope).astype(BF)
                back_up = (back_hidden * curve).astype(BF)
                hidden[at, one] = hid
                back_gu[at, one] = back_gate
                back_gu[at, two] = back_up
                result = result + mm(hid, wd_ref[:, one], 1, 1)
                back = back + mm(back_gate, wi_ref[:, one], 1, 1) + mm(back_up, wi_ref[:, two], 1, 1)
            result_ref[...] = (keep_ref[...] * result).astype(BF)
            into, gain_rows = norm_back(back, middle, scale, gain)
            gain_ref[0:1, :] += jnp.sum(gain_rows, 0, keepdims=True)
            back_middle = back_result + into
            middle_ref[...] = back_middle
            branch = back_middle.astype(BF)
            branch_t[:, at] = jnp.transpose(branch)
            back_ref[...] = mm(branch, wo_ref[...], 1, 0).astype(BF)

        @pl.when(i == steps)
        def _():
            g_out_ref[...] = mm(branch_t[...], mixed[...], 1, 0).astype(BF)

        for t in range(in_tiles):

            @pl.when(i == steps + 1 + t)
            def _(t=t):
                g_in_ref[...] = mm(normed_t[...], back_gu[:, t * tile : (t + 1) * tile], 1, 0).astype(BF)

        for t in range(down_tiles):

            @pl.when(i == steps + 1 + in_tiles + t)
            def _(t=t):
                g_down_ref[...] = mm(low_t[...], hidden[:, t * tile : (t + 1) * tile], 1, 0).astype(BF)

    row = lambda last: pl.BlockSpec((block, last), lambda i: (jnp.minimum(i, steps - 1), 0))
    return pl.pallas_call(
        body,
        grid=(steps + 1 + in_tiles + down_tiles,),
        in_specs=[
            row(width),
            row(width),
            row(width),
            row(1),
            kept(w_out_t.shape),
            kept(w_in.shape),
            kept(w_down_t.shape),
            kept(gains.shape),
        ],
        out_specs=[
            row(width),
            row(width),
            row(width),
            whole((8, width)),
            whole((width, width)),
            pl.BlockSpec((width, tile), lambda i: (0, jnp.clip(i - steps - 1, 0, in_tiles - 1))),
            pl.BlockSpec((width, tile), lambda i: (0, jnp.clip(i - steps - 1 - in_tiles, 0, down_tiles - 1))),
        ],
        out_shape=[
            jax.ShapeDtypeStruct((rows, width), BF),
            jax.ShapeDtypeStruct((rows, width), F32),
            jax.ShapeDtypeStruct((rows, width), BF),
            jax.ShapeDtypeStruct((8, width), F32),
            jax.ShapeDtypeStruct((width, width), BF),
            jax.ShapeDtypeStruct((width, 2 * hidden_units), BF),
            jax.ShapeDtypeStruct((width, hidden_units), BF),
        ],
        scratch_shapes=[
            pltpu.VMEM((width, rows), BF),
            pltpu.VMEM((width, rows), BF),
            pltpu.VMEM((width, rows), BF),
            pltpu.VMEM((rows, width), BF),
            pltpu.VMEM((rows, hidden_units), BF),
            pltpu.VMEM((rows, 2 * hidden_units), BF),
        ],
        compiler_params=pltpu.CompilerParams(vmem_limit_bytes=61 * MIB),
        cost_estimate=pl.CostEstimate(
            flops=6 * rows * width * (width + 3 * hidden_units),
            bytes_accessed=8 * width * (width + 3 * hidden_units),
            transcendentals=rows * hidden_units,
        ),
        name="mlp",
    )(tokens, attended, cotangent, keep, w_out_t, w_in, w_down_t, gains)


def finish_call(tokens, back_project, weight, back_middle, gains, gain_two_grad, block):
    rows, width = tokens.shape
    steps = rows // block
    tiles, tile = 3, width

    def body(x_ref, b_ref, w_ref, m_ref, g_ref, two_ref, out_ref, grad_ref, gain_ref, normed_t, held, gain_rows):
        i = pl.program_id(0)

        @pl.when(i == 0)
        def _():
            gain_rows[...] = jnp.zeros_like(gain_rows)
            gain_rows[1:2, :] = two_ref[0:1, :]

        @pl.when(i < steps)
        def _():
            at = pl.ds(pl.multiple_of(i * block, block), block)
            gain = g_ref[0:1, :]
            x = x_ref[...].astype(F32)
            scale = inverse_rms(x)
            normed_t[:, at] = jnp.transpose((x * scale * gain).astype(BF))
            back = b_ref[...]
            held[at, :] = back
            into, rows_of_gain = norm_back(mm(back, w_ref[...], 1, 1), x, scale, gain)
            out_ref[...] = (m_ref[...] + into).astype(BF)
            gain_rows[0:1, :] += jnp.sum(rows_of_gain, 0, keepdims=True)

        for t in range(tiles):

            @pl.when(i == steps + t)
            def _(t=t):
                grad_ref[...] = mm(normed_t[...], held[:, t * tile : (t + 1) * tile], 1, 0).astype(BF)

        @pl.when(i == steps)
        def _():
            gain_ref[...] = jnp.transpose(gain_rows[...]).astype(BF)

    row = lambda last: pl.BlockSpec((block, last), lambda i: (jnp.minimum(i, steps - 1), 0))
    return pl.pallas_call(
        body,
        grid=(steps + tiles,),
        in_specs=[row(width), row(3 * width), kept(weight.shape), row(width), kept(gains.shape), kept((8, width))],
        out_specs=[
            row(width),
            pl.BlockSpec((width, tile), lambda i: (0, jnp.clip(i - steps, 0, tiles - 1))),
            whole((width, 128)),
        ],
        out_shape=[
            jax.ShapeDtypeStruct((rows, width), BF),
            jax.ShapeDtypeStruct((width, 3 * width), BF),
            jax.ShapeDtypeStruct((width, 128), BF),
        ],
        scratch_shapes=[
            pltpu.VMEM((width, rows), BF),
            pltpu.VMEM((rows, 3 * width), BF),
            pltpu.VMEM((128, width), F32),
        ],
        compiler_params=pltpu.CompilerParams(vmem_limit_bytes=48 * MIB),
        cost_estimate=pl.CostEstimate(
            flops=12 * rows * width * width, bytes_accessed=28 * width * width, transcendentals=rows
        ),
        name="finish",
    )(tokens, back_project, weight, back_middle, gains, gain_two_grad)


def adam_step(master, grad, first, second, factor, rate, decay):
    clipped = factor * grad
    first_new = BETA_ONE * first + (1.0 - BETA_ONE) * clipped
    second_new = BETA_TWO * second + (1.0 - BETA_TWO) * clipped * clipped
    corrected = first_new / (1.0 - BETA_ONE**STEP)
    spread = jnp.sqrt(second_new / (1.0 - BETA_TWO**STEP)) + ADAM_EPS
    master_new = master - rate * (corrected / spread + decay * master)
    return (master_new, first_new, second_new)


def adam_call(squares, grads, masters, firsts, seconds):
    shard = grads[0].shape[0]

    def body(*refs):
        squares_ref, refs = refs[0], refs[1:]
        ins, norm_ref, outs = refs[:20], refs[20], refs[21:]
        norm = jnp.sqrt(squares_ref[0:1, :])
        norm_ref[...] = jnp.broadcast_to(norm, norm_ref.shape)
        factor = jnp.minimum(1.0, CLIP / norm[:, 0:1])
        for j in range(5):
            grad = ins[j][...]
            if j == 4:
                filled = jnp.concatenate([grad, jnp.zeros((128 - shard, 128), F32)], 0)
                grad = jnp.transpose(filled)[:2, :shard]
            made = adam_step(
                ins[5 + j][...], grad, ins[10 + j][...], ins[15 + j][...], factor, RATES[j], DECAYS[j]
            )
            for kind in range(3):
                outs[5 * kind + j][...] = made[kind]
            outs[15 + j][...] = made[0].astype(BF)

    shapes = [jax.ShapeDtypeStruct((8, 128), F32)]
    shapes += [jax.ShapeDtypeStruct(m.shape, F32) for _ in range(3) for m in masters]
    shapes += [jax.ShapeDtypeStruct(m.shape, BF) for m in masters]
    return pl.pallas_call(
        body,
        out_shape=shapes,
        compiler_params=pltpu.CompilerParams(vmem_limit_bytes=56 * MIB),
        name="adam",
    )(squares, *grads, *masters, *firsts, *seconds)


def grid_of(n_img):
    big_y = max(d for d in range(1, n_img + 1) if n_img % d == 0 and d * d <= n_img)
    return big_y, n_img // big_y


def on_device(
    patches,
    cotangent,
    valid_counts,
    qkv_master,
    out_master,
    in_master,
    down_master,
    gain_master,
    qkv_first,
    out_first,
    in_first,
    down_first,
    gain_first,
    qkv_second,
    out_second,
    in_second,
    down_second,
    gain_second,
):
    images, band_rows, width = patches.shape
    n_img, n_band = lax.axis_size("img"), lax.axis_size("band")
    share = n_band // images
    big_y, big_x = grid_of(n_img)
    dims = (big_y, big_x, n_band // 2, share)
    rows = images * band_rows
    shard = qkv_master.shape[0]
    own_comm = shard % 8 == 0
    both = ("img", "band")

    places = [[s * share + r for s in range(images)] for r in range(share)]

    def exchange(chunks):
        return lax.all_to_all(chunks, "band", 0, 0, axis_index_groups=places, tiled=True)

    def flat(got):
        return [g.reshape(width, g.shape[-1]) for g in got]

    def blocks_of(grads):
        return [g.reshape(dims[:3] + (2, shard, g.shape[1])) for g in grads]

    gains_block = jnp.pad(jnp.transpose(gain_master).astype(BF), ((0, 0), (0, 126)))
    early = [qkv_master.astype(BF), gains_block]
    late = [
        jnp.transpose(out_master).astype(BF),
        in_master.astype(BF),
        jnp.transpose(down_master).astype(BF),
    ]
    if own_comm:
        w_qkv, gains, tokens_low = gather_call(dims, "gather", 0, early, patches)
        w_qkv, gains = flat([w_qkv, gains])
    else:
        w_qkv, gains = [lax.all_gather(b, both, axis=0, tiled=True) for b in early]
        tokens_low = exchange(patches)
    band = lax.axis_index("band")
    image, part = band // share, band % share
    count = lax.dynamic_index_in_dim(valid_counts, image, 0, keepdims=False)
    own_places = (
        (jnp.arange(images, dtype=jnp.int32)[:, None] * share + part) * band_rows
        + jnp.arange(band_rows, dtype=jnp.int32)[None, :]
    ).reshape(rows, 1)
    row_keep = (own_places < count).astype(F32)
    key_places = (
        (
            jnp.arange(images, dtype=jnp.int32)[None, :, None] * share
            + lax.rem(part + jnp.arange(share, dtype=jnp.int32), share)[:, None, None]
        )
        * band_rows
        + jnp.arange(band_rows, dtype=jnp.int32)[None, None, :]
    ).reshape(1, share * rows)
    bias = jnp.where(key_places < count, 0.0, NEG).astype(F32)

    tokens = tokens_low.reshape(rows, width)
    project, gain_rows = project_call(tokens, w_qkv, gains, min(256, rows))
    attended, log_sums, kv, cotangent_low, *late_all = attend(
        dims, 1, project, bias, 256, late if own_comm else [], cotangent
    )
    if own_comm:
        w_out_t, w_in, w_down_t = flat(late_all)
    else:
        w_out_t, w_in, w_down_t = [lax.all_gather(b, both, axis=0, tiled=True) for b in late]
    result_low, back_middle, back_attended, gain_two_grad, *late_grads = mlp_call(
        tokens,
        attended,
        cotangent_low.reshape(rows, width),
        row_keep,
        w_out_t,
        w_in,
        w_down_t,
        gain_rows,
        min(512, rows),
    )
    result_low = result_low.reshape(images, band_rows, width)
    back_project, *late_sums, squares, output = attend_back(
        dims,
        2,
        project,
        kv,
        bias,
        attended,
        log_sums,
        back_attended,
        256,
        blocks_of(late_grads) if own_comm else [],
        result_low,
    )
    if not own_comm:
        late_sums = [lax.psum_scatter(g.astype(F32), both, scatter_dimension=0, tiled=True) for g in late_grads]
    back_rows, *early_grads = finish_call(
        tokens, back_project, w_qkv, back_middle, gain_rows, gain_two_grad, min(256, rows)
    )
    back_rows = back_rows.reshape(images, band_rows, width)
    if own_comm:
        qkv_sum, gain_sum, back_input, total = scatter_call(
            dims, "scatter", 3, blocks_of(early_grads), back_rows, squares
        )
    else:
        qkv_sum, gain_sum = [
            lax.psum_scatter(g.astype(F32), both, scatter_dimension=0, tiled=True) for g in early_grads
        ]
        back_input = exchange(back_rows)
        squares = sum(jnp.sum(g * g) for g in late_sums + [qkv_sum, gain_sum])
        total = lax.psum(jnp.broadcast_to(squares, (8, 128)), both)
    out_sum, in_sum, down_sum = late_sums

    def turned(arrays):
        return [jnp.transpose(a) if j in (1, 3) else a for j, a in enumerate(arrays)]

    norm, *updated = adam_call(
        total,
        [qkv_sum, out_sum, in_sum, down_sum, gain_sum],
        turned([qkv_master, out_master, in_master, down_master, gain_master]),
        turned([qkv_first, out_first, in_first, down_first, gain_first]),
        turned([qkv_second, out_second, in_second, down_second, gain_second]),
    )
    updated = [a for kind in range(4) for a in turned(updated[5 * kind : 5 * kind + 5])]
    return (output, back_input, norm[0, 0]) + tuple(updated)


def solution(mesh):
    rows_split, columns_split = P(("img", "band"), None), P(None, ("img", "band"))
    weights = (rows_split, columns_split, rows_split, columns_split, columns_split)
    tokens = P("img", "band", None)
    return jax.shard_map(
        on_device,
        mesh=mesh,
        in_specs=(tokens, tokens, P("img")) + weights * 3,
        out_specs=(tokens, tokens, P()) + weights * 4,
        check_vma=False,
    )
```

```python
import functools

import jax
import jax.numpy as jnp
from jax import lax
from jax.experimental import pallas as pl
from jax.experimental.pallas import tpu as pltpu
from jax.sharding import PartitionSpec as P

HEADS = 12
HEAD_DIM = 64
PAIR = 2 * HEAD_DIM
STEP = 10
EPS = 1e-06
NEG = -1000000000.0
SCALE = 0.125
CLIP = 1.0
BETA_ONE = 0.9
BETA_TWO = 0.999
ADAM_EPS = 1e-08
RATES = (0.06, 0.5, 0.06, 0.04, 0.5)
DECAYS = (0.1, 0.1, 0.1, 0.1, 0.0)
BF = jnp.bfloat16
F32 = jnp.float32
MESH = pl.DeviceIdType.MESH
ANY = pl.BlockSpec(memory_space=pl.ANY)
MIB = 2**20


class Net:
    def __init__(self, dims, send, recv, local):
        self.dims = dims
        big_y, big_x, big_z, share = dims
        img, band = lax.axis_index("img"), lax.axis_index("band")
        self.y, self.x = img // big_x, img % big_x
        self.z, self.c = band // 2, band % 2
        self.twin = 1 - self.c
        image, self.part = band // share, band % share
        self.image, self.images = image, 2 * big_z // share
        self.send, self.recv, self.local = send, recv, local
        self.used, self.used_local = 0, 0
        self.lines = {}
        for name, size in zip("yxzc", (big_y, big_x, big_z, 2)):
            places = []
            for d in range(1, size):
                at = dict(y=self.y, x=self.x, z=self.z, c=self.c)
                at[name] = lax.rem(at[name] + d, size)
                places.append((at[name], (at["y"] * big_x + at["x"], at["z"] * 2 + at["c"])))
            self.lines[name] = places
        self.band, self.img = band, img
        self.lines["band"], self.lines["img"] = [], []
        for d in range(1, 2 * big_z):
            other = lax.rem(band + d, 2 * big_z)
            self.lines["band"].append((other, (img, other)))
        for d in range(1, big_y * big_x):
            other = lax.rem(img + d, big_y * big_x)
            self.lines["img"].append((other, (other, band)))
        self.lines["image"] = []
        for d in range(1, self.images):
            other = lax.rem(image + d, self.images)
            self.lines["image"].append((other, (img, other * share + self.part)))
        self.lines["share"] = []
        for d in range(1, share):
            other = lax.rem(self.part + d, share)
            self.lines["share"].append((other, (img, image * share + other)))

    def line(self, name):
        return self.lines[name]

    def greet(self, kinds):
        barrier = pltpu.get_barrier_semaphore()
        count = 0
        for kind in kinds:
            for _, target in self.lines[kind]:
                pl.semaphore_signal(barrier, inc=1, device_id=target, device_id_type=MESH)
            count += len(self.lines[kind])
        pl.semaphore_wait(barrier, count)

    def copy(self, source, target_ref, target):
        made = self.plan(source, target_ref, target)
        made.start()
        return made

    def plan(self, source, target_ref, target):
        self.used += 1
        return Move(source, target_ref, self.send, self.recv, self.used - 1, target)

    def local_copy(self, source, target_ref):
        self.used_local += 1
        made = Move(source, target_ref, None, self.local, self.used_local - 1, None)
        made.start()
        return made


class Part:
    def __init__(self, ref, index=None):
        self.ref, self.index = ref, index

    def __getitem__(self, index):
        return Part(self.ref, index)

    def view(self):
        return self.ref if self.index is None else self.ref.at[self.index]


class Move:
    def __init__(self, source, target_ref, send, recv, at, target):
        self.source, self.target_ref = source, target_ref
        self.send, self.recv, self.at, self.target = send, recv, at, target

    def build(self):
        if self.target is None:
            return pltpu.make_async_copy(self.source.view(), self.target_ref.view(), self.recv.at[self.at])
        return pltpu.make_async_remote_copy(
            src_ref=self.source.view(),
            dst_ref=self.target_ref.view(),
            send_sem=self.send.at[self.at],
            recv_sem=self.recv.at[self.at],
            device_id=self.target,
            device_id_type=MESH,
        )

    def start(self):
        self.build().start()

    def wait(self):
        self.build().wait()

    def wait_recv(self):
        self.build().wait_recv()

    def wait_send(self):
        self.build().wait_send()


def drive(tasks):
    waiting = list(tasks)
    turn = 0
    while waiting:
        left = []
        for start, task in waiting:
            if start <= turn:
                try:
                    next(task)
                except StopIteration:
                    continue
            left.append((start, task))
        waiting = left
        turn += 1


def exchange_images(net, source, target, idle=1):
    moves = [net.copy(Part(source)[other], Part(target)[net.image], dev) for other, dev in net.line("image")]
    own = net.local_copy(Part(source)[net.image], Part(target)[net.image])
    for _ in range(idle):
        yield
    for move in moves:
        move.wait_recv()
    own.wait()
    for move in moves:
        move.wait_send()


def gather(net, source, target, columns, order):
    cols = pl.ds(*columns)
    y, x, z, c = net.y, net.x, net.z, net.c
    own = net.local_copy(Part(source)[:, cols], Part(target)[y, x, z, c, :, cols])
    sent = [net.copy(Part(source)[:, cols], Part(target)[y, x, z, c, :, cols], dev) for _, dev in net.line("z")]
    yield
    own.wait()
    for move in sent:
        move.wait_recv()
    part = Part(target)[y, x, :, c, :, cols]
    moves = [net.copy(part, part, dev) for _, dev in net.line(order[0])]
    sent += moves
    yield
    for move in moves:
        move.wait_recv()
    part = Part(target)[y, :, :, c, :, cols] if order[0] == "x" else Part(target)[:, x, :, c, :, cols]
    moves = [net.copy(part, part, dev) for _, dev in net.line(order[1])]
    sent += moves
    yield
    for move in moves:
        move.wait_recv()
    part = Part(target)[:, :, :, c, :, cols]
    moves = [net.copy(part, part, dev) for _, dev in net.line("c")]
    sent += moves
    yield
    for move in moves:
        move.wait_recv()
    for move in sent:
        move.wait_send()


def gather_copies(dims):
    return dims[0] + dims[1] + dims[2] - 3 + 1


def scatter(net, grad, held, from_core, from_first, from_second, from_z, out, squares, columns, order, offset=0):
    big_y, big_x, big_z, _ = net.dims
    cols = pl.ds(*columns)
    y, x, z, c = net.y, net.x, net.z, net.c
    sent = []
    (_, twin), = net.line("c")
    moves = [net.copy(Part(grad)[:, :, :, net.twin, :, cols], Part(from_core), twin)]
    sent += moves
    own = net.local_copy(Part(grad)[:, :, :, c, :, cols], Part(held))
    yield
    own.wait()
    moves[0].wait_recv()

    def first_add(at, _):
        a, b, d = at // (big_x * big_z), (at // big_z) % big_x, at % big_z
        held[a, b, d] = (held[a, b, d].astype(F32) + from_core[a, b, d].astype(F32)).astype(BF)
        return 0

    lax.fori_loop(0, big_y * big_x * big_z, first_add, 0)
    moves = []
    for slot, (other, dev) in enumerate(net.line(order[0])):
        part = Part(held)[:, other] if order[0] == "x" else Part(held)[other]
        moves.append(net.copy(part, Part(from_first)[slot], dev))
    sent += moves
    yield
    for move in moves:
        move.wait_recv()
    left = big_y if order[0] == "x" else big_x

    def second_add(at, _):
        a, d = at // big_z, at % big_z
        place = (a, x, d) if order[0] == "x" else (y, a, d)
        total = held[place].astype(F32)
        for slot in range(len(moves)):
            total = total + from_first[slot, a, d].astype(F32)
        held[place] = total.astype(BF)
        return 0

    lax.fori_loop(0, left * big_z, second_add, 0)
    moves = []
    for slot, (other, dev) in enumerate(net.line(order[1])):
        part = Part(held)[other, x] if order[1] == "y" else Part(held)[y, other]
        moves.append(net.copy(part, Part(from_second)[slot], dev))
    sent += moves
    yield
    for move in moves:
        move.wait_recv()

    def third_add(d, _):
        total = held[y, x, d].astype(F32)
        for slot in range(len(moves)):
            total = total + from_second[slot, d].astype(F32)
        held[y, x, d] = total.astype(BF)
        return 0

    lax.fori_loop(0, big_z, third_add, 0)
    moves = []
    for slot, (other, dev) in enumerate(net.line("z")):
        moves.append(net.copy(Part(held)[y, x, other], Part(from_z)[slot], dev))
    sent += moves
    yield
    for move in moves:
        move.wait_recv()
    total = held[y, x, z].astype(F32)
    for slot in range(len(moves)):
        total = total + from_z[slot].astype(F32)
    out[:, offset + columns[0] : offset + columns[0] + columns[1]] = total
    tile = squares[...]
    for a in range(total.shape[0] // 8):
        for b in range(columns[1] // 128):
            piece = total[8 * a : 8 * a + 8, 128 * b : 128 * b + 128]
            tile = tile + piece * piece
    squares[...] = tile
    for move in sent:
        move.wait_send()


def scatter_scratch(dims, rows, columns, order):
    big_y, big_x, big_z, _ = dims
    width = columns[1]
    ahead, left = (big_x, big_y) if order[0] == "x" else (big_y, big_x)
    return [
        pltpu.VMEM((big_y, big_x, big_z, rows, width), BF),
        pltpu.VMEM((big_y, big_x, big_z, rows, width), BF),
        pltpu.VMEM((ahead - 1, left, big_z, rows, width), BF),
        pltpu.VMEM((left - 1, big_z, rows, width), BF),
        pltpu.VMEM((big_z - 1, rows, width), BF),
    ]


def sum_tiles(net, tile, slots):
    first = 0
    for name, me in (("band", net.band), ("img", net.img)):
        places = net.line(name)
        slots[first + me] = tile[...]
        moves = [net.copy(Part(tile), Part(slots)[first + me], dev) for _, dev in places]
        for move in moves:
            move.wait_recv()
        for move in moves:
            move.wait_send()
        total = slots[first]
        for d in range(1, len(places) + 1):
            total = total + slots[first + d]
        tile[...] = total
        first += len(places) + 1


def sems(count):
    return pltpu.SemaphoreType.DMA((max(count, 1),))


def halves(width):
    units = width // 128
    low = (units + 1) // 2 * 128
    if low == width:
        return [((0, width), "xy")]
    return [((0, low), "xy"), ((low, width - low), "yx")]


def pieces(width, shares):
    units, found, start = width // 128, [], 0
    for group in range(len(shares)):
        stop = units * sum(shares[: group + 1]) // sum(shares) * 128
        for columns, order in halves(stop - start):
            found.append((group, (columns[0] + start, columns[1]), order))
        start = stop
    return found


def gather_call(dims, name, number, blocks, images=None):
    big_y, big_x, big_z, share = dims
    parts = [halves(block.shape[1]) for block in blocks]
    copies = sum(len(p) for p in parts) * gather_copies(dims)
    local = sum(len(p) for p in parts)
    n = len(blocks)
    with_images = images is not None
    if with_images:
        copies += images.shape[0] - 1
        local += 1

    def body(*refs):
        ins, rest = refs[: n + with_images], refs[n + with_images :]
        outs, (send, recv, local_sem) = rest[: n + with_images], rest[n + with_images :]
        net = Net(dims, send, recv, local_sem)
        net.greet("zxyc" if not with_images else ["z", "x", "y", "c", "image"])
        tasks = []
        for j in range(n):
            for columns, order in parts[j]:
                tasks.append((0, gather(net, ins[j], outs[j], columns, order)))
        if with_images:
            tasks.append((1, exchange_images(net, ins[n], outs[n], 3)))
        drive(tasks)

    args = list(blocks) + ([images] if with_images else [])
    shapes = [jax.ShapeDtypeStruct((big_y, big_x, big_z, 2) + b.shape, b.dtype) for b in blocks]
    if with_images:
        shapes.append(jax.ShapeDtypeStruct(images.shape, images.dtype))
    return pl.pallas_call(
        body,
        out_shape=shapes,
        in_specs=[ANY] * len(args),
        out_specs=[ANY] * len(shapes),
        scratch_shapes=[sems(copies), sems(copies), sems(local)],
        compiler_params=pltpu.CompilerParams(collective_id=number, has_side_effects=True),
        name=name,
    )(*args)


def finale_call(dims, number, tokens, back_project, weight, back_middle, gains, gain_two_grad, squares, images):
    big_y, big_x, big_z, _ = dims
    rows, width = tokens.shape
    block = rows // images
    devices = 2 * big_x * big_y * big_z
    shard = width // devices
    parts = halves(3 * width + 128)
    tile = 256
    band_size, img_size = 2 * big_z, big_x * big_y
    copies = len(parts) * gather_copies(dims) + images - 1 + band_size + img_size - 2
    local = len(parts) + 5 + 2 * images
    scratch = [sems(copies), sems(copies), sems(local)]
    for columns, order in parts:
        scratch += scatter_scratch(dims, shard, columns, order)
    n_fixed = 3 + 5 * len(parts)
    scratch += [
        pltpu.VMEM((8, 128), F32),
        pltpu.VMEM((band_size + img_size, 8, 128), F32),
        pltpu.VMEM(tokens.shape, BF),
        pltpu.VMEM(back_project.shape, BF),
        pltpu.VMEM(weight.shape, BF),
        pltpu.VMEM(back_middle.shape, F32),
        pltpu.VMEM((images, block, width), BF),
        pltpu.VMEM((width, rows), BF),
        pltpu.VMEM((128, width), F32),
    ]
    scratch += [pltpu.VMEM((big_y, big_x, big_z, 2, shard, columns[1]), BF) for columns, _ in parts]

    def body(*refs):
        x_hbm, b_hbm, w_hbm, m_hbm, g_ref, two_ref, squares_ref = refs[:7]
        sum_ref, moved, total_ref, rest = refs[7], refs[8], refs[9], refs[10:]
        tally, slots, x_all, b_all, w_all, m_all, sent, normed_t, gain_rows = rest[n_fixed : n_fixed + 9]
        grads = rest[n_fixed + 9 :]
        net = Net(dims, *rest[:3])
        order = [other for other, _ in net.line("image")] + [net.image]
        load_w = net.local_copy(Part(w_hbm), Part(w_all))
        loads = []
        for chunk in order:
            at = pl.ds(pl.multiple_of(chunk * block, block), block)
            loads.append([net.local_copy(Part(a)[at, :], Part(b)[at, :]) for a, b in ((b_hbm, b_all), (x_hbm, x_all))])
            if len(loads) == 1:
                load_m = net.local_copy(Part(m_hbm), Part(m_all))
        net.greet(["z", "x", "y", "c", "image", "band", "img"])
        tally[...] = squares_ref[...]
        gain_rows[...] = jnp.zeros_like(gain_rows)
        gain_rows[1:2, :] = two_ref[0:1, :]
        load_w.wait()
        moves = []
        for place, chunk in enumerate(order):
            for load in loads[place]:
                load.wait()
            if place == 0:
                load_m.wait()
            at = pl.ds(pl.multiple_of(chunk * block, block), block)
            gain = g_ref[0:1, :]
            x = x_all[at, :].astype(F32)
            scale = inverse_rms(x)
            normed_t[:, place * block : (place + 1) * block] = jnp.transpose((x * scale * gain).astype(BF))
            into, rows_of_gain = norm_back(mm(b_all[at, :], w_all[:, : 3 * width], 1, 1), x, scale, gain)
            sent[chunk] = (m_all[at, :] + into).astype(BF)
            gain_rows[0:1, :] += jnp.sum(rows_of_gain, 0, keepdims=True)
            if place < images - 1:
                moves.append(net.copy(Part(sent)[chunk], Part(moved)[net.image], net.line("image")[place][1]))
            else:
                own = net.local_copy(Part(sent)[chunk], Part(moved)[net.image])
        tasks = []
        for k, (columns, turn) in enumerate(parts):
            buffers = rest[3 + 5 * k : 8 + 5 * k]
            for low in range(columns[0], min(columns[0] + columns[1], 3 * width), tile):
                total = jnp.zeros((width, tile), F32)
                for place, chunk in enumerate(order):
                    at = pl.ds(pl.multiple_of(chunk * block, block), block)
                    inner = slice(place * block, (place + 1) * block)
                    total = total + mm(normed_t[:, inner], b_all[at, low : low + tile], 1, 0)
                into = slice(low - columns[0], low - columns[0] + tile)
                grads[k][..., into] = total.astype(BF).reshape(grads[k].shape[:5] + (tile,))
            if k == len(parts) - 1:
                turned = jnp.transpose(gain_rows[...]).astype(BF)
                grads[k][..., columns[1] - 128 :] = turned.reshape(grads[k].shape[:5] + (128,))
            task = scatter(net, grads[k], *buffers, sum_ref, tally, (0, columns[1]), turn, columns[0])
            next(task)
            tasks.append((0, task))
        drive(tasks)
        sum_tiles(net, tally, slots)
        total_ref[...] = jnp.broadcast_to(jnp.sum(tally[...], keepdims=True), (8, 128))
        for move in moves:
            move.wait_recv()
        own.wait()
        for move in moves:
            move.wait_send()

    vmem = pl.BlockSpec(memory_space=pltpu.VMEM)
    shapes = [
        jax.ShapeDtypeStruct((shard, 3 * width + 128), F32),
        jax.ShapeDtypeStruct((images, block, width), BF),
        jax.ShapeDtypeStruct((8, 128), F32),
    ]
    return pl.pallas_call(
        body,
        out_shape=shapes,
        in_specs=[ANY] * 4 + [vmem] * 3,
        out_specs=[vmem, ANY, vmem],
        scratch_shapes=scratch,
        compiler_params=pltpu.CompilerParams(
            collective_id=number, has_side_effects=True, vmem_limit_bytes=61 * MIB
        ),
        name="finale",
    )(tokens, back_project, weight, back_middle, gains, gain_two_grad, squares)


def whole(shape):
    return pl.BlockSpec(shape, lambda i: (0,) * len(shape))


def kept(shape):
    return pl.BlockSpec(shape, lambda i: (0,) * len(shape), pipeline_mode=pl.Buffered(1))


def inverse_rms(value):
    return lax.rsqrt(jnp.mean(value * value, -1, keepdims=True) + EPS)


def mm(a, b, ca, cb):
    return lax.dot_general(a, b, (((ca,), (cb,)), ((), ())), preferred_element_type=F32)


def at_turn(turn, events):
    def visit(whens):
        if len(whens) == 1:

            @pl.when(turn == whens[0])
            def _():
                for task in events[whens[0]]:
                    next(task, None)

        elif whens:
            middle = len(whens) // 2

            @pl.when(turn < whens[middle])
            def _():
                visit(whens[:middle])

            @pl.when(turn >= whens[middle])
            def _():
                visit(whens[middle:])

    visit(sorted(events))


def schedule(tasks, turns, last):
    events, tail = {}, []
    for task, when in zip(tasks, turns):
        for turn in when:
            if turn < last:
                events.setdefault(turn, []).append(task)
            else:
                tail.append(task)
    return events, tail


def lanes_of(h):
    lane = lax.broadcasted_iota(jnp.int32, (1, PAIR), 1) < HEAD_DIM
    return lane if h == 0 else ~lane


def attend(dims, number, tokens, weight, bias, block, weights, chunks):
    big_y, big_x, big_z, share = dims
    rows, width = tokens.shape
    pairs = width // PAIR
    others = share - 1
    blocks = 4
    n = len(weights)
    last = LEAD + 4 * pairs
    parts = [
        (j, columns, order, GATHER_TURNS[group])
        for j, w in enumerate(weights)
        for group, columns, order in pieces(w.shape[1], GATHER_SHARES)
    ]
    copies = len(parts) * gather_copies(dims) + others * 2 * pairs + chunks.shape[0] - 1

    def body(*refs):
        x_ref, w_ref, bias_ref, chunks_in = refs[:4]
        blocks_in, refs = refs[4 : 4 + n], refs[4 + n :]
        o_ref, l_ref, kv_out, chunks_out, project_ref, gains_ref, refs = refs[:6] + (refs[6:],)
        gathered, (kv_held, send, recv, local) = refs[:n], refs[n:]
        h = pl.program_id(0)
        net = Net(dims, send, recv, local)

        def move_keys(j):
            moves = []
            for slot, (_, target) in enumerate(net.line("share")):
                source = Part(project_ref)[:, pl.ds(width + PAIR * j, PAIR)]
                moves.append(net.plan(source, Part(kv_held)[others - 1 - slot, j], target))
            return moves

        key_moves = [move_keys(j) for j in range(2 * pairs)]
        keep = Move(Part(kv_held), Part(kv_out), None, local, len(parts) + 1, None)
        tasks = [gather(net, blocks_in[j], gathered[j], columns, order) for j, columns, order, _ in parts]
        tasks.append(exchange_images(net, chunks_in, chunks_out))
        turns = [turn for _, _, _, turn in parts] + [CHUNK_TURNS]
        events, tail = schedule(tasks, turns, last)

        @pl.when(h == 0)
        def _():
            net.greet(["z", "x", "y", "c", "image"] + (["share"] if share > 2 else []))
            gains_ref[...] = jnp.transpose(w_ref[:, 3 * width :].astype(F32))[:8]

        @pl.when(h == 0)
        def _():
            def row_step(i, _):
                at_turn(i, {t: e for t, e in events.items() if t < LEAD})
                at = pl.ds(pl.multiple_of(i * block, block), block)
                x = x_ref[at, :].astype(F32)
                normed = (x * inverse_rms(x) * gains_ref[0:1, :]).astype(BF)
                project_ref[at, :] = mm(normed, w_ref[:, : 3 * width], 1, 0).astype(BF)
                return 0

            lax.fori_loop(0, blocks, row_step, 0)
            for j in range(pairs):
                for move in key_moves[j] + key_moves[j + pairs]:
                    move.start()

        for j in range(pairs):

            @pl.when(h == j)
            def _(j=j):
                for move in key_moves[j] + key_moves[j + pairs]:
                    move.wait_recv()
                if j == pairs - 1:
                    keep.start()

        def own(first):
            return pl.ds(pl.multiple_of((h + first) * PAIR, PAIR), PAIR)

        def step(i, _):
            at_turn(LEAD + h * 4 + i, {t: e for t, e in events.items() if t >= LEAD})
            at = pl.ds(pl.multiple_of(i * block, block), block)
            k = jnp.concatenate([project_ref[:, own(pairs)]] + [kv_held[s, h] for s in range(others)], 0)
            v = jnp.concatenate(
                [project_ref[:, own(2 * pairs)]] + [kv_held[s, h + pairs] for s in range(others)], 0
            )
            q = project_ref[at, own(0)] * jnp.asarray(SCALE, BF)
            mixed, logs = [], []
            for half in range(2):
                scores = mm(jnp.where(lanes_of(half), q, jnp.zeros_like(q)), k, 1, 1) + bias_ref[...]
                highest = jnp.max(scores, -1, keepdims=True)
                powers = jnp.exp(scores - highest)
                total = jnp.sum(powers, -1, keepdims=True)
                mixed.append(mm(powers.astype(BF), v, 1, 0) / total)
                logs.append(highest + jnp.log(total))
            o_ref[at, :] = jnp.where(lanes_of(0), mixed[0], mixed[1]).astype(BF)
            l_ref[at, :] = jnp.where(lanes_of(0), logs[0], logs[1])
            return 0

        lax.fori_loop(0, blocks, step, 0)

        @pl.when(h == pairs - 1)
        def _():
            for task in tail:
                next(task, None)
            for moves in key_moves:
                for move in moves:
                    move.wait_send()
            keep.wait()

    column = lambda first: pl.BlockSpec((rows, PAIR), lambda h: (0, h + first))
    keys = rows * share
    shapes = [
        jax.ShapeDtypeStruct((rows, width), BF),
        jax.ShapeDtypeStruct((rows, width), F32),
        jax.ShapeDtypeStruct((others, 2 * pairs, rows, PAIR), BF),
        jax.ShapeDtypeStruct(chunks.shape, chunks.dtype),
        jax.ShapeDtypeStruct((rows, 3 * width), BF),
        jax.ShapeDtypeStruct((8, width), F32),
    ] + [jax.ShapeDtypeStruct((big_y, big_x, big_z, 2) + w.shape, w.dtype) for w in weights]
    return pl.pallas_call(
        body,
        grid=(pairs,),
        in_specs=[kept(tokens.shape), kept(weight.shape), kept((1, keys))] + [ANY] * (1 + n),
        out_specs=[column(0), column(0), ANY, ANY, kept((rows, 3 * width)), kept((8, width))] + [ANY] * n,
        out_shape=shapes,
        scratch_shapes=[
            pltpu.VMEM((others, 2 * pairs, rows, PAIR), BF),
            sems(copies),
            sems(copies),
            sems(len(parts) + 2),
        ],
        compiler_params=pltpu.CompilerParams(
            collective_id=number, has_side_effects=True, vmem_limit_bytes=60 * MIB
        ),
        cost_estimate=pl.CostEstimate(
            flops=16 * rows * keys * width, bytes_accessed=8 * keys * width, transcendentals=rows * keys * HEADS
        ),
        name="attend",
    )(tokens, weight, bias, chunks, *weights)


LEAD = 4
GATHER_SHARES = (1, 2, 2, 2, 2, 1)
GATHER_TURNS = (
    (0, 3, 4, 7, 9),
    (0, 4, 7, 11, 13),
    (1, 7, 11, 15, 17),
    (2, 11, 15, 20, 22),
    (4, 15, 20, 25, 27),
    (6, 20, 25, 27, 28),
)
CHUNK_TURNS = (12, 28)
SCATTER_TURNS = (((1, 4, 11, 17, 24),), ((0, 2, 8, 14, 20),), ((1, 3, 9, 15, 21),))
RESULT_TURNS = (0, 24)


def attend_back(dims, number, project, kv, bias, mixed, logs, back, block, grads, chunks):
    big_y, big_x, big_z, share = dims
    rows, width = mixed.shape
    pairs = width // PAIR
    others = share - 1
    blocks = 4
    keys = rows * share
    n = len(grads)
    parts = [
        (j, columns, order, SCATTER_TURNS[j][group])
        for j, g in enumerate(grads)
        for group, columns, order in pieces(g.shape[5], (1,) * len(SCATTER_TURNS[j]))
    ]
    copies = len(parts) * gather_copies(dims) + others * 2 * pairs + chunks.shape[0] - 1

    def body(*refs):
        q_ref, k_ref, v_ref, k_other, v_other, bias_ref, mixed_ref, logs_ref, back_ref = refs[:9]
        grads_in, chunks_in, refs = refs[9 : 9 + n], refs[9 + n], refs[10 + n :]
        out_ref, sums, squares, chunks_out, refs = refs[0], refs[1 : 1 + n], refs[1 + n], refs[2 + n], refs[3 + n :]
        dk_sum, dv_sum, dk_own, dv_own, parted, arrived, bias_column = refs[:7]
        send, recv, local = refs[7:10]
        buffers = refs[10:]
        h = pl.program_id(0)
        net = Net(dims, send, recv, local)

        def move_keys(j):
            moves = []
            for slot, (_, target) in enumerate(net.line("share")):
                moves.append(net.plan(Part(parted)[slot, j], Part(arrived)[others - 1 - slot, j], target))
            return moves

        key_moves = [move_keys(j) for j in range(2 * pairs)]
        tasks = [
            scatter(net, grads_in[j], *buffers[5 * k : 5 * k + 5], sums[j], squares, columns, order)
            for k, (j, columns, order, _) in enumerate(parts)
        ]
        tasks.append(exchange_images(net, chunks_in, chunks_out))
        turns = [turn for _, _, _, turn in parts] + [RESULT_TURNS]
        events, tail = schedule(tasks, turns, 4 * pairs)

        @pl.when(h == 0)
        def _():
            net.greet(["z", "x", "y", "c", "image"] + (["share"] if share > 2 else []))
            squares[...] = jnp.zeros_like(squares)
            bias_column[...] = jnp.transpose(jnp.broadcast_to(bias_ref[...], (PAIR, keys)))

        dk_sum[...] = jnp.zeros_like(dk_sum)
        dv_sum[...] = jnp.zeros_like(dv_sum)

        def step(i, _):
            at_turn(h * 4 + i, events)
            at = pl.ds(pl.multiple_of(i * block, block), block)
            k = jnp.concatenate([k_ref[...]] + [k_other[s, 0] for s in range(others)], 0)
            v = jnp.concatenate([v_ref[...]] + [v_other[s, 0] for s in range(others)], 0)
            q, do = q_ref[at, :] * jnp.asarray(SCALE, BF), back_ref[at, :]
            lse = jnp.transpose(logs_ref[at, :])
            products = jnp.transpose(do.astype(F32) * mixed_ref[at, :].astype(F32))
            dqs, dks, dvs = [], [], []
            for half in range(2):
                low, high = half * HEAD_DIM, (half + 1) * HEAD_DIM
                q_h = jnp.where(lanes_of(half), q, jnp.zeros_like(q))
                do_h = jnp.where(lanes_of(half), do, jnp.zeros_like(do))
                row_dots = jnp.sum(products[low:high, :], 0, keepdims=True)
                chances = jnp.exp(mm(k, q_h, 1, 1) + bias_column[:, :1] - lse[low : low + 1, :])
                slopes = mm(v, do_h, 1, 1)
                scores = (chances * (slopes - row_dots)).astype(BF)
                dqs.append(mm(scores, k, 0, 0))
                dks.append(mm(scores, q_h, 1, 0))
                dvs.append(mm(chances.astype(BF), do_h, 1, 0))
            dq = (jnp.where(lanes_of(0), dqs[0], dqs[1]) * SCALE).astype(BF)
            out_ref[at, pl.ds(pl.multiple_of(h * PAIR, PAIR), PAIR)] = dq
            dk_sum[...] += dks[0] + dks[1]
            dv_sum[...] += dvs[0] + dvs[1]
            return 0

        lax.fori_loop(0, blocks, step, 0)

        def finish(j):
            for move in key_moves[j] + key_moves[j + pairs]:
                move.wait_recv()
            for first, kept, total in ((0, j, dk_own), (pairs, j + pairs, dv_own)):
                value = total[...]
                for slot in range(others):
                    value = value + arrived[slot, kept].astype(F32)
                out_ref[:, width + PAIR * kept : width + PAIR * (kept + 1)] = value.astype(BF)

        for j in range(pairs):

            @pl.when(h == j)
            def _(j=j):
                if j > 0:
                    finish(j - 1)
                dk_own[...] = dk_sum[0:rows, :]
                dv_own[...] = dv_sum[0:rows, :]
                for slot in range(others):
                    away = slice(rows * (slot + 1), rows * (slot + 2))
                    parted[slot, j] = dk_sum[away, :].astype(BF)
                    parted[slot, j + pairs] = dv_sum[away, :].astype(BF)
                for move in key_moves[j] + key_moves[j + pairs]:
                    move.start()
                if j == pairs - 1:
                    for task in tail:
                        next(task, None)
                    finish(j)
                    for moves in key_moves:
                        for move in moves:
                            move.wait_send()

    column = lambda first: pl.BlockSpec((rows, PAIR), lambda h: (0, h + first))
    other = lambda first: pl.BlockSpec((others, 1, rows, PAIR), lambda h: (0, h + first, 0, 0))
    whole = lambda shape: pl.BlockSpec(shape, lambda h: (0,) * len(shape))
    shard = grads[0].shape[4] if n else 0
    shapes = (
        [jax.ShapeDtypeStruct((rows, 3 * width), BF)]
        + [jax.ShapeDtypeStruct((shard, g.shape[5]), F32) for g in grads]
        + [jax.ShapeDtypeStruct((8, 128), F32)]
    )
    moved = jax.ShapeDtypeStruct(chunks.shape, chunks.dtype)
    scratch = [
        pltpu.VMEM((keys, PAIR), F32),
        pltpu.VMEM((keys, PAIR), F32),
        pltpu.VMEM((rows, PAIR), F32),
        pltpu.VMEM((rows, PAIR), F32),
        pltpu.VMEM((others, 2 * pairs, rows, PAIR), BF),
        pltpu.VMEM((others, 2 * pairs, rows, PAIR), BF),
        pltpu.VMEM((keys, PAIR), F32),
        sems(copies),
        sems(copies),
        sems(len(parts) + 1),
    ]
    for _, columns, order, _ in parts:
        scratch += scatter_scratch(dims, shard, columns, order)
    return pl.pallas_call(
        body,
        grid=(pairs,),
        in_specs=[
            column(0),
            column(pairs),
            column(2 * pairs),
            other(0),
            other(pairs),
            whole((1, keys)),
            column(0),
            column(0),
            column(0),
        ]
        + [ANY] * (n + 1),
        out_specs=[whole(s.shape) for s in shapes] + [ANY],
        out_shape=shapes + [moved],
        scratch_shapes=scratch,
        compiler_params=pltpu.CompilerParams(
            collective_id=number, has_side_effects=True, vmem_limit_bytes=60 * MIB
        ),
        cost_estimate=pl.CostEstimate(
            flops=40 * rows * keys * width, bytes_accessed=16 * keys * width, transcendentals=rows * keys * HEADS
        ),
        name="attend_back",
    )(project, project, project, kv, kv, bias, mixed, logs, back, *grads, chunks)


def norm_back(back, value, scale, gain):
    scaled = back * gain
    inner = jnp.mean(scaled * value, -1, keepdims=True)
    return scale * scaled - value * (scale * scale * scale * inner), back * (value * scale)


GELU_A = 0.7978845608028654
GELU_B = 0.044715


def mlp_call(tokens, attended, cotangent, keep, weights, gains, block):
    rows, width = tokens.shape
    hidden_units = (weights.shape[1] - width) // 3
    steps = rows // block
    tile = 512
    in_tiles, down_tiles = 2 * hidden_units // tile, hidden_units // tile
    part = 512

    def body(
        x_ref, a_ref, c_ref, keep_ref, w_ref, g_ref,
        result_ref, middle_ref, back_ref, gain_ref, g_out_ref, g_in_ref, g_down_ref,
        normed_t, low_t, branch_t, mixed, hidden, back_gu,
    ):
        i = pl.program_id(0)
        wo_ref = w_ref.at[:, :width]
        wi_ref = w_ref.at[:, width : width + 2 * hidden_units]
        wd_ref = w_ref.at[:, width + 2 * hidden_units :]

        @pl.when(i == 0)
        def _():
            gain_ref[...] = jnp.zeros_like(gain_ref)

        @pl.when(i < steps)
        def _():
            at = pl.ds(pl.multiple_of(i * block, block), block)
            gain = g_ref[1:2, :]
            a = a_ref[...]
            mixed[at, :] = a
            middle = x_ref[...].astype(F32) + mm(a, wo_ref[...], 1, 1)
            scale = inverse_rms(middle)
            normed = (middle * scale * gain).astype(BF)
            normed_t[:, at] = jnp.transpose(normed)
            back_result = keep_ref[...] * c_ref[...].astype(F32)
            low = back_result.astype(BF)
            low_t[:, at] = jnp.transpose(low)
            result, back = middle, jnp.zeros_like(middle)
            for p in range(hidden_units // part):
                one = slice(p * part, (p + 1) * part)
                two = slice(hidden_units + p * part, hidden_units + (p + 1) * part)
                gate = mm(normed, wi_ref[:, one], 1, 0)
                up = mm(normed, wi_ref[:, two], 1, 0)
                back_hidden = mm(low, wd_ref[:, one], 1, 0)
                square = gate * gate
                bend = jnp.tanh(GELU_A * (gate + GELU_B * (gate * square)))
                half = 0.5 + 0.5 * bend
                curve = gate * half
                slope = half + (0.5 * GELU_A) * gate * (1.0 - bend * bend) * (1.0 + (3.0 * GELU_B) * square)
                hid = (curve * up).astype(BF)
                back_gate = (back_hidden * up * slope).astype(BF)
                back_up = (back_hidden * curve).astype(BF)
                hidden[at, one] = hid
                back_gu[at, one] = back_gate
                back_gu[at, two] = back_up
                result = result + mm(hid, wd_ref[:, one], 1, 1)
                back = back + mm(back_gate, wi_ref[:, one], 1, 1) + mm(back_up, wi_ref[:, two], 1, 1)
            result_ref[...] = (keep_ref[...] * result).astype(BF)
            into, gain_rows = norm_back(back, middle, scale, gain)
            gain_ref[0:1, :] += jnp.sum(gain_rows, 0, keepdims=True)
            back_middle = back_result + into
            middle_ref[...] = back_middle
            branch = back_middle.astype(BF)
            branch_t[:, at] = jnp.transpose(branch)
            back_ref[...] = mm(branch, wo_ref[...], 1, 0).astype(BF)

        @pl.when(i == steps)
        def _():
            g_out_ref[...] = mm(branch_t[...], mixed[...], 1, 0).astype(BF)

        for t in range(in_tiles):

            @pl.when(i == steps + 1 + t)
            def _(t=t):
                g_in_ref[...] = mm(normed_t[...], back_gu[:, t * tile : (t + 1) * tile], 1, 0).astype(BF)

        for t in range(down_tiles):

            @pl.when(i == steps + 1 + in_tiles + t)
            def _(t=t):
                g_down_ref[...] = mm(low_t[...], hidden[:, t * tile : (t + 1) * tile], 1, 0).astype(BF)

    row = lambda last: pl.BlockSpec((block, last), lambda i: (jnp.minimum(i, steps - 1), 0))
    return pl.pallas_call(
        body,
        grid=(steps + 1 + in_tiles + down_tiles,),
        in_specs=[
            row(width),
            row(width),
            row(width),
            row(1),
            kept(weights.shape),
            kept(gains.shape),
        ],
        out_specs=[
            row(width),
            row(width),
            row(width),
            whole((8, width)),
            whole((width, width)),
            pl.BlockSpec((width, tile), lambda i: (0, jnp.clip(i - steps - 1, 0, in_tiles - 1))),
            pl.BlockSpec((width, tile), lambda i: (0, jnp.clip(i - steps - 1 - in_tiles, 0, down_tiles - 1))),
        ],
        out_shape=[
            jax.ShapeDtypeStruct((rows, width), BF),
            jax.ShapeDtypeStruct((rows, width), F32),
            jax.ShapeDtypeStruct((rows, width), BF),
            jax.ShapeDtypeStruct((8, width), F32),
            jax.ShapeDtypeStruct((width, width), BF),
            jax.ShapeDtypeStruct((width, 2 * hidden_units), BF),
            jax.ShapeDtypeStruct((width, hidden_units), BF),
        ],
        scratch_shapes=[
            pltpu.VMEM((width, rows), BF),
            pltpu.VMEM((width, rows), BF),
            pltpu.VMEM((width, rows), BF),
            pltpu.VMEM((rows, width), BF),
            pltpu.VMEM((rows, hidden_units), BF),
            pltpu.VMEM((rows, 2 * hidden_units), BF),
        ],
        compiler_params=pltpu.CompilerParams(vmem_limit_bytes=61 * MIB),
        cost_estimate=pl.CostEstimate(
            flops=6 * rows * width * (width + 3 * hidden_units),
            bytes_accessed=8 * width * (width + 3 * hidden_units),
            transcendentals=rows * hidden_units,
        ),
        name="mlp",
    )(tokens, attended, cotangent, keep, weights, gains)


def finish_call(tokens, back_project, weight, back_middle, gains, gain_two_grad, block):
    rows, width = tokens.shape
    steps = rows // block
    tiles, tile = 3, width

    def body(x_ref, b_ref, w_ref, m_ref, g_ref, two_ref, out_ref, grad_ref, gain_ref, normed_t, held, gain_rows):
        i = pl.program_id(0)

        @pl.when(i == 0)
        def _():
            gain_rows[...] = jnp.zeros_like(gain_rows)
            gain_rows[1:2, :] = two_ref[0:1, :]

        @pl.when(i < steps)
        def _():
            at = pl.ds(pl.multiple_of(i * block, block), block)
            gain = g_ref[0:1, :]
            x = x_ref[...].astype(F32)
            scale = inverse_rms(x)
            normed_t[:, at] = jnp.transpose((x * scale * gain).astype(BF))
            back = b_ref[...]
            held[at, :] = back
            into, rows_of_gain = norm_back(mm(back, w_ref[:, : 3 * width], 1, 1), x, scale, gain)
            out_ref[...] = (m_ref[...] + into).astype(BF)
            gain_rows[0:1, :] += jnp.sum(rows_of_gain, 0, keepdims=True)

        for t in range(tiles):

            @pl.when(i == steps + t)
            def _(t=t):
                grad_ref[...] = mm(normed_t[...], held[:, t * tile : (t + 1) * tile], 1, 0).astype(BF)

        @pl.when(i == steps)
        def _():
            gain_ref[...] = jnp.transpose(gain_rows[...]).astype(BF)

    row = lambda last: pl.BlockSpec((block, last), lambda i: (jnp.minimum(i, steps - 1), 0))
    return pl.pallas_call(
        body,
        grid=(steps + tiles,),
        in_specs=[row(width), row(3 * width), kept(weight.shape), row(width), kept(gains.shape), kept((8, width))],
        out_specs=[
            row(width),
            pl.BlockSpec((width, tile), lambda i: (0, jnp.clip(i - steps, 0, tiles - 1))),
            whole((width, 128)),
        ],
        out_shape=[
            jax.ShapeDtypeStruct((rows, width), BF),
            jax.ShapeDtypeStruct((width, 3 * width), BF),
            jax.ShapeDtypeStruct((width, 128), BF),
        ],
        scratch_shapes=[
            pltpu.VMEM((width, rows), BF),
            pltpu.VMEM((rows, 3 * width), BF),
            pltpu.VMEM((128, width), F32),
        ],
        compiler_params=pltpu.CompilerParams(vmem_limit_bytes=48 * MIB),
        cost_estimate=pl.CostEstimate(
            flops=12 * rows * width * width, bytes_accessed=28 * width * width, transcendentals=rows
        ),
        name="finish",
    )(tokens, back_project, weight, back_middle, gains, gain_two_grad)


def adam_step(master, grad, first, second, factor, rate, decay):
    clipped = factor * grad
    first_new = BETA_ONE * first + (1.0 - BETA_ONE) * clipped
    second_new = BETA_TWO * second + (1.0 - BETA_TWO) * clipped * clipped
    corrected = first_new / (1.0 - BETA_ONE**STEP)
    spread = jnp.sqrt(second_new / (1.0 - BETA_TWO**STEP)) + ADAM_EPS
    master_new = master - rate * (corrected / spread + decay * master)
    return (master_new, first_new, second_new)


def adam_call(squares, grads, masters, firsts, seconds):
    shard, width = grads[0].shape[0], grads[0].shape[1] - 128

    def body(*refs):
        squares_ref, refs = refs[0], refs[1:]
        ins, norm_ref, outs = refs[:19], refs[19], refs[20:]
        norm = jnp.sqrt(squares_ref[0:1, :])
        norm_ref[0, 0] = norm[0, 0]
        factor = jnp.minimum(1.0, CLIP / norm[:, 0:1])
        for j in range(5):
            grad = ins[0][:, :width] if j == 0 else ins[0][:, width:] if j == 4 else ins[j][...]
            if j == 4:
                filled = jnp.concatenate([grad, jnp.zeros((128 - shard, 128), F32)], 0)
                grad = jnp.transpose(filled)[:2, :shard]
            made = adam_step(
                ins[4 + j][...], grad, ins[9 + j][...], ins[14 + j][...], factor, RATES[j], DECAYS[j]
            )
            for kind in range(3):
                outs[5 * kind + j][...] = made[kind]
            outs[15 + j][...] = made[0].astype(BF)

    shapes = [jax.ShapeDtypeStruct((1, 1), F32)]
    shapes += [jax.ShapeDtypeStruct(m.shape, F32) for _ in range(3) for m in masters]
    shapes += [jax.ShapeDtypeStruct(m.shape, BF) for m in masters]
    vmem = pl.BlockSpec(memory_space=pltpu.VMEM)
    return pl.pallas_call(
        body,
        out_shape=shapes,
        out_specs=[pl.BlockSpec(memory_space=pltpu.SMEM)] + [vmem] * 20,
        compiler_params=pltpu.CompilerParams(vmem_limit_bytes=60 * MIB),
        name="adam",
    )(squares, *grads, *masters, *firsts, *seconds)


def prepare_call(dims, counts, qkv, out_t, in_up, down_t, gains, rows, band_rows):
    share = dims[3]
    images = rows // band_rows
    shard, width = qkv.shape[0], out_t.shape[1]
    wide = in_up.shape[1]

    def body(counts_ref, qkv_ref, out_ref, in_ref, down_ref, gain_ref, early_ref, late_ref, keep_ref, bias_ref):
        early_ref[:, : 3 * width] = qkv_ref[...].astype(BF)
        filled = jnp.concatenate([gain_ref[...], jnp.zeros((2, 128 - shard), F32)], 1)
        filled = jnp.concatenate([filled, jnp.zeros((126, 128), F32)], 0)
        early_ref[:, 3 * width :] = jnp.transpose(filled)[:shard].astype(BF)
        late_ref[:, :width] = out_ref[...].astype(BF)
        late_ref[:, width : width + wide] = in_ref[...].astype(BF)
        late_ref[:, width + wide :] = down_ref[...].astype(BF)
        band = lax.axis_index("band")
        image, part = band // share, lax.rem(band, share)
        count = counts_ref[image]
        down = lax.broadcasted_iota(jnp.int32, (band_rows, 1), 0)
        along = lax.broadcasted_iota(jnp.int32, (1, band_rows), 1)
        for s in range(images):
            first = (s * share + part) * band_rows
            keep_ref[s * band_rows : (s + 1) * band_rows, :] = jnp.where(down + first < count, 1.0, 0.0)
            for other in range(share):
                first = (s * share + lax.rem(part + other, share)) * band_rows
                at = (other * images + s) * band_rows
                bias_ref[:, at : at + band_rows] = jnp.where(along + first < count, 0.0, NEG)

    vmem = pl.BlockSpec(memory_space=pltpu.VMEM)
    return pl.pallas_call(
        body,
        out_shape=[
            jax.ShapeDtypeStruct((shard, 3 * width + 128), BF),
            jax.ShapeDtypeStruct((shard, width + wide + down_t.shape[1]), BF),
            jax.ShapeDtypeStruct((rows, 1), F32),
            jax.ShapeDtypeStruct((1, share * rows), F32),
        ],
        in_specs=[pl.BlockSpec(memory_space=pltpu.SMEM)] + [vmem] * 5,
        out_specs=[vmem] * 4,
        compiler_params=pltpu.CompilerParams(vmem_limit_bytes=60 * MIB),
        name="prepare",
    )(counts, qkv, out_t, in_up, down_t, gains)


def grid_of(n_img):
    big_y = max(d for d in range(1, n_img + 1) if n_img % d == 0 and d * d <= n_img)
    return big_y, n_img // big_y


def on_device(
    patches,
    cotangent,
    valid_counts,
    qkv_master,
    out_master,
    in_master,
    down_master,
    gain_master,
    qkv_first,
    out_first,
    in_first,
    down_first,
    gain_first,
    qkv_second,
    out_second,
    in_second,
    down_second,
    gain_second,
):
    images, band_rows, width = patches.shape
    n_img, n_band = lax.axis_size("img"), lax.axis_size("band")
    share = n_band // images
    big_y, big_x = grid_of(n_img)
    dims = (big_y, big_x, n_band // 2, share)
    rows = images * band_rows
    shard = qkv_master.shape[0]
    own_comm = shard % 8 == 0
    both = ("img", "band")

    places = [[s * share + r for s in range(images)] for r in range(share)]

    def exchange(chunks):
        return lax.all_to_all(chunks, "band", 0, 0, axis_index_groups=places, tiled=True)

    def blocks_of(grads):
        return [g.reshape(dims[:3] + (2, shard, g.shape[1])) for g in grads]

    early, late, row_keep, bias = prepare_call(
        dims,
        valid_counts,
        qkv_master,
        jnp.transpose(out_master),
        in_master,
        jnp.transpose(down_master),
        gain_master,
        rows,
        band_rows,
    )
    if own_comm:
        w_early, tokens_low = gather_call(dims, "gather", 0, [early], patches)
        w_early = w_early.reshape(width, early.shape[1])
    else:
        w_early = lax.all_gather(early, both, axis=0, tiled=True)
        tokens_low = exchange(patches)
    tokens = tokens_low.reshape(rows, width)
    attended, log_sums, kv, cotangent_low, project, gain_rows, *late_all = attend(
        dims, 1, tokens, w_early, bias, rows // 4, [late] if own_comm else [], cotangent
    )
    if own_comm:
        w_late = late_all[0].reshape(width, late.shape[1])
    else:
        w_late = lax.all_gather(late, both, axis=0, tiled=True)

    result_low, back_middle, back_attended, gain_two_grad, *late_grads = mlp_call(
        tokens,
        attended,
        cotangent_low.reshape(rows, width),
        row_keep,
        w_late,
        gain_rows,
        min(512, rows),
    )
    result_low = result_low.reshape(images, band_rows, width)
    back_project, *late_sums, squares, output = attend_back(
        dims,
        2,
        project,
        kv,
        bias,
        attended,
        log_sums,
        back_attended,
        rows // 4,
        blocks_of(late_grads) if own_comm else [],
        result_low,
    )
    if not own_comm:
        late_sums = [lax.psum_scatter(g.astype(F32), both, scatter_dimension=0, tiled=True) for g in late_grads]
    if own_comm:
        qkv_sum, back_input, total = finale_call(
            dims, 3, tokens, back_project, w_early, back_middle, gain_rows, gain_two_grad, squares, images
        )
    else:
        back_rows, *early_grads = finish_call(
            tokens, back_project, w_early, back_middle, gain_rows, gain_two_grad, min(256, rows)
        )
        grad = jnp.concatenate([g.astype(F32) for g in early_grads], 1)
        qkv_sum = lax.psum_scatter(grad, both, scatter_dimension=0, tiled=True)
        back_input = exchange(back_rows.reshape(images, band_rows, width))
        squares = sum(jnp.sum(g * g) for g in late_sums + [qkv_sum])
        total = lax.psum(jnp.broadcast_to(squares, (8, 128)), both)
    out_sum, in_sum, down_sum = late_sums

    def turned(arrays):
        return [jnp.transpose(a) if j in (1, 3) else a for j, a in enumerate(arrays)]

    norm, *updated = adam_call(
        total,
        [qkv_sum, out_sum, in_sum, down_sum],
        turned([qkv_master, out_master, in_master, down_master, gain_master]),
        turned([qkv_first, out_first, in_first, down_first, gain_first]),
        turned([qkv_second, out_second, in_second, down_second, gain_second]),
    )
    updated = [a for kind in range(4) for a in turned(updated[5 * kind : 5 * kind + 5])]
    return (output, back_input, norm.reshape(())) + tuple(updated)


def solution(mesh):
    rows_split, columns_split = P(("img", "band"), None), P(None, ("img", "band"))
    weights = (rows_split, columns_split, rows_split, columns_split, columns_split)
    tokens = P("img", "band", None)
    return jax.shard_map(
        on_device,
        mesh=mesh,
        in_specs=(tokens, tokens, P("img")) + weights * 3,
        out_specs=(tokens, tokens, P()) + weights * 4,
        check_vma=False,
    )
```

```python
import functools

import jax
import jax.numpy as jnp
from jax import lax
from jax.experimental import pallas as pl
from jax.experimental.pallas import tpu as pltpu
from jax.sharding import PartitionSpec as P

HEADS = 12
HEAD_DIM = 64
PAIR = 2 * HEAD_DIM
STEP = 10
EPS = 1e-06
NEG = -1000000000.0
SCALE = 0.125
CLIP = 1.0
BETA_ONE = 0.9
BETA_TWO = 0.999
ADAM_EPS = 1e-08
RATES = (0.06, 0.5, 0.06, 0.04, 0.5)
DECAYS = (0.1, 0.1, 0.1, 0.1, 0.0)
BF = jnp.bfloat16
F32 = jnp.float32
MESH = pl.DeviceIdType.MESH
ANY = pl.BlockSpec(memory_space=pl.ANY)
MIB = 2**20


class Net:
    def __init__(self, dims, send, recv, local):
        self.dims = dims
        big_y, big_x, big_z, share = dims
        img, band = lax.axis_index("img"), lax.axis_index("band")
        self.y, self.x = img // big_x, img % big_x
        self.z, self.c = band // 2, band % 2
        self.twin = 1 - self.c
        image, self.part = band // share, band % share
        self.image, self.images = image, 2 * big_z // share
        self.send, self.recv, self.local = send, recv, local
        self.used, self.used_local = 0, 0
        self.lines = {}
        for name, size in zip("yxzc", (big_y, big_x, big_z, 2)):
            places = []
            for d in range(1, size):
                at = dict(y=self.y, x=self.x, z=self.z, c=self.c)
                at[name] = lax.rem(at[name] + d, size)
                places.append((at[name], (at["y"] * big_x + at["x"], at["z"] * 2 + at["c"])))
            self.lines[name] = places
        self.band, self.img = band, img
        self.lines["band"], self.lines["img"] = [], []
        for d in range(1, 2 * big_z):
            other = lax.rem(band + d, 2 * big_z)
            self.lines["band"].append((other, (img, other)))
        for d in range(1, big_y * big_x):
            other = lax.rem(img + d, big_y * big_x)
            self.lines["img"].append((other, (other, band)))
        across, along = lax.rem(self.x + 1, big_x), lax.rem(self.y + 1, big_y)
        one = self.c
        self.near = (jnp.where(one == 0, self.y, along), jnp.where(one == 0, across, self.x))
        self.next = (jnp.where(one == 0, along, self.y), jnp.where(one == 0, self.x, across))
        self.far = (along, across)
        self.near_device = (self.near[0] * big_x + self.near[1], band)
        self.next_device = (self.next[0] * big_x + self.next[1], band)
        self.lines["image"] = []
        for d in range(1, self.images):
            other = lax.rem(image + d, self.images)
            self.lines["image"].append((other, (img, other * share + self.part)))
        self.lines["share"] = []
        for d in range(1, share):
            other = lax.rem(self.part + d, share)
            self.lines["share"].append((other, (img, image * share + other)))

    def line(self, name):
        return self.lines[name]

    def greet(self, kinds):
        barrier = pltpu.get_barrier_semaphore()
        count = 0
        for kind in kinds:
            for _, target in self.lines[kind]:
                pl.semaphore_signal(barrier, inc=1, device_id=target, device_id_type=MESH)
            count += len(self.lines[kind])
        pl.semaphore_wait(barrier, count)

    def copy(self, source, target_ref, target):
        made = self.plan(source, target_ref, target)
        made.start()
        return made

    def plan(self, source, target_ref, target):
        self.used += 1
        return Move(source, target_ref, self.send, self.recv, self.used - 1, target)

    def local_copy(self, source, target_ref):
        self.used_local += 1
        made = Move(source, target_ref, None, self.local, self.used_local - 1, None)
        made.start()
        return made


class Part:
    def __init__(self, ref, index=None):
        self.ref, self.index = ref, index

    def __getitem__(self, index):
        return Part(self.ref, index)

    def view(self):
        return self.ref if self.index is None else self.ref.at[self.index]


class Move:
    def __init__(self, source, target_ref, send, recv, at, target):
        self.source, self.target_ref = source, target_ref
        self.send, self.recv, self.at, self.target = send, recv, at, target

    def build(self):
        if self.target is None:
            return pltpu.make_async_copy(self.source.view(), self.target_ref.view(), self.recv.at[self.at])
        return pltpu.make_async_remote_copy(
            src_ref=self.source.view(),
            dst_ref=self.target_ref.view(),
            send_sem=self.send.at[self.at],
            recv_sem=self.recv.at[self.at],
            device_id=self.target,
            device_id_type=MESH,
        )

    def start(self):
        self.build().start()

    def wait(self):
        self.build().wait()

    def wait_recv(self):
        self.build().wait_recv()

    def wait_send(self):
        self.build().wait_send()


def drive(tasks):
    waiting = list(tasks)
    turn = 0
    while waiting:
        left = []
        for start, task in waiting:
            if start <= turn:
                try:
                    next(task)
                except StopIteration:
                    continue
            left.append((start, task))
        waiting = left
        turn += 1


def exchange_images(net, source, target, idle=1):
    moves = [net.copy(Part(source)[other], Part(target)[net.image], dev) for other, dev in net.line("image")]
    own = net.local_copy(Part(source)[net.image], Part(target)[net.image])
    for _ in range(idle):
        yield
    for move in moves:
        move.wait_recv()
    own.wait()
    for move in moves:
        move.wait_send()


def gather(net, source, target, columns):
    cols = pl.ds(*columns)
    y, x, c = net.y, net.x, net.c
    (_, twin), = net.line("c")

    def blocks(place):
        return Part(target)[place[0], place[1], :, c, :, cols]

    here = Part(target)[y, x, net.z, c, :, cols]
    own = net.local_copy(Part(source)[:, cols], here)
    from_z = [net.copy(Part(source)[:, cols], here, dev) for _, dev in net.line("z")]
    yield
    own.wait()
    for move in from_z:
        move.wait_recv()
    mine = blocks((y, x))
    first = net.copy(mine, mine, net.near_device)
    second = net.copy(mine, mine, net.next_device)
    twins = [net.copy(mine, mine, twin)]
    yield
    first.wait_recv()
    near = blocks(net.near)
    third = net.copy(near, near, net.next_device)
    twins.append(net.copy(near, near, twin))
    yield
    second.wait_recv()
    third.wait_recv()
    for place in (net.next, net.far):
        twins.append(net.copy(blocks(place), blocks(place), twin))
    yield
    for move in twins:
        move.wait_recv()
    for move in from_z + [first, second, third] + twins:
        move.wait_send()


def gather_copies(dims):
    return dims[2] - 1 + 3 + 4


def scatter_copies(dims):
    return dims[0] + dims[1] + dims[2] - 3 + 1


def add_up(own, others):
    if len(others) == 1:
        return own + others[0]
    total = own.astype(F32)
    for other in others:
        total = total + other.astype(F32)
    return total.astype(own.dtype)


def scatter(net, grad, held, from_core, from_first, from_second, from_z, out, squares, columns, order, offset=0):
    big_y, big_x, big_z, _ = net.dims
    cols = pl.ds(*columns)
    y, x, z, c = net.y, net.x, net.z, net.c
    sent = []
    (_, twin), = net.line("c")
    moves = [net.copy(Part(grad)[:, :, :, net.twin, :, cols], Part(from_core), twin)]
    sent += moves
    own = net.local_copy(Part(grad)[:, :, :, c, :, cols], Part(held))
    yield
    own.wait()
    moves[0].wait_recv()

    def first_add(at, _):
        a, b, d = at // (big_x * big_z), (at // big_z) % big_x, at % big_z
        held[a, b, d] = held[a, b, d] + from_core[a, b, d]
        return 0

    lax.fori_loop(0, big_y * big_x * big_z, first_add, 0)
    moves = []
    for slot, (other, dev) in enumerate(net.line(order[0])):
        part = Part(held)[:, other] if order[0] == "x" else Part(held)[other]
        moves.append(net.copy(part, Part(from_first)[slot], dev))
    sent += moves
    yield
    for move in moves:
        move.wait_recv()
    left = big_y if order[0] == "x" else big_x

    def second_add(at, _):
        a, d = at // big_z, at % big_z
        place = (a, x, d) if order[0] == "x" else (y, a, d)
        held[place] = add_up(held[place], [from_first[slot, a, d] for slot in range(len(moves))])
        return 0

    lax.fori_loop(0, left * big_z, second_add, 0)
    moves = []
    for slot, (other, dev) in enumerate(net.line(order[1])):
        part = Part(held)[other, x] if order[1] == "y" else Part(held)[y, other]
        moves.append(net.copy(part, Part(from_second)[slot], dev))
    sent += moves
    yield
    for move in moves:
        move.wait_recv()

    def third_add(d, _):
        held[y, x, d] = add_up(held[y, x, d], [from_second[slot, d] for slot in range(len(moves))])
        return 0

    lax.fori_loop(0, big_z, third_add, 0)
    moves = []
    for slot, (other, dev) in enumerate(net.line("z")):
        moves.append(net.copy(Part(held)[y, x, other], Part(from_z)[slot], dev))
    sent += moves
    yield
    for move in moves:
        move.wait_recv()
    total = held[y, x, z].astype(F32)
    for slot in range(len(moves)):
        total = total + from_z[slot].astype(F32)
    out[:, offset + columns[0] : offset + columns[0] + columns[1]] = total
    tile = squares[...]
    for a in range(total.shape[0] // 8):
        for b in range(columns[1] // 128):
            piece = total[8 * a : 8 * a + 8, 128 * b : 128 * b + 128]
            tile = tile + piece * piece
    squares[...] = tile
    for move in sent:
        move.wait_send()


def scatter_scratch(dims, rows, columns, order):
    big_y, big_x, big_z, _ = dims
    width = columns[1]
    ahead, left = (big_x, big_y) if order[0] == "x" else (big_y, big_x)
    return [
        pltpu.VMEM((big_y, big_x, big_z, rows, width), BF),
        pltpu.VMEM((big_y, big_x, big_z, rows, width), BF),
        pltpu.VMEM((ahead - 1, left, big_z, rows, width), BF),
        pltpu.VMEM((left - 1, big_z, rows, width), BF),
        pltpu.VMEM((big_z - 1, rows, width), BF),
    ]


def sum_tiles(net, tile, slots):
    first = 0
    for name, me in (("band", net.band), ("img", net.img)):
        places = net.line(name)
        slots[first + me] = tile[...]
        moves = [net.copy(Part(tile), Part(slots)[first + me], dev) for _, dev in places]
        for move in moves:
            move.wait_recv()
        for move in moves:
            move.wait_send()
        total = slots[first]
        for d in range(1, len(places) + 1):
            total = total + slots[first + d]
        tile[...] = total
        first += len(places) + 1


def sems(count):
    return pltpu.SemaphoreType.DMA((max(count, 1),))


def halves(width):
    units = width // 128
    low = (units + 1) // 2 * 128
    if low == width:
        return [((0, width), "xy")]
    return [((0, low), "xy"), ((low, width - low), "yx")]


def pieces(width, shares):
    units, found, start = width // 128, [], 0
    for group in range(len(shares)):
        stop = units * sum(shares[: group + 1]) // sum(shares) * 128
        found.append((start, stop - start))
        start = stop
    return found


def gather_call(dims, name, number, blocks, images=None):
    big_y, big_x, big_z, share = dims
    parts = [[(0, block.shape[1])] for block in blocks]
    copies = sum(len(p) for p in parts) * gather_copies(dims)
    local = sum(len(p) for p in parts)
    n = len(blocks)
    with_images = images is not None
    if with_images:
        copies += images.shape[0] - 1
        local += 1

    def body(*refs):
        ins, rest = refs[: n + with_images], refs[n + with_images :]
        outs, (send, recv, local_sem) = rest[: n + with_images], rest[n + with_images :]
        net = Net(dims, send, recv, local_sem)
        net.greet("zxyc" if not with_images else ["z", "x", "y", "c", "image"])
        tasks = []
        for j in range(n):
            for columns in parts[j]:
                tasks.append((0, gather(net, ins[j], outs[j], columns)))
        if with_images:
            tasks.append((1, exchange_images(net, ins[n], outs[n], 3)))
        drive(tasks)

    args = list(blocks) + ([images] if with_images else [])
    shapes = [jax.ShapeDtypeStruct((big_y, big_x, big_z, 2) + b.shape, b.dtype) for b in blocks]
    if with_images:
        shapes.append(jax.ShapeDtypeStruct(images.shape, images.dtype))
    return pl.pallas_call(
        body,
        out_shape=shapes,
        in_specs=[ANY] * len(args),
        out_specs=[ANY] * len(shapes),
        scratch_shapes=[sems(copies), sems(copies), sems(local)],
        compiler_params=pltpu.CompilerParams(collective_id=number, has_side_effects=True),
        name=name,
    )(*args)


def finale_call(dims, number, tokens, back_project, weight, back_middle, gains, gain_two_grad, squares, images):
    big_y, big_x, big_z, _ = dims
    rows, width = tokens.shape
    block = rows // images
    devices = 2 * big_x * big_y * big_z
    shard = width // devices
    parts = halves(3 * width + 128)
    tile = 256
    band_size, img_size = 2 * big_z, big_x * big_y
    copies = len(parts) * scatter_copies(dims) + images - 1 + band_size + img_size - 2
    local = len(parts) + 5 + 2 * images
    scratch = [sems(copies), sems(copies), sems(local)]
    for columns, order in parts:
        scratch += scatter_scratch(dims, shard, columns, order)
    n_fixed = 3 + 5 * len(parts)
    scratch += [
        pltpu.VMEM((8, 128), F32),
        pltpu.VMEM((band_size + img_size, 8, 128), F32),
        pltpu.VMEM(tokens.shape, BF),
        pltpu.VMEM(back_project.shape, BF),
        pltpu.VMEM(weight.shape, BF),
        pltpu.VMEM(back_middle.shape, F32),
        pltpu.VMEM((images, block, width), BF),
        pltpu.VMEM((width, rows), BF),
        pltpu.VMEM((128, width), F32),
    ]
    scratch += [pltpu.VMEM((big_y, big_x, big_z, 2, shard, columns[1]), BF) for columns, _ in parts]

    def body(*refs):
        x_hbm, b_hbm, w_hbm, m_hbm, g_ref, two_ref, squares_ref = refs[:7]
        sum_ref, moved, total_ref, rest = refs[7], refs[8], refs[9], refs[10:]
        tally, slots, x_all, b_all, w_all, m_all, sent, normed_t, gain_rows = rest[n_fixed : n_fixed + 9]
        grads = rest[n_fixed + 9 :]
        net = Net(dims, *rest[:3])
        order = [other for other, _ in net.line("image")] + [net.image]
        load_w = net.local_copy(Part(w_hbm), Part(w_all))
        loads = []
        for chunk in order:
            at = pl.ds(pl.multiple_of(chunk * block, block), block)
            loads.append([net.local_copy(Part(a)[at, :], Part(b)[at, :]) for a, b in ((b_hbm, b_all), (x_hbm, x_all))])
            if len(loads) == 1:
                load_m = net.local_copy(Part(m_hbm), Part(m_all))
        net.greet(["z", "x", "y", "c", "image", "band", "img"])
        tally[...] = squares_ref[...]
        gain_rows[...] = jnp.zeros_like(gain_rows)
        gain_rows[1:2, :] = two_ref[0:1, :]
        load_w.wait()
        moves = []
        for place, chunk in enumerate(order):
            for load in loads[place]:
                load.wait()
            if place == 0:
                load_m.wait()
            at = pl.ds(pl.multiple_of(chunk * block, block), block)
            gain = g_ref[0:1, :]
            x = x_all[at, :].astype(F32)
            scale = inverse_rms(x)
            normed_t[:, place * block : (place + 1) * block] = jnp.transpose((x * scale * gain).astype(BF))
            into, rows_of_gain = norm_back(mm(b_all[at, :], w_all[:, : 3 * width], 1, 1), x, scale, gain)
            sent[chunk] = (m_all[at, :] + into).astype(BF)
            gain_rows[0:1, :] += jnp.sum(rows_of_gain, 0, keepdims=True)
            if place < images - 1:
                moves.append(net.copy(Part(sent)[chunk], Part(moved)[net.image], net.line("image")[place][1]))
            else:
                own = net.local_copy(Part(sent)[chunk], Part(moved)[net.image])
        tasks = []
        for k, (columns, turn) in enumerate(parts):
            buffers = rest[3 + 5 * k : 8 + 5 * k]
            for low in range(columns[0], min(columns[0] + columns[1], 3 * width), tile):
                total = jnp.zeros((width, tile), F32)
                for place, chunk in enumerate(order):
                    at = pl.ds(pl.multiple_of(chunk * block, block), block)
                    inner = slice(place * block, (place + 1) * block)
                    total = total + mm(normed_t[:, inner], b_all[at, low : low + tile], 1, 0)
                into = slice(low - columns[0], low - columns[0] + tile)
                grads[k][..., into] = total.astype(BF).reshape(grads[k].shape[:5] + (tile,))
            if k == len(parts) - 1:
                turned = jnp.transpose(gain_rows[...]).astype(BF)
                grads[k][..., columns[1] - 128 :] = turned.reshape(grads[k].shape[:5] + (128,))
            task = scatter(net, grads[k], *buffers, sum_ref, tally, (0, columns[1]), turn, columns[0])
            next(task)
            tasks.append((0, task))
        drive(tasks)
        sum_tiles(net, tally, slots)
        total_ref[...] = jnp.broadcast_to(jnp.sum(tally[...], keepdims=True), (8, 128))
        for move in moves:
            move.wait_recv()
        own.wait()
        for move in moves:
            move.wait_send()

    vmem = pl.BlockSpec(memory_space=pltpu.VMEM)
    shapes = [
        jax.ShapeDtypeStruct((shard, 3 * width + 128), F32),
        jax.ShapeDtypeStruct((images, block, width), BF),
        jax.ShapeDtypeStruct((8, 128), F32),
    ]
    return pl.pallas_call(
        body,
        out_shape=shapes,
        in_specs=[ANY] * 4 + [vmem] * 3,
        out_specs=[vmem, ANY, vmem],
        scratch_shapes=scratch,
        compiler_params=pltpu.CompilerParams(
            collective_id=number, has_side_effects=True, vmem_limit_bytes=61 * MIB
        ),
        name="finale",
    )(tokens, back_project, weight, back_middle, gains, gain_two_grad, squares)


def whole(shape):
    return pl.BlockSpec(shape, lambda i: (0,) * len(shape))


def kept(shape):
    return pl.BlockSpec(shape, lambda i: (0,) * len(shape), pipeline_mode=pl.Buffered(1))


def inverse_rms(value):
    return lax.rsqrt(jnp.mean(value * value, -1, keepdims=True) + EPS)


def mm(a, b, ca, cb):
    return lax.dot_general(a, b, (((ca,), (cb,)), ((), ())), preferred_element_type=F32)


def at_turn(turn, events):
    def visit(whens):
        if len(whens) == 1:

            @pl.when(turn == whens[0])
            def _():
                for task in events[whens[0]]:
                    next(task, None)

        elif whens:
            middle = len(whens) // 2

            @pl.when(turn < whens[middle])
            def _():
                visit(whens[:middle])

            @pl.when(turn >= whens[middle])
            def _():
                visit(whens[middle:])

    visit(sorted(events))


def schedule(tasks, turns, last):
    events, tail = {}, []
    for task, when in zip(tasks, turns):
        for turn in when:
            if turn < last:
                events.setdefault(turn, []).append(task)
            else:
                tail.append(task)
    return events, tail


def lanes_of(h):
    lane = lax.broadcasted_iota(jnp.int32, (1, PAIR), 1) < HEAD_DIM
    return lane if h == 0 else ~lane


def attend(dims, number, tokens, weight, bias, block, weights, chunks):
    big_y, big_x, big_z, share = dims
    rows, width = tokens.shape
    pairs = width // PAIR
    others = share - 1
    blocks = 4
    n = len(weights)
    last = LEAD + 4 * pairs
    parts = [
        (j, columns, GATHER_TURNS[group])
        for j, w in enumerate(weights)
        for group, columns in enumerate(pieces(w.shape[1], GATHER_SHARES))
    ]
    copies = len(parts) * gather_copies(dims) + others * 2 * pairs + chunks.shape[0] - 1

    def body(*refs):
        x_ref, w_ref, bias_ref, chunks_in = refs[:4]
        blocks_in, refs = refs[4 : 4 + n], refs[4 + n :]
        o_ref, l_ref, kv_out, chunks_out, project_ref, gains_ref, refs = refs[:6] + (refs[6:],)
        gathered, (kv_held, send, recv, local) = refs[:n], refs[n:]
        h = pl.program_id(0)
        net = Net(dims, send, recv, local)

        def move_keys(j):
            moves = []
            for slot, (_, target) in enumerate(net.line("share")):
                source = Part(project_ref)[:, pl.ds(width + PAIR * j, PAIR)]
                moves.append(net.plan(source, Part(kv_held)[others - 1 - slot, j], target))
            return moves

        key_moves = [move_keys(j) for j in range(2 * pairs)]
        keep = Move(Part(kv_held), Part(kv_out), None, local, len(parts) + 1, None)
        tasks = [gather(net, blocks_in[j], gathered[j], columns) for j, columns, _ in parts]
        tasks.append(exchange_images(net, chunks_in, chunks_out))
        turns = [turn for _, _, turn in parts] + [CHUNK_TURNS]
        events, tail = schedule(tasks, turns, last)

        @pl.when(h == 0)
        def _():
            net.greet(["z", "x", "y", "c", "image"] + (["share"] if share > 2 else []))
            gains_ref[...] = jnp.transpose(w_ref[:, 3 * width :].astype(F32))[:8]

        @pl.when(h == 0)
        def _():
            def row_step(i, _):
                at_turn(i, {t: e for t, e in events.items() if t < LEAD})
                at = pl.ds(pl.multiple_of(i * block, block), block)
                x = x_ref[at, :].astype(F32)
                normed = (x * inverse_rms(x) * gains_ref[0:1, :]).astype(BF)
                project_ref[at, :] = mm(normed, w_ref[:, : 3 * width], 1, 0).astype(BF)
                return 0

            lax.fori_loop(0, blocks, row_step, 0)
            for j in range(pairs):
                for move in key_moves[j] + key_moves[j + pairs]:
                    move.start()

        for j in range(pairs):

            @pl.when(h == j)
            def _(j=j):
                for move in key_moves[j] + key_moves[j + pairs]:
                    move.wait_recv()
                if j == pairs - 1:
                    keep.start()

        def own(first):
            return pl.ds(pl.multiple_of((h + first) * PAIR, PAIR), PAIR)

        def step(i, _):
            at_turn(LEAD + h * 4 + i, {t: e for t, e in events.items() if t >= LEAD})
            at = pl.ds(pl.multiple_of(i * block, block), block)
            k = jnp.concatenate([project_ref[:, own(pairs)]] + [kv_held[s, h] for s in range(others)], 0)
            v = jnp.concatenate(
                [project_ref[:, own(2 * pairs)]] + [kv_held[s, h + pairs] for s in range(others)], 0
            )
            q = project_ref[at, own(0)] * jnp.asarray(SCALE, BF)
            mixed, logs = [], []
            for half in range(2):
                scores = mm(jnp.where(lanes_of(half), q, jnp.zeros_like(q)), k, 1, 1) + bias_ref[...]
                highest = jnp.max(scores, -1, keepdims=True)
                powers = jnp.exp(scores - highest)
                total = jnp.sum(powers, -1, keepdims=True)
                mixed.append(mm(powers.astype(BF), v, 1, 0) / total)
                logs.append(highest + jnp.log(total))
            o_ref[at, :] = jnp.where(lanes_of(0), mixed[0], mixed[1]).astype(BF)
            l_ref[at, :] = jnp.where(lanes_of(0), logs[0], logs[1])
            return 0

        lax.fori_loop(0, blocks, step, 0)

        @pl.when(h == pairs - 1)
        def _():
            for task in tail:
                next(task, None)
            for moves in key_moves:
                for move in moves:
                    move.wait_send()
            keep.wait()

    column = lambda first: pl.BlockSpec((rows, PAIR), lambda h: (0, h + first))
    keys = rows * share
    shapes = [
        jax.ShapeDtypeStruct((rows, width), BF),
        jax.ShapeDtypeStruct((rows, width), F32),
        jax.ShapeDtypeStruct((others, 2 * pairs, rows, PAIR), BF),
        jax.ShapeDtypeStruct(chunks.shape, chunks.dtype),
        jax.ShapeDtypeStruct((rows, 3 * width), BF),
        jax.ShapeDtypeStruct((8, width), F32),
    ] + [jax.ShapeDtypeStruct((big_y, big_x, big_z, 2) + w.shape, w.dtype) for w in weights]
    return pl.pallas_call(
        body,
        grid=(pairs,),
        in_specs=[kept(tokens.shape), kept(weight.shape), kept((1, keys))] + [ANY] * (1 + n),
        out_specs=[column(0), column(0), ANY, ANY, kept((rows, 3 * width)), kept((8, width))] + [ANY] * n,
        out_shape=shapes,
        scratch_shapes=[
            pltpu.VMEM((others, 2 * pairs, rows, PAIR), BF),
            sems(copies),
            sems(copies),
            sems(len(parts) + 2),
        ],
        compiler_params=pltpu.CompilerParams(
            collective_id=number, has_side_effects=True, vmem_limit_bytes=60 * MIB
        ),
        cost_estimate=pl.CostEstimate(
            flops=16 * rows * keys * width, bytes_accessed=8 * keys * width, transcendentals=rows * keys * HEADS
        ),
        name="attend",
    )(tokens, weight, bias, chunks, *weights)


LEAD = 4
GATHER_SHARES = (1, 2, 2, 2, 2, 1)
GATHER_TURNS = (
    (0, 3, 6, 10, 12),
    (0, 5, 10, 14, 18),
    (1, 8, 14, 19, 22),
    (2, 12, 19, 23, 26),
    (3, 15, 22, 27, 28),
    (5, 18, 25, 28, 28),
)
CHUNK_TURNS = (12, 28)
SCATTER_TURNS = (
    ((2, 5, 13, 20, 24),),
    ((0, 2, 8, 15, 21), (0, 3, 10, 17, 23)),
    ((1, 4, 12, 19, 24),),
)
RESULT_TURNS = (0, 24)


def attend_back(dims, number, project, kv, bias, mixed, logs, back, block, grads, chunks):
    big_y, big_x, big_z, share = dims
    rows, width = mixed.shape
    pairs = width // PAIR
    others = share - 1
    blocks = 4
    keys = rows * share
    n = len(grads)
    parts = [
        (j, (low + first, wide), order, SCATTER_TURNS[j][group])
        for j, g in enumerate(grads)
        for group, (first, width_of) in enumerate(pieces(g.shape[5], (1,) * len(SCATTER_TURNS[j])))
        for (low, wide), order in halves(width_of)
    ]
    copies = len(parts) * scatter_copies(dims) + others * 2 * pairs + chunks.shape[0] - 1

    def body(*refs):
        q_ref, k_ref, v_ref, k_other, v_other, bias_ref, mixed_ref, logs_ref, back_ref = refs[:9]
        grads_in, chunks_in, refs = refs[9 : 9 + n], refs[9 + n], refs[10 + n :]
        out_ref, sums, squares, chunks_out, refs = refs[0], refs[1 : 1 + n], refs[1 + n], refs[2 + n], refs[3 + n :]
        dk_sums, dv_sums, parted, arrived, bias_column = refs[:5]
        send, recv, local = refs[5:8]
        buffers = refs[8:]
        h = pl.program_id(0)
        net = Net(dims, send, recv, local)

        def move_keys(j):
            moves = []
            for slot, (_, target) in enumerate(net.line("share")):
                moves.append(net.plan(Part(parted)[slot, j], Part(arrived)[others - 1 - slot, j], target))
            return moves

        key_moves = [move_keys(j) for j in range(2 * pairs)]
        tasks = [
            scatter(net, grads_in[j], *buffers[5 * k : 5 * k + 5], sums[j], squares, columns, order)
            for k, (j, columns, order, _) in enumerate(parts)
        ]
        tasks.append(exchange_images(net, chunks_in, chunks_out))
        turns = [turn for _, _, _, turn in parts] + [RESULT_TURNS]
        events, tail = schedule(tasks, turns, 4 * pairs)

        @pl.when(h == 0)
        def _():
            net.greet(["z", "x", "y", "c", "image"] + (["share"] if share > 2 else []))
            squares[...] = jnp.zeros_like(squares)
            bias_column[...] = jnp.transpose(jnp.broadcast_to(bias_ref[...], (PAIR, keys)))

        turn = lax.rem(h, 2)
        dk_sums[turn] = jnp.zeros((keys, PAIR), F32)
        dv_sums[turn] = jnp.zeros((keys, PAIR), F32)

        def step(i, _):
            at_turn(h * 4 + i, events)
            at = pl.ds(pl.multiple_of(i * block, block), block)
            k = jnp.concatenate([k_ref[...]] + [k_other[s, 0] for s in range(others)], 0)
            v = jnp.concatenate([v_ref[...]] + [v_other[s, 0] for s in range(others)], 0)
            q, do = q_ref[at, :] * jnp.asarray(SCALE, BF), back_ref[at, :]
            lse = jnp.transpose(logs_ref[at, :])
            products = jnp.transpose(do.astype(F32) * mixed_ref[at, :].astype(F32))
            dqs, dks, dvs = [], [], []
            mask = jnp.concatenate([bias_column[...]] * (block // PAIR), 1)
            for half in range(2):
                low, high = half * HEAD_DIM, (half + 1) * HEAD_DIM
                q_h = jnp.where(lanes_of(half), q, jnp.zeros_like(q))
                do_h = jnp.where(lanes_of(half), do, jnp.zeros_like(do))
                row_dots = jnp.sum(products[low:high, :], 0, keepdims=True)
                chances = jnp.exp(mm(k, q_h, 1, 1) + mask - lse[low : low + 1, :])
                slopes = mm(v, do_h, 1, 1)
                scores = (chances * (slopes - row_dots)).astype(BF)
                dqs.append(mm(scores, k, 0, 0))
                dks.append(mm(scores, q_h, 1, 0))
                dvs.append(mm(chances.astype(BF), do_h, 1, 0))
            dq = (jnp.where(lanes_of(0), dqs[0], dqs[1]) * SCALE).astype(BF)
            out_ref[at, pl.ds(pl.multiple_of(h * PAIR, PAIR), PAIR)] = dq
            dk_sums[turn] += dks[0] + dks[1]
            dv_sums[turn] += dvs[0] + dvs[1]
            return 0

        lax.fori_loop(0, blocks, step, 0)

        def finish(j):
            for move in key_moves[j] + key_moves[j + pairs]:
                move.wait_recv()
            for kept, sums_of in ((j, dk_sums), (j + pairs, dv_sums)):
                value = sums_of[j % 2, 0:rows, :]
                for slot in range(others):
                    value = value + arrived[slot, kept].astype(F32)
                out_ref[:, width + PAIR * kept : width + PAIR * (kept + 1)] = value.astype(BF)

        for j in range(pairs):

            @pl.when(h == j)
            def _(j=j):
                if j > 0:
                    finish(j - 1)
                for slot in range(others):
                    away = slice(rows * (slot + 1), rows * (slot + 2))
                    parted[slot, j] = dk_sums[j % 2, away, :].astype(BF)
                    parted[slot, j + pairs] = dv_sums[j % 2, away, :].astype(BF)
                for move in key_moves[j] + key_moves[j + pairs]:
                    move.start()
                if j == pairs - 1:
                    for task in tail:
                        next(task, None)
                    finish(j)
                    for moves in key_moves:
                        for move in moves:
                            move.wait_send()

    column = lambda first: pl.BlockSpec((rows, PAIR), lambda h: (0, h + first))
    other = lambda first: pl.BlockSpec((others, 1, rows, PAIR), lambda h: (0, h + first, 0, 0))
    whole = lambda shape: pl.BlockSpec(shape, lambda h: (0,) * len(shape))
    shard = grads[0].shape[4] if n else 0
    shapes = (
        [jax.ShapeDtypeStruct((rows, 3 * width), BF)]
        + [jax.ShapeDtypeStruct((shard, g.shape[5]), F32) for g in grads]
        + [jax.ShapeDtypeStruct((8, 128), F32)]
    )
    moved = jax.ShapeDtypeStruct(chunks.shape, chunks.dtype)
    scratch = [
        pltpu.VMEM((2, keys, PAIR), F32),
        pltpu.VMEM((2, keys, PAIR), F32),
        pltpu.VMEM((others, 2 * pairs, rows, PAIR), BF),
        pltpu.VMEM((others, 2 * pairs, rows, PAIR), BF),
        pltpu.VMEM((keys, PAIR), F32),
        sems(copies),
        sems(copies),
        sems(len(parts) + 1),
    ]
    for _, columns, order, _ in parts:
        scratch += scatter_scratch(dims, shard, columns, order)
    return pl.pallas_call(
        body,
        grid=(pairs,),
        in_specs=[
            column(0),
            column(pairs),
            column(2 * pairs),
            other(0),
            other(pairs),
            whole((1, keys)),
            column(0),
            column(0),
            column(0),
        ]
        + [ANY] * (n + 1),
        out_specs=[whole(s.shape) for s in shapes] + [ANY],
        out_shape=shapes + [moved],
        scratch_shapes=scratch,
        compiler_params=pltpu.CompilerParams(
            collective_id=number, has_side_effects=True, vmem_limit_bytes=60 * MIB
        ),
        cost_estimate=pl.CostEstimate(
            flops=40 * rows * keys * width, bytes_accessed=16 * keys * width, transcendentals=rows * keys * HEADS
        ),
        name="attend_back",
    )(project, project, project, kv, kv, bias, mixed, logs, back, *grads, chunks)


def norm_back(back, value, scale, gain):
    scaled = back * gain
    inner = jnp.mean(scaled * value, -1, keepdims=True)
    return scale * scaled - value * (scale * scale * scale * inner), back * (value * scale)


GELU_A = 0.7978845608028654
GELU_B = 0.044715


def mlp_call(tokens, attended, cotangent, keep, weights, gains, block):
    rows, width = tokens.shape
    hidden_units = (weights.shape[1] - width) // 3
    steps = rows // block
    tile = 512
    in_tiles, down_tiles = 2 * hidden_units // tile, hidden_units // tile
    part = 512

    def body(
        x_ref, a_ref, c_ref, keep_ref, w_ref, g_ref,
        result_ref, middle_ref, back_ref, gain_ref, g_out_ref, g_in_ref, g_down_ref,
        normed_t, low_t, branch_t, mixed, hidden, back_gu,
    ):
        i = pl.program_id(0)
        wo_ref = w_ref.at[:, :width]
        wi_ref = w_ref.at[:, width : width + 2 * hidden_units]
        wd_ref = w_ref.at[:, width + 2 * hidden_units :]

        @pl.when(i == 0)
        def _():
            gain_ref[...] = jnp.zeros_like(gain_ref)

        @pl.when(i < steps)
        def _():
            at = pl.ds(pl.multiple_of(i * block, block), block)
            gain = g_ref[1:2, :]
            a = a_ref[...]
            mixed[at, :] = a
            middle = x_ref[...].astype(F32) + mm(a, wo_ref[...], 1, 1)
            scale = inverse_rms(middle)
            normed = (middle * scale * gain).astype(BF)
            normed_t[:, at] = jnp.transpose(normed)
            back_result = keep_ref[...] * c_ref[...].astype(F32)
            low = back_result.astype(BF)
            low_t[:, at] = jnp.transpose(low)
            result, back = middle, jnp.zeros_like(middle)
            for p in range(hidden_units // part):
                one = slice(p * part, (p + 1) * part)
                two = slice(hidden_units + p * part, hidden_units + (p + 1) * part)
                gate = mm(normed, wi_ref[:, one], 1, 0)
                up = mm(normed, wi_ref[:, two], 1, 0)
                back_hidden = mm(low, wd_ref[:, one], 1, 0)
                square = gate * gate
                bend = jnp.tanh(GELU_A * (gate + GELU_B * (gate * square)))
                half = 0.5 + 0.5 * bend
                curve = gate * half
                slope = half + (0.5 * GELU_A) * gate * (1.0 - bend * bend) * (1.0 + (3.0 * GELU_B) * square)
                hid = (curve * up).astype(BF)
                back_gate = (back_hidden * up * slope).astype(BF)
                back_up = (back_hidden * curve).astype(BF)
                hidden[at, one] = hid
                back_gu[at, one] = back_gate
                back_gu[at, two] = back_up
                result = result + mm(hid, wd_ref[:, one], 1, 1)
                back = back + mm(back_gate, wi_ref[:, one], 1, 1) + mm(back_up, wi_ref[:, two], 1, 1)
            result_ref[...] = (keep_ref[...] * result).astype(BF)
            into, gain_rows = norm_back(back, middle, scale, gain)
            gain_ref[0:1, :] += jnp.sum(gain_rows, 0, keepdims=True)
            back_middle = back_result + into
            middle_ref[...] = back_middle
            branch = back_middle.astype(BF)
            branch_t[:, at] = jnp.transpose(branch)
            back_ref[...] = mm(branch, wo_ref[...], 1, 0).astype(BF)

        @pl.when(i == steps)
        def _():
            g_out_ref[...] = mm(branch_t[...], mixed[...], 1, 0).astype(BF)

        for t in range(in_tiles):

            @pl.when(i == steps + 1 + t)
            def _(t=t):
                g_in_ref[...] = mm(normed_t[...], back_gu[:, t * tile : (t + 1) * tile], 1, 0).astype(BF)

        for t in range(down_tiles):

            @pl.when(i == steps + 1 + in_tiles + t)
            def _(t=t):
                g_down_ref[...] = mm(low_t[...], hidden[:, t * tile : (t + 1) * tile], 1, 0).astype(BF)

    row = lambda last: pl.BlockSpec((block, last), lambda i: (jnp.minimum(i, steps - 1), 0))
    return pl.pallas_call(
        body,
        grid=(steps + 1 + in_tiles + down_tiles,),
        in_specs=[
            row(width),
            row(width),
            row(width),
            row(1),
            kept(weights.shape),
            kept(gains.shape),
        ],
        out_specs=[
            row(width),
            row(width),
            row(width),
            whole((8, width)),
            whole((width, width)),
            pl.BlockSpec((width, tile), lambda i: (0, jnp.clip(i - steps - 1, 0, in_tiles - 1))),
            pl.BlockSpec((width, tile), lambda i: (0, jnp.clip(i - steps - 1 - in_tiles, 0, down_tiles - 1))),
        ],
        out_shape=[
            jax.ShapeDtypeStruct((rows, width), BF),
            jax.ShapeDtypeStruct((rows, width), F32),
            jax.ShapeDtypeStruct((rows, width), BF),
            jax.ShapeDtypeStruct((8, width), F32),
            jax.ShapeDtypeStruct((width, width), BF),
            jax.ShapeDtypeStruct((width, 2 * hidden_units), BF),
            jax.ShapeDtypeStruct((width, hidden_units), BF),
        ],
        scratch_shapes=[
            pltpu.VMEM((width, rows), BF),
            pltpu.VMEM((width, rows), BF),
            pltpu.VMEM((width, rows), BF),
            pltpu.VMEM((rows, width), BF),
            pltpu.VMEM((rows, hidden_units), BF),
            pltpu.VMEM((rows, 2 * hidden_units), BF),
        ],
        compiler_params=pltpu.CompilerParams(vmem_limit_bytes=61 * MIB),
        cost_estimate=pl.CostEstimate(
            flops=6 * rows * width * (width + 3 * hidden_units),
            bytes_accessed=8 * width * (width + 3 * hidden_units),
            transcendentals=rows * hidden_units,
        ),
        name="mlp",
    )(tokens, attended, cotangent, keep, weights, gains)


def finish_call(tokens, back_project, weight, back_middle, gains, gain_two_grad, block):
    rows, width = tokens.shape
    steps = rows // block
    tiles, tile = 3, width

    def body(x_ref, b_ref, w_ref, m_ref, g_ref, two_ref, out_ref, grad_ref, gain_ref, normed_t, held, gain_rows):
        i = pl.program_id(0)

        @pl.when(i == 0)
        def _():
            gain_rows[...] = jnp.zeros_like(gain_rows)
            gain_rows[1:2, :] = two_ref[0:1, :]

        @pl.when(i < steps)
        def _():
            at = pl.ds(pl.multiple_of(i * block, block), block)
            gain = g_ref[0:1, :]
            x = x_ref[...].astype(F32)
            scale = inverse_rms(x)
            normed_t[:, at] = jnp.transpose((x * scale * gain).astype(BF))
            back = b_ref[...]
            held[at, :] = back
            into, rows_of_gain = norm_back(mm(back, w_ref[:, : 3 * width], 1, 1), x, scale, gain)
            out_ref[...] = (m_ref[...] + into).astype(BF)
            gain_rows[0:1, :] += jnp.sum(rows_of_gain, 0, keepdims=True)

        for t in range(tiles):

            @pl.when(i == steps + t)
            def _(t=t):
                grad_ref[...] = mm(normed_t[...], held[:, t * tile : (t + 1) * tile], 1, 0).astype(BF)

        @pl.when(i == steps)
        def _():
            gain_ref[...] = jnp.transpose(gain_rows[...]).astype(BF)

    row = lambda last: pl.BlockSpec((block, last), lambda i: (jnp.minimum(i, steps - 1), 0))
    return pl.pallas_call(
        body,
        grid=(steps + tiles,),
        in_specs=[row(width), row(3 * width), kept(weight.shape), row(width), kept(gains.shape), kept((8, width))],
        out_specs=[
            row(width),
            pl.BlockSpec((width, tile), lambda i: (0, jnp.clip(i - steps, 0, tiles - 1))),
            whole((width, 128)),
        ],
        out_shape=[
            jax.ShapeDtypeStruct((rows, width), BF),
            jax.ShapeDtypeStruct((width, 3 * width), BF),
            jax.ShapeDtypeStruct((width, 128), BF),
        ],
        scratch_shapes=[
            pltpu.VMEM((width, rows), BF),
            pltpu.VMEM((rows, 3 * width), BF),
            pltpu.VMEM((128, width), F32),
        ],
        compiler_params=pltpu.CompilerParams(vmem_limit_bytes=48 * MIB),
        cost_estimate=pl.CostEstimate(
            flops=12 * rows * width * width, bytes_accessed=28 * width * width, transcendentals=rows
        ),
        name="finish",
    )(tokens, back_project, weight, back_middle, gains, gain_two_grad)


def adam_step(master, grad, first, second, factor, rate, decay):
    clipped = factor * grad
    first_new = BETA_ONE * first + (1.0 - BETA_ONE) * clipped
    second_new = BETA_TWO * second + (1.0 - BETA_TWO) * clipped * clipped
    corrected = first_new / (1.0 - BETA_ONE**STEP)
    spread = jnp.sqrt(second_new / (1.0 - BETA_TWO**STEP)) + ADAM_EPS
    master_new = master - rate * (corrected / spread + decay * master)
    return (master_new, first_new, second_new)


def adam_call(squares, grads, masters, firsts, seconds):
    shard, width = grads[0].shape[0], grads[0].shape[1] - 128

    def body(*refs):
        squares_ref, refs = refs[0], refs[1:]
        ins, norm_ref, outs = refs[:19], refs[19], refs[20:]
        norm = jnp.sqrt(squares_ref[0:1, :])
        norm_ref[0, 0] = norm[0, 0]
        factor = jnp.minimum(1.0, CLIP / norm[:, 0:1])
        for j in range(5):
            grad = ins[0][:, :width] if j == 0 else ins[0][:, width:] if j == 4 else ins[j][...]
            if j == 4:
                filled = jnp.concatenate([grad, jnp.zeros((128 - shard, 128), F32)], 0)
                grad = jnp.transpose(filled)[:2, :shard]
            made = adam_step(
                ins[4 + j][...], grad, ins[9 + j][...], ins[14 + j][...], factor, RATES[j], DECAYS[j]
            )
            for kind in range(3):
                outs[5 * kind + j][...] = made[kind]
            outs[15 + j][...] = made[0].astype(BF)

    shapes = [jax.ShapeDtypeStruct((1, 1), F32)]
    shapes += [jax.ShapeDtypeStruct(m.shape, F32) for _ in range(3) for m in masters]
    shapes += [jax.ShapeDtypeStruct(m.shape, BF) for m in masters]
    vmem = pl.BlockSpec(memory_space=pltpu.VMEM)
    return pl.pallas_call(
        body,
        out_shape=shapes,
        out_specs=[pl.BlockSpec(memory_space=pltpu.SMEM)] + [vmem] * 20,
        compiler_params=pltpu.CompilerParams(vmem_limit_bytes=60 * MIB),
        name="adam",
    )(squares, *grads, *masters, *firsts, *seconds)


def prepare_call(dims, counts, qkv, out_t, in_up, down_t, gains, rows, band_rows):
    share = dims[3]
    images = rows // band_rows
    shard, width = qkv.shape[0], out_t.shape[1]
    wide = in_up.shape[1]

    def body(counts_ref, qkv_ref, out_ref, in_ref, down_ref, gain_ref, early_ref, late_ref, keep_ref, bias_ref):
        early_ref[:, : 3 * width] = qkv_ref[...].astype(BF)
        filled = jnp.concatenate([gain_ref[...], jnp.zeros((2, 128 - shard), F32)], 1)
        filled = jnp.concatenate([filled, jnp.zeros((126, 128), F32)], 0)
        early_ref[:, 3 * width :] = jnp.transpose(filled)[:shard].astype(BF)
        late_ref[:, :width] = out_ref[...].astype(BF)
        late_ref[:, width : width + wide] = in_ref[...].astype(BF)
        late_ref[:, width + wide :] = down_ref[...].astype(BF)
        band = lax.axis_index("band")
        image, part = band // share, lax.rem(band, share)
        count = counts_ref[image]
        down = lax.broadcasted_iota(jnp.int32, (band_rows, 1), 0)
        along = lax.broadcasted_iota(jnp.int32, (1, band_rows), 1)
        for s in range(images):
            first = (s * share + part) * band_rows
            keep_ref[s * band_rows : (s + 1) * band_rows, :] = jnp.where(down + first < count, 1.0, 0.0)
            for other in range(share):
                first = (s * share + lax.rem(part + other, share)) * band_rows
                at = (other * images + s) * band_rows
                bias_ref[:, at : at + band_rows] = jnp.where(along + first < count, 0.0, NEG)

    vmem = pl.BlockSpec(memory_space=pltpu.VMEM)
    return pl.pallas_call(
        body,
        out_shape=[
            jax.ShapeDtypeStruct((shard, 3 * width + 128), BF),
            jax.ShapeDtypeStruct((shard, width + wide + down_t.shape[1]), BF),
            jax.ShapeDtypeStruct((rows, 1), F32),
            jax.ShapeDtypeStruct((1, share * rows), F32),
        ],
        in_specs=[pl.BlockSpec(memory_space=pltpu.SMEM)] + [vmem] * 5,
        out_specs=[vmem] * 4,
        compiler_params=pltpu.CompilerParams(vmem_limit_bytes=60 * MIB),
        name="prepare",
    )(counts, qkv, out_t, in_up, down_t, gains)


def grid_of(n_img):
    big_y = max(d for d in range(1, n_img + 1) if n_img % d == 0 and d * d <= n_img)
    return big_y, n_img // big_y


def on_device(
    patches,
    cotangent,
    valid_counts,
    qkv_master,
    out_master,
    in_master,
    down_master,
    gain_master,
    qkv_first,
    out_first,
    in_first,
    down_first,
    gain_first,
    qkv_second,
    out_second,
    in_second,
    down_second,
    gain_second,
):
    images, band_rows, width = patches.shape
    n_img, n_band = lax.axis_size("img"), lax.axis_size("band")
    share = n_band // images
    big_y, big_x = grid_of(n_img)
    dims = (big_y, big_x, n_band // 2, share)
    rows = images * band_rows
    shard = qkv_master.shape[0]
    own_comm = shard % 8 == 0 and big_y == big_x == 2
    both = ("img", "band")

    places = [[s * share + r for s in range(images)] for r in range(share)]

    def exchange(chunks):
        return lax.all_to_all(chunks, "band", 0, 0, axis_index_groups=places, tiled=True)

    def blocks_of(grads):
        return [g.reshape(dims[:3] + (2, shard, g.shape[1])) for g in grads]

    early, late, row_keep, bias = prepare_call(
        dims,
        valid_counts,
        qkv_master,
        jnp.transpose(out_master),
        in_master,
        jnp.transpose(down_master),
        gain_master,
        rows,
        band_rows,
    )
    if own_comm:
        w_early, tokens_low = gather_call(dims, "gather", 0, [early], patches)
        w_early = w_early.reshape(width, early.shape[1])
    else:
        w_early = lax.all_gather(early, both, axis=0, tiled=True)
        tokens_low = exchange(patches)
    tokens = tokens_low.reshape(rows, width)
    attended, log_sums, kv, cotangent_low, project, gain_rows, *late_all = attend(
        dims, 1, tokens, w_early, bias, rows // 4, [late] if own_comm else [], cotangent
    )
    if own_comm:
        w_late = late_all[0].reshape(width, late.shape[1])
    else:
        w_late = lax.all_gather(late, both, axis=0, tiled=True)

    result_low, back_middle, back_attended, gain_two_grad, *late_grads = mlp_call(
        tokens,
        attended,
        cotangent_low.reshape(rows, width),
        row_keep,
        w_late,
        gain_rows,
        min(512, rows),
    )
    result_low = result_low.reshape(images, band_rows, width)
    back_project, *late_sums, squares, output = attend_back(
        dims,
        2,
        project,
        kv,
        bias,
        attended,
        log_sums,
        back_attended,
        rows // 4,
        blocks_of(late_grads) if own_comm else [],
        result_low,
    )
    if not own_comm:
        late_sums = [lax.psum_scatter(g.astype(F32), both, scatter_dimension=0, tiled=True) for g in late_grads]
    if own_comm:
        qkv_sum, back_input, total = finale_call(
            dims, 3, tokens, back_project, w_early, back_middle, gain_rows, gain_two_grad, squares, images
        )
    else:
        back_rows, *early_grads = finish_call(
            tokens, back_project, w_early, back_middle, gain_rows, gain_two_grad, min(256, rows)
        )
        grad = jnp.concatenate([g.astype(F32) for g in early_grads], 1)
        qkv_sum = lax.psum_scatter(grad, both, scatter_dimension=0, tiled=True)
        back_input = exchange(back_rows.reshape(images, band_rows, width))
        squares = sum(jnp.sum(g * g) for g in late_sums + [qkv_sum])
        total = lax.psum(jnp.broadcast_to(squares, (8, 128)), both)
    out_sum, in_sum, down_sum = late_sums

    def turned(arrays):
        return [jnp.transpose(a) if j in (1, 3) else a for j, a in enumerate(arrays)]

    norm, *updated = adam_call(
        total,
        [qkv_sum, out_sum, in_sum, down_sum],
        turned([qkv_master, out_master, in_master, down_master, gain_master]),
        turned([qkv_first, out_first, in_first, down_first, gain_first]),
        turned([qkv_second, out_second, in_second, down_second, gain_second]),
    )
    updated = [a for kind in range(4) for a in turned(updated[5 * kind : 5 * kind + 5])]
    return (output, back_input, norm.reshape(())) + tuple(updated)


def solution(mesh):
    rows_split, columns_split = P(("img", "band"), None), P(None, ("img", "band"))
    weights = (rows_split, columns_split, rows_split, columns_split, columns_split)
    tokens = P("img", "band", None)
    return jax.shard_map(
        on_device,
        mesh=mesh,
        in_specs=(tokens, tokens, P("img")) + weights * 3,
        out_specs=(tokens, tokens, P()) + weights * 4,
        check_vma=False,
    )
```

```python
import functools

import jax
import jax.numpy as jnp
from jax import lax
from jax.experimental import pallas as pl
from jax.experimental.pallas import tpu as pltpu
from jax.sharding import PartitionSpec as P

HEADS = 12
HEAD_DIM = 64
PAIR = 2 * HEAD_DIM
STEP = 10
EPS = 1e-06
NEG = -1000000000.0
SCALE = 0.125
CLIP = 1.0
BETA_ONE = 0.9
BETA_TWO = 0.999
ADAM_EPS = 1e-08
RATES = (0.06, 0.5, 0.06, 0.04, 0.5)
DECAYS = (0.1, 0.1, 0.1, 0.1, 0.0)
BF = jnp.bfloat16
F32 = jnp.float32
MESH = pl.DeviceIdType.MESH
ANY = pl.BlockSpec(memory_space=pl.ANY)
MIB = 2**20


class Net:
    def __init__(self, dims, send, recv, local):
        self.dims = dims
        big_y, big_x, big_z, share = dims
        img, band = lax.axis_index("img"), lax.axis_index("band")
        self.y, self.x = img // big_x, img % big_x
        self.z, self.c = band // 2, band % 2
        self.twin = 1 - self.c
        image, self.part = band // share, band % share
        self.image, self.images = image, 2 * big_z // share
        self.send, self.recv, self.local = send, recv, local
        self.used, self.used_local = 0, 0
        self.lines = {}
        for name, size in zip("yxzc", (big_y, big_x, big_z, 2)):
            places = []
            for d in range(1, size):
                at = dict(y=self.y, x=self.x, z=self.z, c=self.c)
                at[name] = lax.rem(at[name] + d, size)
                places.append((at[name], (at["y"] * big_x + at["x"], at["z"] * 2 + at["c"])))
            self.lines[name] = places
        self.band, self.img = band, img
        self.lines["band"], self.lines["img"] = [], []
        for d in range(1, 2 * big_z):
            other = lax.rem(band + d, 2 * big_z)
            self.lines["band"].append((other, (img, other)))
        for d in range(1, big_y * big_x):
            other = lax.rem(img + d, big_y * big_x)
            self.lines["img"].append((other, (other, band)))
        across, along = lax.rem(self.x + 1, big_x), lax.rem(self.y + 1, big_y)
        one = self.c
        self.near = (jnp.where(one == 0, self.y, along), jnp.where(one == 0, across, self.x))
        self.next = (jnp.where(one == 0, along, self.y), jnp.where(one == 0, self.x, across))
        self.far = (along, across)
        self.near_device = (self.near[0] * big_x + self.near[1], band)
        self.next_device = (self.next[0] * big_x + self.next[1], band)
        self.lines["image"] = []
        for d in range(1, self.images):
            other = lax.rem(image + d, self.images)
            self.lines["image"].append((other, (img, other * share + self.part)))
        self.lines["share"] = []
        for d in range(1, share):
            other = lax.rem(self.part + d, share)
            self.lines["share"].append((other, (img, image * share + other)))

    def line(self, name):
        return self.lines[name]

    def greet(self, kinds):
        barrier = pltpu.get_barrier_semaphore()
        count = 0
        for kind in kinds:
            for _, target in self.lines[kind]:
                pl.semaphore_signal(barrier, inc=1, device_id=target, device_id_type=MESH)
            count += len(self.lines[kind])
        pl.semaphore_wait(barrier, count)

    def copy(self, source, target_ref, target):
        made = self.plan(source, target_ref, target)
        made.start()
        return made

    def plan(self, source, target_ref, target):
        self.used += 1
        return Move(source, target_ref, self.send, self.recv, self.used - 1, target)

    def local_copy(self, source, target_ref):
        self.used_local += 1
        made = Move(source, target_ref, None, self.local, self.used_local - 1, None)
        made.start()
        return made


class Part:
    def __init__(self, ref, index=None):
        self.ref, self.index = ref, index

    def __getitem__(self, index):
        return Part(self.ref, index)

    def view(self):
        return self.ref if self.index is None else self.ref.at[self.index]


class Move:
    def __init__(self, source, target_ref, send, recv, at, target):
        self.source, self.target_ref = source, target_ref
        self.send, self.recv, self.at, self.target = send, recv, at, target

    def build(self):
        if self.target is None:
            return pltpu.make_async_copy(self.source.view(), self.target_ref.view(), self.recv.at[self.at])
        return pltpu.make_async_remote_copy(
            src_ref=self.source.view(),
            dst_ref=self.target_ref.view(),
            send_sem=self.send.at[self.at],
            recv_sem=self.recv.at[self.at],
            device_id=self.target,
            device_id_type=MESH,
        )

    def start(self):
        self.build().start()

    def wait(self):
        self.build().wait()

    def wait_recv(self):
        self.build().wait_recv()

    def wait_send(self):
        self.build().wait_send()


def drive(tasks):
    waiting = list(tasks)
    turn = 0
    while waiting:
        left = []
        for start, task in waiting:
            if start <= turn:
                try:
                    next(task)
                except StopIteration:
                    continue
            left.append((start, task))
        waiting = left
        turn += 1


def exchange_images(net, source, target, idle=1):
    moves = [net.copy(Part(source)[other], Part(target)[net.image], dev) for other, dev in net.line("image")]
    own = net.local_copy(Part(source)[net.image], Part(target)[net.image])
    for _ in range(idle):
        yield
    for move in moves:
        move.wait_recv()
    own.wait()
    for move in moves:
        move.wait_send()


def gather(net, source, target, columns):
    cols = pl.ds(*columns)
    y, x, c = net.y, net.x, net.c
    (_, twin), = net.line("c")

    def blocks(place):
        return Part(target)[place[0], place[1], :, c, :, cols]

    here = Part(target)[y, x, net.z, c, :, cols]
    own = net.local_copy(Part(source)[:, cols], here)
    from_z = [net.copy(Part(source)[:, cols], here, dev) for _, dev in net.line("z")]
    yield
    own.wait()
    for move in from_z:
        move.wait_recv()
    mine = blocks((y, x))
    first = net.copy(mine, mine, net.near_device)
    second = net.copy(mine, mine, net.next_device)
    twins = [net.copy(mine, mine, twin)]
    yield
    first.wait_recv()
    near = blocks(net.near)
    third = net.copy(near, near, net.next_device)
    twins.append(net.copy(near, near, twin))
    yield
    second.wait_recv()
    third.wait_recv()
    for place in (net.next, net.far):
        twins.append(net.copy(blocks(place), blocks(place), twin))
    yield
    for move in twins:
        move.wait_recv()
    for move in from_z + [first, second, third] + twins:
        move.wait_send()


def gather_copies(dims):
    return dims[2] - 1 + 3 + 4


def scatter_copies(dims):
    return dims[0] + dims[1] + dims[2] - 3 + 1


def add_up(own, others):
    if len(others) == 1:
        return own + others[0]
    total = own.astype(F32)
    for other in others:
        total = total + other.astype(F32)
    return total.astype(own.dtype)


def scatter(net, grad, held, from_core, from_first, from_second, from_z, out, squares, columns, order, offset=0):
    big_y, big_x, big_z, _ = net.dims
    cols = pl.ds(*columns)
    y, x, z, c = net.y, net.x, net.z, net.c
    sent = []
    (_, twin), = net.line("c")
    moves = [net.copy(Part(grad)[:, :, :, net.twin, :, cols], Part(from_core), twin)]
    sent += moves
    own = net.local_copy(Part(grad)[:, :, :, c, :, cols], Part(held))
    yield
    own.wait()
    moves[0].wait_recv()

    def first_add(at, _):
        a, b, d = at // (big_x * big_z), (at // big_z) % big_x, at % big_z
        held[a, b, d] = held[a, b, d] + from_core[a, b, d]
        return 0

    lax.fori_loop(0, big_y * big_x * big_z, first_add, 0)
    moves = []
    for slot, (other, dev) in enumerate(net.line(order[0])):
        part = Part(held)[:, other] if order[0] == "x" else Part(held)[other]
        moves.append(net.copy(part, Part(from_first)[slot], dev))
    sent += moves
    yield
    for move in moves:
        move.wait_recv()
    left = big_y if order[0] == "x" else big_x

    def second_add(at, _):
        a, d = at // big_z, at % big_z
        place = (a, x, d) if order[0] == "x" else (y, a, d)
        held[place] = add_up(held[place], [from_first[slot, a, d] for slot in range(len(moves))])
        return 0

    lax.fori_loop(0, left * big_z, second_add, 0)
    moves = []
    for slot, (other, dev) in enumerate(net.line(order[1])):
        part = Part(held)[other, x] if order[1] == "y" else Part(held)[y, other]
        moves.append(net.copy(part, Part(from_second)[slot], dev))
    sent += moves
    yield
    for move in moves:
        move.wait_recv()

    def third_add(d, _):
        held[y, x, d] = add_up(held[y, x, d], [from_second[slot, d] for slot in range(len(moves))])
        return 0

    lax.fori_loop(0, big_z, third_add, 0)
    moves = []
    for slot, (other, dev) in enumerate(net.line("z")):
        moves.append(net.copy(Part(held)[y, x, other], Part(from_z)[slot], dev))
    sent += moves
    yield
    for move in moves:
        move.wait_recv()
    total = held[y, x, z].astype(F32)
    for slot in range(len(moves)):
        total = total + from_z[slot].astype(F32)
    out[:, offset + columns[0] : offset + columns[0] + columns[1]] = total
    tile = squares[...]
    for a in range(total.shape[0] // 8):
        for b in range(columns[1] // 128):
            piece = total[8 * a : 8 * a + 8, 128 * b : 128 * b + 128]
            tile = tile + piece * piece
    squares[...] = tile
    for move in sent:
        move.wait_send()


def scatter_scratch(dims, rows, columns, order):
    big_y, big_x, big_z, _ = dims
    width = columns[1]
    ahead, left = (big_x, big_y) if order[0] == "x" else (big_y, big_x)
    return [
        pltpu.VMEM((big_y, big_x, big_z, rows, width), BF),
        pltpu.VMEM((big_y, big_x, big_z, rows, width), BF),
        pltpu.VMEM((ahead - 1, left, big_z, rows, width), BF),
        pltpu.VMEM((left - 1, big_z, rows, width), BF),
        pltpu.VMEM((big_z - 1, rows, width), BF),
    ]


def sum_tiles(net, tile, slots):
    first = 0
    for name, me in (("band", net.band), ("img", net.img)):
        places = net.line(name)
        slots[first + me] = tile[...]
        moves = [net.copy(Part(tile), Part(slots)[first + me], dev) for _, dev in places]
        for move in moves:
            move.wait_recv()
        for move in moves:
            move.wait_send()
        total = slots[first]
        for d in range(1, len(places) + 1):
            total = total + slots[first + d]
        tile[...] = total
        first += len(places) + 1


def sems(count):
    return pltpu.SemaphoreType.DMA((max(count, 1),))


def halves(width):
    units = width // 128
    low = (units + 1) // 2 * 128
    if low == width:
        return [((0, width), "xy")]
    return [((0, low), "xy"), ((low, width - low), "yx")]


def pieces(width, shares):
    units, found, start = width // 128, [], 0
    for group in range(len(shares)):
        stop = units * sum(shares[: group + 1]) // sum(shares) * 128
        found.append((start, stop - start))
        start = stop
    return found


def gather_call(dims, name, number, blocks, images=None):
    big_y, big_x, big_z, share = dims
    parts = [[(0, block.shape[1])] for block in blocks]
    copies = sum(len(p) for p in parts) * gather_copies(dims)
    local = sum(len(p) for p in parts)
    n = len(blocks)
    with_images = images is not None
    if with_images:
        copies += images.shape[0] - 1
        local += 1

    def body(*refs):
        ins, rest = refs[: n + with_images], refs[n + with_images :]
        outs, (send, recv, local_sem) = rest[: n + with_images], rest[n + with_images :]
        net = Net(dims, send, recv, local_sem)
        net.greet("zxyc" if not with_images else ["z", "x", "y", "c", "image"])
        tasks = []
        for j in range(n):
            for columns in parts[j]:
                tasks.append((0, gather(net, ins[j], outs[j], columns)))
        if with_images:
            tasks.append((1, exchange_images(net, ins[n], outs[n], 3)))
        drive(tasks)

    args = list(blocks) + ([images] if with_images else [])
    shapes = [jax.ShapeDtypeStruct((big_y, big_x, big_z, 2) + b.shape, b.dtype) for b in blocks]
    if with_images:
        shapes.append(jax.ShapeDtypeStruct(images.shape, images.dtype))
    return pl.pallas_call(
        body,
        out_shape=shapes,
        in_specs=[ANY] * len(args),
        out_specs=[ANY] * len(shapes),
        scratch_shapes=[sems(copies), sems(copies), sems(local)],
        compiler_params=pltpu.CompilerParams(collective_id=number, has_side_effects=True),
        name=name,
    )(*args)


def finale_call(dims, number, tokens, back_project, weight, back_middle, gains, gain_two_grad, squares, images):
    big_y, big_x, big_z, _ = dims
    rows, width = tokens.shape
    block = rows // images
    devices = 2 * big_x * big_y * big_z
    shard = width // devices
    parts = halves(3 * width + 128)
    tile = 256
    band_size, img_size = 2 * big_z, big_x * big_y
    copies = len(parts) * scatter_copies(dims) + images - 1 + band_size + img_size - 2
    local = len(parts) + 5 + 2 * images
    scratch = [sems(copies), sems(copies), sems(local)]
    for columns, order in parts:
        scratch += scatter_scratch(dims, shard, columns, order)
    n_fixed = 3 + 5 * len(parts)
    scratch += [
        pltpu.VMEM((8, 128), F32),
        pltpu.VMEM((band_size + img_size, 8, 128), F32),
        pltpu.VMEM(tokens.shape, BF),
        pltpu.VMEM(back_project.shape, BF),
        pltpu.VMEM(weight.shape, BF),
        pltpu.VMEM(back_middle.shape, F32),
        pltpu.VMEM((images, block, width), BF),
        pltpu.VMEM((width, rows), BF),
        pltpu.VMEM((128, width), F32),
    ]
    scratch += [pltpu.VMEM((big_y, big_x, big_z, 2, shard, columns[1]), BF) for columns, _ in parts]

    def body(*refs):
        x_hbm, b_hbm, w_hbm, m_hbm, g_ref, two_ref, squares_ref = refs[:7]
        sum_ref, moved, total_ref, rest = refs[7], refs[8], refs[9], refs[10:]
        tally, slots, x_all, b_all, w_all, m_all, sent, normed_t, gain_rows = rest[n_fixed : n_fixed + 9]
        grads = rest[n_fixed + 9 :]
        net = Net(dims, *rest[:3])
        order = [other for other, _ in net.line("image")] + [net.image]
        load_w = net.local_copy(Part(w_hbm), Part(w_all))
        loads = []
        for chunk in order:
            at = pl.ds(pl.multiple_of(chunk * block, block), block)
            loads.append([net.local_copy(Part(a)[at, :], Part(b)[at, :]) for a, b in ((b_hbm, b_all), (x_hbm, x_all))])
            if len(loads) == 1:
                load_m = net.local_copy(Part(m_hbm), Part(m_all))
        net.greet(["z", "x", "y", "c", "image", "band", "img"])
        tally[...] = squares_ref[...]
        gain_rows[...] = jnp.zeros_like(gain_rows)
        gain_rows[1:2, :] = two_ref[0:1, :]
        load_w.wait()
        moves = []
        for place, chunk in enumerate(order):
            for load in loads[place]:
                load.wait()
            if place == 0:
                load_m.wait()
            at = pl.ds(pl.multiple_of(chunk * block, block), block)
            gain = g_ref[0:1, :]
            x = x_all[at, :].astype(F32)
            scale = inverse_rms(x)
            normed_t[:, place * block : (place + 1) * block] = jnp.transpose((x * scale * gain).astype(BF))
            into, rows_of_gain = norm_back(mm(b_all[at, :], w_all[:, : 3 * width], 1, 1), x, scale, gain)
            sent[chunk] = (m_all[at, :] + into).astype(BF)
            gain_rows[0:1, :] += jnp.sum(rows_of_gain, 0, keepdims=True)
            if place < images - 1:
                moves.append(net.copy(Part(sent)[chunk], Part(moved)[net.image], net.line("image")[place][1]))
            else:
                own = net.local_copy(Part(sent)[chunk], Part(moved)[net.image])
        tasks = []
        for k, (columns, turn) in enumerate(parts):
            buffers = rest[3 + 5 * k : 8 + 5 * k]
            for low in range(columns[0], min(columns[0] + columns[1], 3 * width), tile):
                total = jnp.zeros((width, tile), F32)
                for place, chunk in enumerate(order):
                    at = pl.ds(pl.multiple_of(chunk * block, block), block)
                    inner = slice(place * block, (place + 1) * block)
                    total = total + mm(normed_t[:, inner], b_all[at, low : low + tile], 1, 0)
                into = slice(low - columns[0], low - columns[0] + tile)
                grads[k][..., into] = total.astype(BF).reshape(grads[k].shape[:5] + (tile,))
            if k == len(parts) - 1:
                turned = jnp.transpose(gain_rows[...]).astype(BF)
                grads[k][..., columns[1] - 128 :] = turned.reshape(grads[k].shape[:5] + (128,))
            task = scatter(net, grads[k], *buffers, sum_ref, tally, (0, columns[1]), turn, columns[0])
            next(task)
            tasks.append((0, task))
        drive(tasks)
        sum_tiles(net, tally, slots)
        total_ref[...] = jnp.broadcast_to(jnp.sum(tally[...], keepdims=True), (8, 128))
        for move in moves:
            move.wait_recv()
        own.wait()
        for move in moves:
            move.wait_send()

    vmem = pl.BlockSpec(memory_space=pltpu.VMEM)
    shapes = [
        jax.ShapeDtypeStruct((shard, 3 * width + 128), F32),
        jax.ShapeDtypeStruct((images, block, width), BF),
        jax.ShapeDtypeStruct((8, 128), F32),
    ]
    return pl.pallas_call(
        body,
        out_shape=shapes,
        in_specs=[ANY] * 4 + [vmem] * 3,
        out_specs=[vmem, ANY, vmem],
        scratch_shapes=scratch,
        compiler_params=pltpu.CompilerParams(
            collective_id=number, has_side_effects=True, vmem_limit_bytes=61 * MIB
        ),
        name="finale",
    )(tokens, back_project, weight, back_middle, gains, gain_two_grad, squares)


def whole(shape):
    return pl.BlockSpec(shape, lambda i: (0,) * len(shape))


def kept(shape):
    return pl.BlockSpec(shape, lambda i: (0,) * len(shape), pipeline_mode=pl.Buffered(1))


def inverse_rms(value):
    return lax.rsqrt(jnp.mean(value * value, -1, keepdims=True) + EPS)


def mm(a, b, ca, cb):
    return lax.dot_general(a, b, (((ca,), (cb,)), ((), ())), preferred_element_type=F32)


def at_turn(turn, events):
    def visit(whens):
        if len(whens) == 1:

            @pl.when(turn == whens[0])
            def _():
                for task in events[whens[0]]:
                    next(task, None)

        elif whens:
            middle = len(whens) // 2

            @pl.when(turn < whens[middle])
            def _():
                visit(whens[:middle])

            @pl.when(turn >= whens[middle])
            def _():
                visit(whens[middle:])

    visit(sorted(events))


def schedule(tasks, turns, last):
    events, tail = {}, []
    for task, when in zip(tasks, turns):
        for turn in when:
            if turn < last:
                events.setdefault(turn, []).append(task)
            else:
                tail.append(task)
    return events, tail


def lanes_of(h):
    lane = lax.broadcasted_iota(jnp.int32, (1, PAIR), 1) < HEAD_DIM
    return lane if h == 0 else ~lane


def attend(dims, number, tokens, weight, bias, block, weights, chunks):
    big_y, big_x, big_z, share = dims
    rows, width = tokens.shape
    pairs = width // PAIR
    others = share - 1
    blocks = 4
    n = len(weights)
    last = LEAD + 4 * pairs
    parts = [
        (j, columns, GATHER_TURNS[group])
        for j, w in enumerate(weights)
        for group, columns in enumerate(pieces(w.shape[1], GATHER_SHARES))
    ]
    copies = len(parts) * gather_copies(dims) + others * 2 * pairs + chunks.shape[0] - 1

    def body(*refs):
        x_ref, w_ref, bias_ref, chunks_in = refs[:4]
        blocks_in, refs = refs[4 : 4 + n], refs[4 + n :]
        o_ref, l_ref, kv_out, chunks_out, project_ref, gains_ref, refs = refs[:6] + (refs[6:],)
        gathered, (kv_held, send, recv, local) = refs[:n], refs[n:]
        h = pl.program_id(0)
        net = Net(dims, send, recv, local)

        def move_keys(j):
            moves = []
            for slot, (_, target) in enumerate(net.line("share")):
                source = Part(project_ref)[:, pl.ds(width + PAIR * j, PAIR)]
                moves.append(net.plan(source, Part(kv_held)[others - 1 - slot, j], target))
            return moves

        key_moves = [move_keys(j) for j in range(2 * pairs)]
        keep = Move(Part(kv_held), Part(kv_out), None, local, len(parts) + 1, None)
        tasks = [gather(net, blocks_in[j], gathered[j], columns) for j, columns, _ in parts]
        tasks.append(exchange_images(net, chunks_in, chunks_out))
        turns = [turn for _, _, turn in parts] + [CHUNK_TURNS]
        events, tail = schedule(tasks, turns, last)

        @pl.when(h == 0)
        def _():
            net.greet(["z", "x", "y", "c", "image"] + (["share"] if share > 2 else []))
            gains_ref[...] = jnp.transpose(w_ref[:, 3 * width :].astype(F32))[:8]

        @pl.when(h == 0)
        def _():
            def row_step(i, _):
                at_turn(i, {t: e for t, e in events.items() if t < LEAD})
                at = pl.ds(pl.multiple_of(i * block, block), block)
                x = x_ref[at, :].astype(F32)
                normed = (x * inverse_rms(x) * gains_ref[0:1, :]).astype(BF)
                project_ref[at, :] = mm(normed, w_ref[:, : 3 * width], 1, 0).astype(BF)
                return 0

            lax.fori_loop(0, blocks, row_step, 0)
            for j in range(pairs):
                for move in key_moves[j] + key_moves[j + pairs]:
                    move.start()

        for j in range(pairs):

            @pl.when(h == j)
            def _(j=j):
                for move in key_moves[j] + key_moves[j + pairs]:
                    move.wait_recv()
                if j == pairs - 1:
                    keep.start()

        def own(first):
            return pl.ds(pl.multiple_of((h + first) * PAIR, PAIR), PAIR)

        def step(i, _):
            at_turn(LEAD + h * 4 + i, {t: e for t, e in events.items() if t >= LEAD})
            at = pl.ds(pl.multiple_of(i * block, block), block)
            k = jnp.concatenate([project_ref[:, own(pairs)]] + [kv_held[s, h] for s in range(others)], 0)
            v = jnp.concatenate(
                [project_ref[:, own(2 * pairs)]] + [kv_held[s, h + pairs] for s in range(others)], 0
            )
            q = project_ref[at, own(0)] * jnp.asarray(SCALE, BF)
            mixed, logs = [], []
            for half in range(2):
                scores = mm(jnp.where(lanes_of(half), q, jnp.zeros_like(q)), k, 1, 1) + bias_ref[...]
                highest = jnp.max(scores, -1, keepdims=True)
                powers = jnp.exp(scores - highest)
                total = jnp.sum(powers, -1, keepdims=True)
                mixed.append(mm(powers.astype(BF), v, 1, 0) / total)
                logs.append(highest + jnp.log(total))
            o_ref[at, :] = jnp.where(lanes_of(0), mixed[0], mixed[1]).astype(BF)
            l_ref[at, :] = jnp.where(lanes_of(0), logs[0], logs[1])
            return 0

        lax.fori_loop(0, blocks, step, 0)

        @pl.when(h == pairs - 1)
        def _():
            for task in tail:
                next(task, None)
            for moves in key_moves:
                for move in moves:
                    move.wait_send()
            keep.wait()

    column = lambda first: pl.BlockSpec((rows, PAIR), lambda h: (0, h + first))
    keys = rows * share
    shapes = [
        jax.ShapeDtypeStruct((rows, width), BF),
        jax.ShapeDtypeStruct((rows, width), F32),
        jax.ShapeDtypeStruct((others, 2 * pairs, rows, PAIR), BF),
        jax.ShapeDtypeStruct(chunks.shape, chunks.dtype),
        jax.ShapeDtypeStruct((rows, 3 * width), BF),
        jax.ShapeDtypeStruct((8, width), F32),
    ] + [jax.ShapeDtypeStruct((big_y, big_x, big_z, 2) + w.shape, w.dtype) for w in weights]
    return pl.pallas_call(
        body,
        grid=(pairs,),
        in_specs=[kept(tokens.shape), kept(weight.shape), kept((1, keys))] + [ANY] * (1 + n),
        out_specs=[column(0), column(0), ANY, ANY, kept((rows, 3 * width)), kept((8, width))] + [ANY] * n,
        out_shape=shapes,
        scratch_shapes=[
            pltpu.VMEM((others, 2 * pairs, rows, PAIR), BF),
            sems(copies),
            sems(copies),
            sems(len(parts) + 2),
        ],
        compiler_params=pltpu.CompilerParams(
            collective_id=number, has_side_effects=True, vmem_limit_bytes=60 * MIB
        ),
        cost_estimate=pl.CostEstimate(
            flops=16 * rows * keys * width, bytes_accessed=8 * keys * width, transcendentals=rows * keys * HEADS
        ),
        name="attend",
    )(tokens, weight, bias, chunks, *weights)


LEAD = 4
GATHER_SHARES = (1, 2, 2, 2, 2, 1)
GATHER_TURNS = (
    (0, 3, 6, 10, 12),
    (0, 5, 10, 14, 18),
    (1, 8, 14, 19, 22),
    (2, 12, 19, 23, 26),
    (3, 15, 22, 27, 28),
    (5, 18, 25, 28, 28),
)
CHUNK_TURNS = (12, 28)
SCATTER_TURNS = (
    ((2, 5, 13, 20, 24),),
    ((0, 2, 8, 15, 21), (0, 3, 10, 17, 23)),
    ((1, 4, 12, 19, 24),),
)
RESULT_TURNS = (0, 24)


def attend_back(dims, number, project, kv, bias, mixed, logs, back, block, grads, chunks):
    big_y, big_x, big_z, share = dims
    rows, width = mixed.shape
    pairs = width // PAIR
    others = share - 1
    blocks = 4
    keys = rows * share
    n = len(grads)
    parts = [
        (j, (low + first, wide), order, SCATTER_TURNS[j][group])
        for j, g in enumerate(grads)
        for group, (first, width_of) in enumerate(pieces(g.shape[5], (1,) * len(SCATTER_TURNS[j])))
        for (low, wide), order in halves(width_of)
    ]
    copies = len(parts) * scatter_copies(dims) + others * 2 * pairs + chunks.shape[0] - 1

    def body(*refs):
        q_ref, k_ref, v_ref, k_other, v_other, bias_ref, mixed_ref, logs_ref, back_ref = refs[:9]
        grads_in, chunks_in, refs = refs[9 : 9 + n], refs[9 + n], refs[10 + n :]
        out_ref, sums, squares, chunks_out, refs = refs[0], refs[1 : 1 + n], refs[1 + n], refs[2 + n], refs[3 + n :]
        dk_sums, dv_sums, parted, arrived, bias_column = refs[:5]
        send, recv, local = refs[5:8]
        buffers = refs[8:]
        h = pl.program_id(0)
        net = Net(dims, send, recv, local)

        def move_keys(j):
            moves = []
            for slot, (_, target) in enumerate(net.line("share")):
                moves.append(net.plan(Part(parted)[slot, j], Part(arrived)[others - 1 - slot, j], target))
            return moves

        key_moves = [move_keys(j) for j in range(2 * pairs)]
        tasks = [
            scatter(net, grads_in[j], *buffers[5 * k : 5 * k + 5], sums[j], squares, columns, order)
            for k, (j, columns, order, _) in enumerate(parts)
        ]
        tasks.append(exchange_images(net, chunks_in, chunks_out))
        turns = [turn for _, _, _, turn in parts] + [RESULT_TURNS]
        events, tail = schedule(tasks, turns, 4 * pairs)

        @pl.when(h == 0)
        def _():
            net.greet(["z", "x", "y", "c", "image"] + (["share"] if share > 2 else []))
            squares[...] = jnp.zeros_like(squares)
            bias_column[...] = jnp.transpose(jnp.broadcast_to(bias_ref[...], (PAIR, keys)))

        turn = lax.rem(h, 2)
        dk_sums[turn] = jnp.zeros((keys, PAIR), F32)
        dv_sums[turn] = jnp.zeros((keys, PAIR), F32)

        def step(i, _):
            at_turn(h * 4 + i, events)
            at = pl.ds(pl.multiple_of(i * block, block), block)
            k = jnp.concatenate([k_ref[...]] + [k_other[s, 0] for s in range(others)], 0)
            v = jnp.concatenate([v_ref[...]] + [v_other[s, 0] for s in range(others)], 0)
            q, do = q_ref[at, :] * jnp.asarray(SCALE, BF), back_ref[at, :]
            lse = jnp.transpose(logs_ref[at, :])
            products = jnp.transpose(do.astype(F32) * mixed_ref[at, :].astype(F32))
            dqs, dks, dvs = [], [], []
            mask = jnp.concatenate([bias_column[...]] * (block // PAIR), 1)
            for half in range(2):
                low, high = half * HEAD_DIM, (half + 1) * HEAD_DIM
                q_h = jnp.where(lanes_of(half), q, jnp.zeros_like(q))
                do_h = jnp.where(lanes_of(half), do, jnp.zeros_like(do))
                row_dots = jnp.sum(products[low:high, :], 0, keepdims=True)
                chances = jnp.exp(mm(k, q_h, 1, 1) + mask - lse[low : low + 1, :])
                slopes = mm(v, do_h, 1, 1)
                scores = (chances * (slopes - row_dots)).astype(BF)
                dqs.append(mm(scores, k, 0, 0))
                dks.append(mm(scores, q_h, 1, 0))
                dvs.append(mm(chances.astype(BF), do_h, 1, 0))
            dq = (jnp.where(lanes_of(0), dqs[0], dqs[1]) * SCALE).astype(BF)
            out_ref[at, pl.ds(pl.multiple_of(h * PAIR, PAIR), PAIR)] = dq
            dk_sums[turn] += dks[0] + dks[1]
            dv_sums[turn] += dvs[0] + dvs[1]
            return 0

        lax.fori_loop(0, blocks, step, 0)

        def finish(j):
            for move in key_moves[j] + key_moves[j + pairs]:
                move.wait_recv()
            for kept, sums_of in ((j, dk_sums), (j + pairs, dv_sums)):
                value = sums_of[j % 2, 0:rows, :]
                for slot in range(others):
                    value = value + arrived[slot, kept].astype(F32)
                out_ref[:, width + PAIR * kept : width + PAIR * (kept + 1)] = value.astype(BF)

        for j in range(pairs):

            @pl.when(h == j)
            def _(j=j):
                if j > 0:
                    finish(j - 1)
                for slot in range(others):
                    away = slice(rows * (slot + 1), rows * (slot + 2))
                    parted[slot, j] = dk_sums[j % 2, away, :].astype(BF)
                    parted[slot, j + pairs] = dv_sums[j % 2, away, :].astype(BF)
                for move in key_moves[j] + key_moves[j + pairs]:
                    move.start()
                if j == pairs - 1:
                    for task in tail:
                        next(task, None)
                    finish(j)
                    for moves in key_moves:
                        for move in moves:
                            move.wait_send()

    column = lambda first: pl.BlockSpec((rows, PAIR), lambda h: (0, h + first))
    other = lambda first: pl.BlockSpec((others, 1, rows, PAIR), lambda h: (0, h + first, 0, 0))
    whole = lambda shape: pl.BlockSpec(shape, lambda h: (0,) * len(shape))
    shard = grads[0].shape[4] if n else 0
    shapes = (
        [jax.ShapeDtypeStruct((rows, 3 * width), BF)]
        + [jax.ShapeDtypeStruct((shard, g.shape[5]), F32) for g in grads]
        + [jax.ShapeDtypeStruct((8, 128), F32)]
    )
    moved = jax.ShapeDtypeStruct(chunks.shape, chunks.dtype)
    scratch = [
        pltpu.VMEM((2, keys, PAIR), F32),
        pltpu.VMEM((2, keys, PAIR), F32),
        pltpu.VMEM((others, 2 * pairs, rows, PAIR), BF),
        pltpu.VMEM((others, 2 * pairs, rows, PAIR), BF),
        pltpu.VMEM((keys, PAIR), F32),
        sems(copies),
        sems(copies),
        sems(len(parts) + 1),
    ]
    for _, columns, order, _ in parts:
        scratch += scatter_scratch(dims, shard, columns, order)
    return pl.pallas_call(
        body,
        grid=(pairs,),
        in_specs=[
            column(0),
            column(pairs),
            column(2 * pairs),
            other(0),
            other(pairs),
            whole((1, keys)),
            column(0),
            column(0),
            column(0),
        ]
        + [ANY] * (n + 1),
        out_specs=[whole(s.shape) for s in shapes] + [ANY],
        out_shape=shapes + [moved],
        scratch_shapes=scratch,
        compiler_params=pltpu.CompilerParams(
            collective_id=number, has_side_effects=True, vmem_limit_bytes=60 * MIB
        ),
        cost_estimate=pl.CostEstimate(
            flops=40 * rows * keys * width, bytes_accessed=16 * keys * width, transcendentals=rows * keys * HEADS
        ),
        name="attend_back",
    )(project, project, project, kv, kv, bias, mixed, logs, back, *grads, chunks)


def norm_back(back, value, scale, gain):
    scaled = back * gain
    inner = jnp.mean(scaled * value, -1, keepdims=True)
    return scale * scaled - value * (scale * scale * scale * inner), back * (value * scale)


GELU_A = 0.7978845608028654
GELU_B = 0.044715


def mlp_call(tokens, attended, cotangent, keep, weights, gains, block):
    rows, width = tokens.shape
    hidden_units = (weights.shape[1] - width) // 3
    steps = rows // block
    tile = 1024
    in_tiles, down_tiles = 2 * hidden_units // tile, hidden_units // tile
    part = 512

    def body(
        x_ref, a_ref, c_ref, keep_ref, w_ref, g_ref,
        result_ref, middle_ref, back_ref, gain_ref, g_out_ref, g_in_ref, g_down_ref,
        normed_t, low_t, branch_t, mixed, hidden, back_gu,
    ):
        i = pl.program_id(0)
        wo_ref = w_ref.at[:, :width]
        wi_ref = w_ref.at[:, width : width + 2 * hidden_units]
        wd_ref = w_ref.at[:, width + 2 * hidden_units :]

        @pl.when(i == 0)
        def _():
            gain_ref[...] = jnp.zeros_like(gain_ref)

        @pl.when(i < steps)
        def _():
            at = pl.ds(pl.multiple_of(i * block, block), block)
            gain = g_ref[1:2, :]
            a = a_ref[...]
            mixed[at, :] = a
            middle = x_ref[...].astype(F32) + mm(a, wo_ref[...], 1, 1)
            scale = inverse_rms(middle)
            normed = (middle * scale * gain).astype(BF)
            normed_t[:, at] = jnp.transpose(normed)
            back_result = keep_ref[...] * c_ref[...].astype(F32)
            low = back_result.astype(BF)
            low_t[:, at] = jnp.transpose(low)
            result, back = middle, jnp.zeros_like(middle)
            for p in range(hidden_units // part):
                one = slice(p * part, (p + 1) * part)
                two = slice(hidden_units + p * part, hidden_units + (p + 1) * part)
                gate = mm(normed, wi_ref[:, one], 1, 0)
                up = mm(normed, wi_ref[:, two], 1, 0)
                back_hidden = mm(low, wd_ref[:, one], 1, 0)
                square = gate * gate
                bend = jnp.tanh(GELU_A * (gate + GELU_B * (gate * square)))
                half = 0.5 + 0.5 * bend
                curve = gate * half
                slope = half + (0.5 * GELU_A) * gate * (1.0 - bend * bend) * (1.0 + (3.0 * GELU_B) * square)
                hid = (curve * up).astype(BF)
                back_gate = (back_hidden * up * slope).astype(BF)
                back_up = (back_hidden * curve).astype(BF)
                hidden[at, one] = hid
                back_gu[at, one] = back_gate
                back_gu[at, two] = back_up
                result = result + mm(hid, wd_ref[:, one], 1, 1)
                back = back + mm(back_gate, wi_ref[:, one], 1, 1) + mm(back_up, wi_ref[:, two], 1, 1)
            result_ref[...] = (keep_ref[...] * result).astype(BF)
            into, gain_rows = norm_back(back, middle, scale, gain)
            gain_ref[0:1, :] += jnp.sum(gain_rows, 0, keepdims=True)
            back_middle = back_result + into
            middle_ref[...] = back_middle
            branch = back_middle.astype(BF)
            branch_t[:, at] = jnp.transpose(branch)
            back_ref[...] = mm(branch, wo_ref[...], 1, 0).astype(BF)

        @pl.when(i == steps)
        def _():
            g_out_ref[...] = mm(branch_t[...], mixed[...], 1, 0).astype(BF)

        for t in range(in_tiles):

            @pl.when(i == steps + 1 + t)
            def _(t=t):
                g_in_ref[...] = mm(normed_t[...], back_gu[:, t * tile : (t + 1) * tile], 1, 0).astype(BF)

        for t in range(down_tiles):

            @pl.when(i == steps + 1 + in_tiles + t)
            def _(t=t):
                g_down_ref[...] = mm(low_t[...], hidden[:, t * tile : (t + 1) * tile], 1, 0).astype(BF)

    row = lambda last: pl.BlockSpec((block, last), lambda i: (jnp.minimum(i, steps - 1), 0))
    return pl.pallas_call(
        body,
        grid=(steps + 1 + in_tiles + down_tiles,),
        in_specs=[
            row(width),
            row(width),
            row(width),
            row(1),
            kept(weights.shape),
            kept(gains.shape),
        ],
        out_specs=[
            row(width),
            row(width),
            row(width),
            whole((8, width)),
            whole((width, width)),
            pl.BlockSpec((width, tile), lambda i: (0, jnp.clip(i - steps - 1, 0, in_tiles - 1))),
            pl.BlockSpec((width, tile), lambda i: (0, jnp.clip(i - steps - 1 - in_tiles, 0, down_tiles - 1))),
        ],
        out_shape=[
            jax.ShapeDtypeStruct((rows, width), BF),
            jax.ShapeDtypeStruct((rows, width), F32),
            jax.ShapeDtypeStruct((rows, width), BF),
            jax.ShapeDtypeStruct((8, width), F32),
            jax.ShapeDtypeStruct((width, width), BF),
            jax.ShapeDtypeStruct((width, 2 * hidden_units), BF),
            jax.ShapeDtypeStruct((width, hidden_units), BF),
        ],
        scratch_shapes=[
            pltpu.VMEM((width, rows), BF),
            pltpu.VMEM((width, rows), BF),
            pltpu.VMEM((width, rows), BF),
            pltpu.VMEM((rows, width), BF),
            pltpu.VMEM((rows, hidden_units), BF),
            pltpu.VMEM((rows, 2 * hidden_units), BF),
        ],
        compiler_params=pltpu.CompilerParams(vmem_limit_bytes=61 * MIB),
        cost_estimate=pl.CostEstimate(
            flops=6 * rows * width * (width + 3 * hidden_units),
            bytes_accessed=8 * width * (width + 3 * hidden_units),
            transcendentals=rows * hidden_units,
        ),
        name="mlp",
    )(tokens, attended, cotangent, keep, weights, gains)


def finish_call(tokens, back_project, weight, back_middle, gains, gain_two_grad, block):
    rows, width = tokens.shape
    steps = rows // block
    tiles, tile = 3, width

    def body(x_ref, b_ref, w_ref, m_ref, g_ref, two_ref, out_ref, grad_ref, gain_ref, normed_t, held, gain_rows):
        i = pl.program_id(0)

        @pl.when(i == 0)
        def _():
            gain_rows[...] = jnp.zeros_like(gain_rows)
            gain_rows[1:2, :] = two_ref[0:1, :]

        @pl.when(i < steps)
        def _():
            at = pl.ds(pl.multiple_of(i * block, block), block)
            gain = g_ref[0:1, :]
            x = x_ref[...].astype(F32)
            scale = inverse_rms(x)
            normed_t[:, at] = jnp.transpose((x * scale * gain).astype(BF))
            back = b_ref[...]
            held[at, :] = back
            into, rows_of_gain = norm_back(mm(back, w_ref[:, : 3 * width], 1, 1), x, scale, gain)
            out_ref[...] = (m_ref[...] + into).astype(BF)
            gain_rows[0:1, :] += jnp.sum(rows_of_gain, 0, keepdims=True)

        for t in range(tiles):

            @pl.when(i == steps + t)
            def _(t=t):
                grad_ref[...] = mm(normed_t[...], held[:, t * tile : (t + 1) * tile], 1, 0).astype(BF)

        @pl.when(i == steps)
        def _():
            gain_ref[...] = jnp.transpose(gain_rows[...]).astype(BF)

    row = lambda last: pl.BlockSpec((block, last), lambda i: (jnp.minimum(i, steps - 1), 0))
    return pl.pallas_call(
        body,
        grid=(steps + tiles,),
        in_specs=[row(width), row(3 * width), kept(weight.shape), row(width), kept(gains.shape), kept((8, width))],
        out_specs=[
            row(width),
            pl.BlockSpec((width, tile), lambda i: (0, jnp.clip(i - steps, 0, tiles - 1))),
            whole((width, 128)),
        ],
        out_shape=[
            jax.ShapeDtypeStruct((rows, width), BF),
            jax.ShapeDtypeStruct((width, 3 * width), BF),
            jax.ShapeDtypeStruct((width, 128), BF),
        ],
        scratch_shapes=[
            pltpu.VMEM((width, rows), BF),
            pltpu.VMEM((rows, 3 * width), BF),
            pltpu.VMEM((128, width), F32),
        ],
        compiler_params=pltpu.CompilerParams(vmem_limit_bytes=48 * MIB),
        cost_estimate=pl.CostEstimate(
            flops=12 * rows * width * width, bytes_accessed=28 * width * width, transcendentals=rows
        ),
        name="finish",
    )(tokens, back_project, weight, back_middle, gains, gain_two_grad)


def adam_step(master, grad, first, second, factor, rate, decay):
    clipped = factor * grad
    first_new = BETA_ONE * first + (1.0 - BETA_ONE) * clipped
    second_new = BETA_TWO * second + (1.0 - BETA_TWO) * clipped * clipped
    corrected = first_new / (1.0 - BETA_ONE**STEP)
    spread = jnp.sqrt(second_new / (1.0 - BETA_TWO**STEP)) + ADAM_EPS
    master_new = master - rate * (corrected / spread + decay * master)
    return (master_new, first_new, second_new)


def adam_call(squares, grads, masters, firsts, seconds):
    shard, width = grads[0].shape[0], grads[0].shape[1] - 128

    def body(*refs):
        squares_ref, refs = refs[0], refs[1:]
        ins, norm_ref, outs = refs[:19], refs[19], refs[20:]
        norm = jnp.sqrt(squares_ref[0:1, :])
        norm_ref[0, 0] = norm[0, 0]
        factor = jnp.minimum(1.0, CLIP / norm[:, 0:1])
        for j in range(5):
            grad = ins[0][:, :width] if j == 0 else ins[0][:, width:] if j == 4 else ins[j][...]
            if j == 4:
                filled = jnp.concatenate([grad, jnp.zeros((128 - shard, 128), F32)], 0)
                grad = jnp.transpose(filled)[:2, :shard]
            made = adam_step(
                ins[4 + j][...], grad, ins[9 + j][...], ins[14 + j][...], factor, RATES[j], DECAYS[j]
            )
            for kind in range(3):
                outs[5 * kind + j][...] = made[kind]
            outs[15 + j][...] = made[0].astype(BF)

    shapes = [jax.ShapeDtypeStruct((1, 1), F32)]
    shapes += [jax.ShapeDtypeStruct(m.shape, F32) for _ in range(3) for m in masters]
    shapes += [jax.ShapeDtypeStruct(m.shape, BF) for m in masters]
    vmem = pl.BlockSpec(memory_space=pltpu.VMEM)
    return pl.pallas_call(
        body,
        out_shape=shapes,
        out_specs=[pl.BlockSpec(memory_space=pltpu.SMEM)] + [vmem] * 20,
        compiler_params=pltpu.CompilerParams(vmem_limit_bytes=60 * MIB),
        name="adam",
    )(squares, *grads, *masters, *firsts, *seconds)


def prepare_call(dims, counts, qkv, out_t, in_up, down_t, gains, rows, band_rows):
    share = dims[3]
    images = rows // band_rows
    shard, width = qkv.shape[0], out_t.shape[1]
    wide = in_up.shape[1]

    def body(counts_ref, qkv_ref, out_ref, in_ref, down_ref, gain_ref, early_ref, late_ref, keep_ref, bias_ref):
        early_ref[:, : 3 * width] = qkv_ref[...].astype(BF)
        filled = jnp.concatenate([gain_ref[...], jnp.zeros((2, 128 - shard), F32)], 1)
        filled = jnp.concatenate([filled, jnp.zeros((126, 128), F32)], 0)
        early_ref[:, 3 * width :] = jnp.transpose(filled)[:shard].astype(BF)
        late_ref[:, :width] = out_ref[...].astype(BF)
        late_ref[:, width : width + wide] = in_ref[...].astype(BF)
        late_ref[:, width + wide :] = down_ref[...].astype(BF)
        band = lax.axis_index("band")
        image, part = band // share, lax.rem(band, share)
        count = counts_ref[image]
        down = lax.broadcasted_iota(jnp.int32, (band_rows, 1), 0)
        along = lax.broadcasted_iota(jnp.int32, (1, band_rows), 1)
        for s in range(images):
            first = (s * share + part) * band_rows
            keep_ref[s * band_rows : (s + 1) * band_rows, :] = jnp.where(down + first < count, 1.0, 0.0)
            for other in range(share):
                first = (s * share + lax.rem(part + other, share)) * band_rows
                at = (other * images + s) * band_rows
                bias_ref[:, at : at + band_rows] = jnp.where(along + first < count, 0.0, NEG)

    vmem = pl.BlockSpec(memory_space=pltpu.VMEM)
    return pl.pallas_call(
        body,
        out_shape=[
            jax.ShapeDtypeStruct((shard, 3 * width + 128), BF),
            jax.ShapeDtypeStruct((shard, width + wide + down_t.shape[1]), BF),
            jax.ShapeDtypeStruct((rows, 1), F32),
            jax.ShapeDtypeStruct((1, share * rows), F32),
        ],
        in_specs=[pl.BlockSpec(memory_space=pltpu.SMEM)] + [vmem] * 5,
        out_specs=[vmem] * 4,
        compiler_params=pltpu.CompilerParams(vmem_limit_bytes=60 * MIB),
        name="prepare",
    )(counts, qkv, out_t, in_up, down_t, gains)


def grid_of(n_img):
    big_y = max(d for d in range(1, n_img + 1) if n_img % d == 0 and d * d <= n_img)
    return big_y, n_img // big_y


def on_device(
    patches,
    cotangent,
    valid_counts,
    qkv_master,
    out_master,
    in_master,
    down_master,
    gain_master,
    qkv_first,
    out_first,
    in_first,
    down_first,
    gain_first,
    qkv_second,
    out_second,
    in_second,
    down_second,
    gain_second,
):
    images, band_rows, width = patches.shape
    n_img, n_band = lax.axis_size("img"), lax.axis_size("band")
    share = n_band // images
    big_y, big_x = grid_of(n_img)
    dims = (big_y, big_x, n_band // 2, share)
    rows = images * band_rows
    shard = qkv_master.shape[0]
    own_comm = shard % 8 == 0 and big_y == big_x == 2
    both = ("img", "band")

    places = [[s * share + r for s in range(images)] for r in range(share)]

    def exchange(chunks):
        return lax.all_to_all(chunks, "band", 0, 0, axis_index_groups=places, tiled=True)

    def blocks_of(grads):
        return [g.reshape(dims[:3] + (2, shard, g.shape[1])) for g in grads]

    early, late, row_keep, bias = prepare_call(
        dims,
        valid_counts,
        qkv_master,
        jnp.transpose(out_master),
        in_master,
        jnp.transpose(down_master),
        gain_master,
        rows,
        band_rows,
    )
    if own_comm:
        w_early, tokens_low = gather_call(dims, "gather", 0, [early], patches)
        w_early = w_early.reshape(width, early.shape[1])
    else:
        w_early = lax.all_gather(early, both, axis=0, tiled=True)
        tokens_low = exchange(patches)
    tokens = tokens_low.reshape(rows, width)
    attended, log_sums, kv, cotangent_low, project, gain_rows, *late_all = attend(
        dims, 1, tokens, w_early, bias, rows // 4, [late] if own_comm else [], cotangent
    )
    if own_comm:
        w_late = late_all[0].reshape(width, late.shape[1])
    else:
        w_late = lax.all_gather(late, both, axis=0, tiled=True)

    result_low, back_middle, back_attended, gain_two_grad, *late_grads = mlp_call(
        tokens,
        attended,
        cotangent_low.reshape(rows, width),
        row_keep,
        w_late,
        gain_rows,
        min(256, rows),
    )
    result_low = result_low.reshape(images, band_rows, width)
    back_project, *late_sums, squares, output = attend_back(
        dims,
        2,
        project,
        kv,
        bias,
        attended,
        log_sums,
        back_attended,
        rows // 4,
        blocks_of(late_grads) if own_comm else [],
        result_low,
    )
    if not own_comm:
        late_sums = [lax.psum_scatter(g.astype(F32), both, scatter_dimension=0, tiled=True) for g in late_grads]
    if own_comm:
        qkv_sum, back_input, total = finale_call(
            dims, 3, tokens, back_project, w_early, back_middle, gain_rows, gain_two_grad, squares, images
        )
    else:
        back_rows, *early_grads = finish_call(
            tokens, back_project, w_early, back_middle, gain_rows, gain_two_grad, min(256, rows)
        )
        grad = jnp.concatenate([g.astype(F32) for g in early_grads], 1)
        qkv_sum = lax.psum_scatter(grad, both, scatter_dimension=0, tiled=True)
        back_input = exchange(back_rows.reshape(images, band_rows, width))
        squares = sum(jnp.sum(g * g) for g in late_sums + [qkv_sum])
        total = lax.psum(jnp.broadcast_to(squares, (8, 128)), both)
    out_sum, in_sum, down_sum = late_sums

    def turned(arrays):
        return [jnp.transpose(a) if j in (1, 3) else a for j, a in enumerate(arrays)]

    norm, *updated = adam_call(
        total,
        [qkv_sum, out_sum, in_sum, down_sum],
        turned([qkv_master, out_master, in_master, down_master, gain_master]),
        turned([qkv_first, out_first, in_first, down_first, gain_first]),
        turned([qkv_second, out_second, in_second, down_second, gain_second]),
    )
    updated = [a for kind in range(4) for a in turned(updated[5 * kind : 5 * kind + 5])]
    return (output, back_input, norm.reshape(())) + tuple(updated)


def solution(mesh):
    rows_split, columns_split = P(("img", "band"), None), P(None, ("img", "band"))
    weights = (rows_split, columns_split, rows_split, columns_split, columns_split)
    tokens = P("img", "band", None)
    return jax.shard_map(
        on_device,
        mesh=mesh,
        in_specs=(tokens, tokens, P("img")) + weights * 3,
        out_specs=(tokens, tokens, P()) + weights * 4,
        check_vma=False,
    )
```

```python
import functools

import jax
import jax.numpy as jnp
from jax import lax
from jax.experimental import pallas as pl
from jax.experimental.pallas import tpu as pltpu
from jax.sharding import PartitionSpec as P

HEADS = 12
HEAD_DIM = 64
PAIR = 2 * HEAD_DIM
STEP = 10
EPS = 1e-06
NEG = -1000000000.0
SCALE = 0.125
CLIP = 1.0
BETA_ONE = 0.9
BETA_TWO = 0.999
ADAM_EPS = 1e-08
RATES = (0.06, 0.5, 0.06, 0.04, 0.5)
DECAYS = (0.1, 0.1, 0.1, 0.1, 0.0)
BF = jnp.bfloat16
F32 = jnp.float32
MESH = pl.DeviceIdType.MESH
ANY = pl.BlockSpec(memory_space=pl.ANY)
MIB = 2**20


class Net:
    def __init__(self, dims, send, recv, local):
        self.dims = dims
        big_y, big_x, big_z, share = dims
        img, band = lax.axis_index("img"), lax.axis_index("band")
        self.y, self.x = img // big_x, img % big_x
        self.z, self.c = band // 2, band % 2
        self.twin = 1 - self.c
        image, self.part = band // share, band % share
        self.image, self.images = image, 2 * big_z // share
        self.send, self.recv, self.local = send, recv, local
        self.used, self.used_local = 0, 0
        self.lines = {}
        for name, size in zip("yxzc", (big_y, big_x, big_z, 2)):
            places = []
            for d in range(1, size):
                at = dict(y=self.y, x=self.x, z=self.z, c=self.c)
                at[name] = lax.rem(at[name] + d, size)
                places.append((at[name], (at["y"] * big_x + at["x"], at["z"] * 2 + at["c"])))
            self.lines[name] = places
        self.band, self.img = band, img
        self.lines["band"], self.lines["img"] = [], []
        for d in range(1, 2 * big_z):
            other = lax.rem(band + d, 2 * big_z)
            self.lines["band"].append((other, (img, other)))
        for d in range(1, big_y * big_x):
            other = lax.rem(img + d, big_y * big_x)
            self.lines["img"].append((other, (other, band)))
        across, along = lax.rem(self.x + 1, big_x), lax.rem(self.y + 1, big_y)
        one = self.c
        self.near = (jnp.where(one == 0, self.y, along), jnp.where(one == 0, across, self.x))
        self.next = (jnp.where(one == 0, along, self.y), jnp.where(one == 0, self.x, across))
        self.far = (along, across)
        self.near_device = (self.near[0] * big_x + self.near[1], band)
        self.next_device = (self.next[0] * big_x + self.next[1], band)
        self.lines["image"] = []
        for d in range(1, self.images):
            other = lax.rem(image + d, self.images)
            self.lines["image"].append((other, (img, other * share + self.part)))
        self.lines["share"] = []
        for d in range(1, share):
            other = lax.rem(self.part + d, share)
            self.lines["share"].append((other, (img, image * share + other)))

    def line(self, name):
        return self.lines[name]

    def greet(self, kinds):
        barrier = pltpu.get_barrier_semaphore()
        count = 0
        for kind in kinds:
            for _, target in self.lines[kind]:
                pl.semaphore_signal(barrier, inc=1, device_id=target, device_id_type=MESH)
            count += len(self.lines[kind])
        pl.semaphore_wait(barrier, count)

    def copy(self, source, target_ref, target):
        made = self.plan(source, target_ref, target)
        made.start()
        return made

    def plan(self, source, target_ref, target):
        self.used += 1
        return Move(source, target_ref, self.send, self.recv, self.used - 1, target)

    def local_copy(self, source, target_ref):
        self.used_local += 1
        made = Move(source, target_ref, None, self.local, self.used_local - 1, None)
        made.start()
        return made


class Part:
    def __init__(self, ref, index=None):
        self.ref, self.index = ref, index

    def __getitem__(self, index):
        return Part(self.ref, index)

    def view(self):
        return self.ref if self.index is None else self.ref.at[self.index]


class Move:
    def __init__(self, source, target_ref, send, recv, at, target):
        self.source, self.target_ref = source, target_ref
        self.send, self.recv, self.at, self.target = send, recv, at, target

    def build(self):
        if self.target is None:
            return pltpu.make_async_copy(self.source.view(), self.target_ref.view(), self.recv.at[self.at])
        return pltpu.make_async_remote_copy(
            src_ref=self.source.view(),
            dst_ref=self.target_ref.view(),
            send_sem=self.send.at[self.at],
            recv_sem=self.recv.at[self.at],
            device_id=self.target,
            device_id_type=MESH,
        )

    def start(self):
        self.build().start()

    def wait(self):
        self.build().wait()

    def wait_recv(self):
        self.build().wait_recv()

    def wait_send(self):
        self.build().wait_send()


def drive(tasks):
    waiting = list(tasks)
    turn = 0
    while waiting:
        left = []
        for start, task in waiting:
            if start <= turn:
                try:
                    next(task)
                except StopIteration:
                    continue
            left.append((start, task))
        waiting = left
        turn += 1


def exchange_images(net, source, target, idle=1):
    moves = [net.copy(Part(source)[other], Part(target)[net.image], dev) for other, dev in net.line("image")]
    own = net.local_copy(Part(source)[net.image], Part(target)[net.image])
    for _ in range(idle):
        yield
    for move in moves:
        move.wait_recv()
    own.wait()
    for move in moves:
        move.wait_send()


def gather(net, source, target, columns):
    cols = pl.ds(*columns)
    y, x, c = net.y, net.x, net.c
    (_, twin), = net.line("c")

    def blocks(place):
        return Part(target)[place[0], place[1], :, c, :, cols]

    here = Part(target)[y, x, net.z, c, :, cols]
    own = net.local_copy(Part(source)[:, cols], here)
    from_z = [net.copy(Part(source)[:, cols], here, dev) for _, dev in net.line("z")]
    yield
    own.wait()
    for move in from_z:
        move.wait_recv()
    mine = blocks((y, x))
    first = net.copy(mine, mine, net.near_device)
    second = net.copy(mine, mine, net.next_device)
    twins = [net.copy(mine, mine, twin)]
    yield
    first.wait_recv()
    near = blocks(net.near)
    third = net.copy(near, near, net.next_device)
    twins.append(net.copy(near, near, twin))
    yield
    second.wait_recv()
    third.wait_recv()
    for place in (net.next, net.far):
        twins.append(net.copy(blocks(place), blocks(place), twin))
    yield
    for move in twins:
        move.wait_recv()
    for move in from_z + [first, second, third] + twins:
        move.wait_send()


def gather_copies(dims):
    return dims[2] - 1 + 3 + 4


def scatter_copies(dims):
    return dims[0] + dims[1] + dims[2] - 3 + 1


def add_up(own, others):
    if len(others) == 1:
        return own + others[0]
    total = own.astype(F32)
    for other in others:
        total = total + other.astype(F32)
    return total.astype(own.dtype)


def scatter(net, grad, held, from_core, from_first, from_second, from_z, out, squares, columns, order, offset=0):
    big_y, big_x, big_z, _ = net.dims
    cols = pl.ds(*columns)
    y, x, z, c = net.y, net.x, net.z, net.c
    sent = []
    (_, twin), = net.line("c")
    moves = [net.copy(Part(grad)[:, :, :, net.twin, :, cols], Part(from_core), twin)]
    sent += moves
    own = net.local_copy(Part(grad)[:, :, :, c, :, cols], Part(held))
    yield
    own.wait()
    moves[0].wait_recv()

    def first_add(at, _):
        a, b, d = at // (big_x * big_z), (at // big_z) % big_x, at % big_z
        held[a, b, d] = held[a, b, d] + from_core[a, b, d]
        return 0

    lax.fori_loop(0, big_y * big_x * big_z, first_add, 0)
    moves = []
    for slot, (other, dev) in enumerate(net.line(order[0])):
        part = Part(held)[:, other] if order[0] == "x" else Part(held)[other]
        moves.append(net.copy(part, Part(from_first)[slot], dev))
    sent += moves
    yield
    for move in moves:
        move.wait_recv()
    left = big_y if order[0] == "x" else big_x

    def second_add(at, _):
        a, d = at // big_z, at % big_z
        place = (a, x, d) if order[0] == "x" else (y, a, d)
        held[place] = add_up(held[place], [from_first[slot, a, d] for slot in range(len(moves))])
        return 0

    lax.fori_loop(0, left * big_z, second_add, 0)
    moves = []
    for slot, (other, dev) in enumerate(net.line(order[1])):
        part = Part(held)[other, x] if order[1] == "y" else Part(held)[y, other]
        moves.append(net.copy(part, Part(from_second)[slot], dev))
    sent += moves
    yield
    for move in moves:
        move.wait_recv()

    def third_add(d, _):
        held[y, x, d] = add_up(held[y, x, d], [from_second[slot, d] for slot in range(len(moves))])
        return 0

    lax.fori_loop(0, big_z, third_add, 0)
    moves = []
    for slot, (other, dev) in enumerate(net.line("z")):
        moves.append(net.copy(Part(held)[y, x, other], Part(from_z)[slot], dev))
    sent += moves
    yield
    for move in moves:
        move.wait_recv()
    total = held[y, x, z].astype(F32)
    for slot in range(len(moves)):
        total = total + from_z[slot].astype(F32)
    out[:, offset + columns[0] : offset + columns[0] + columns[1]] = total
    tile = squares[...]
    for a in range(total.shape[0] // 8):
        for b in range(columns[1] // 128):
            piece = total[8 * a : 8 * a + 8, 128 * b : 128 * b + 128]
            tile = tile + piece * piece
    squares[...] = tile
    for move in sent:
        move.wait_send()


def scatter_scratch(dims, rows, columns, order):
    big_y, big_x, big_z, _ = dims
    width = columns[1]
    ahead, left = (big_x, big_y) if order[0] == "x" else (big_y, big_x)
    return [
        pltpu.VMEM((big_y, big_x, big_z, rows, width), BF),
        pltpu.VMEM((big_y, big_x, big_z, rows, width), BF),
        pltpu.VMEM((ahead - 1, left, big_z, rows, width), BF),
        pltpu.VMEM((left - 1, big_z, rows, width), BF),
        pltpu.VMEM((big_z - 1, rows, width), BF),
    ]


def sum_tiles(net, tile, slots):
    first = 0
    for name, me in (("band", net.band), ("img", net.img)):
        places = net.line(name)
        slots[first + me] = tile[...]
        moves = [net.copy(Part(tile), Part(slots)[first + me], dev) for _, dev in places]
        for move in moves:
            move.wait_recv()
        for move in moves:
            move.wait_send()
        total = slots[first]
        for d in range(1, len(places) + 1):
            total = total + slots[first + d]
        tile[...] = total
        first += len(places) + 1


def sems(count):
    return pltpu.SemaphoreType.DMA((max(count, 1),))


def halves(width):
    units = width // 128
    low = (units + 1) // 2 * 128
    if low == width:
        return [((0, width), "xy")]
    return [((0, low), "xy"), ((low, width - low), "yx")]


def pieces(width, shares):
    units, found, start = width // 128, [], 0
    for group in range(len(shares)):
        stop = units * sum(shares[: group + 1]) // sum(shares) * 128
        found.append((start, stop - start))
        start = stop
    return found


def gather_call(dims, name, number, blocks, images=None):
    big_y, big_x, big_z, share = dims
    parts = [[(0, block.shape[1])] for block in blocks]
    copies = sum(len(p) for p in parts) * gather_copies(dims)
    local = sum(len(p) for p in parts)
    n = len(blocks)
    with_images = images is not None
    if with_images:
        copies += images.shape[0] - 1
        local += 1

    def body(*refs):
        ins, rest = refs[: n + with_images], refs[n + with_images :]
        outs, (send, recv, local_sem) = rest[: n + with_images], rest[n + with_images :]
        net = Net(dims, send, recv, local_sem)
        net.greet("zxyc" if not with_images else ["z", "x", "y", "c", "image"])
        tasks = []
        for j in range(n):
            for columns in parts[j]:
                tasks.append((0, gather(net, ins[j], outs[j], columns)))
        if with_images:
            tasks.append((1, exchange_images(net, ins[n], outs[n], 3)))
        drive(tasks)

    args = list(blocks) + ([images] if with_images else [])
    shapes = [jax.ShapeDtypeStruct((big_y, big_x, big_z, 2) + b.shape, b.dtype) for b in blocks]
    if with_images:
        shapes.append(jax.ShapeDtypeStruct(images.shape, images.dtype))
    return pl.pallas_call(
        body,
        out_shape=shapes,
        in_specs=[ANY] * len(args),
        out_specs=[ANY] * len(shapes),
        scratch_shapes=[sems(copies), sems(copies), sems(local)],
        compiler_params=pltpu.CompilerParams(collective_id=number, has_side_effects=True),
        name=name,
    )(*args)


def finale_call(dims, number, tokens, back_project, weight, back_middle, gains, gain_two_grad, squares, images):
    big_y, big_x, big_z, _ = dims
    rows, width = tokens.shape
    block = rows // images
    devices = 2 * big_x * big_y * big_z
    shard = width // devices
    parts = halves(3 * width + 128)
    tile = 256
    band_size, img_size = 2 * big_z, big_x * big_y
    copies = len(parts) * scatter_copies(dims) + images - 1 + band_size + img_size - 2
    local = len(parts) + 5 + 2 * images
    scratch = [sems(copies), sems(copies), sems(local)]
    for columns, order in parts:
        scratch += scatter_scratch(dims, shard, columns, order)
    n_fixed = 3 + 5 * len(parts)
    scratch += [
        pltpu.VMEM((8, 128), F32),
        pltpu.VMEM((band_size + img_size, 8, 128), F32),
        pltpu.VMEM(tokens.shape, BF),
        pltpu.VMEM(back_project.shape, BF),
        pltpu.VMEM(weight.shape, BF),
        pltpu.VMEM(back_middle.shape, F32),
        pltpu.VMEM((images, block, width), BF),
        pltpu.VMEM((width, rows), BF),
        pltpu.VMEM((128, width), F32),
    ]
    scratch += [pltpu.VMEM((big_y, big_x, big_z, 2, shard, columns[1]), BF) for columns, _ in parts]

    def body(*refs):
        x_hbm, b_hbm, w_hbm, m_hbm, g_ref, two_ref, squares_ref = refs[:7]
        sum_ref, moved, total_ref, rest = refs[7], refs[8], refs[9], refs[10:]
        tally, slots, x_all, b_all, w_all, m_all, sent, normed_t, gain_rows = rest[n_fixed : n_fixed + 9]
        grads = rest[n_fixed + 9 :]
        net = Net(dims, *rest[:3])
        order = [other for other, _ in net.line("image")] + [net.image]
        load_w = net.local_copy(Part(w_hbm), Part(w_all))
        loads = []
        for chunk in order:
            at = pl.ds(pl.multiple_of(chunk * block, block), block)
            loads.append([net.local_copy(Part(a)[at, :], Part(b)[at, :]) for a, b in ((b_hbm, b_all), (x_hbm, x_all))])
            if len(loads) == 1:
                load_m = net.local_copy(Part(m_hbm), Part(m_all))
        net.greet(["z", "x", "y", "c", "image", "band", "img"])
        tally[...] = squares_ref[...]
        gain_rows[...] = jnp.zeros_like(gain_rows)
        gain_rows[1:2, :] = two_ref[0:1, :]
        load_w.wait()
        moves = []
        for place, chunk in enumerate(order):
            for load in loads[place]:
                load.wait()
            if place == 0:
                load_m.wait()
            at = pl.ds(pl.multiple_of(chunk * block, block), block)
            gain = g_ref[0:1, :]
            x = x_all[at, :].astype(F32)
            scale = inverse_rms(x)
            normed_t[:, place * block : (place + 1) * block] = jnp.transpose((x * scale * gain).astype(BF))
            into, rows_of_gain = norm_back(mm(b_all[at, :], w_all[:, : 3 * width], 1, 1), x, scale, gain)
            sent[chunk] = (m_all[at, :] + into).astype(BF)
            gain_rows[0:1, :] += jnp.sum(rows_of_gain, 0, keepdims=True)
            if place < images - 1:
                moves.append(net.copy(Part(sent)[chunk], Part(moved)[net.image], net.line("image")[place][1]))
            else:
                own = net.local_copy(Part(sent)[chunk], Part(moved)[net.image])
        tasks = []
        for k, (columns, turn) in enumerate(parts):
            buffers = rest[3 + 5 * k : 8 + 5 * k]
            for low in range(columns[0], min(columns[0] + columns[1], 3 * width), tile):
                total = jnp.zeros((width, tile), F32)
                for place, chunk in enumerate(order):
                    at = pl.ds(pl.multiple_of(chunk * block, block), block)
                    inner = slice(place * block, (place + 1) * block)
                    total = total + mm(normed_t[:, inner], b_all[at, low : low + tile], 1, 0)
                into = slice(low - columns[0], low - columns[0] + tile)
                grads[k][..., into] = total.astype(BF).reshape(grads[k].shape[:5] + (tile,))
            if k == len(parts) - 1:
                turned = jnp.transpose(gain_rows[...]).astype(BF)
                grads[k][..., columns[1] - 128 :] = turned.reshape(grads[k].shape[:5] + (128,))
            task = scatter(net, grads[k], *buffers, sum_ref, tally, (0, columns[1]), turn, columns[0])
            next(task)
            tasks.append((0, task))
        drive(tasks)
        sum_tiles(net, tally, slots)
        total_ref[...] = jnp.broadcast_to(jnp.sum(tally[...], keepdims=True), (8, 128))
        for move in moves:
            move.wait_recv()
        own.wait()
        for move in moves:
            move.wait_send()

    vmem = pl.BlockSpec(memory_space=pltpu.VMEM)
    shapes = [
        jax.ShapeDtypeStruct((shard, 3 * width + 128), F32),
        jax.ShapeDtypeStruct((images, block, width), BF),
        jax.ShapeDtypeStruct((8, 128), F32),
    ]
    return pl.pallas_call(
        body,
        out_shape=shapes,
        in_specs=[ANY] * 4 + [vmem] * 3,
        out_specs=[vmem, ANY, vmem],
        scratch_shapes=scratch,
        compiler_params=pltpu.CompilerParams(
            collective_id=number, has_side_effects=True, vmem_limit_bytes=61 * MIB
        ),
        name="finale",
    )(tokens, back_project, weight, back_middle, gains, gain_two_grad, squares)


def whole(shape):
    return pl.BlockSpec(shape, lambda i: (0,) * len(shape))


def kept(shape):
    return pl.BlockSpec(shape, lambda i: (0,) * len(shape), pipeline_mode=pl.Buffered(1))


def inverse_rms(value):
    return lax.rsqrt(jnp.mean(value * value, -1, keepdims=True) + EPS)


def mm(a, b, ca, cb):
    return lax.dot_general(a, b, (((ca,), (cb,)), ((), ())), preferred_element_type=F32)


def at_turn(turn, events):
    def visit(whens):
        if len(whens) == 1:

            @pl.when(turn == whens[0])
            def _():
                for task in events[whens[0]]:
                    next(task, None)

        elif whens:
            middle = len(whens) // 2

            @pl.when(turn < whens[middle])
            def _():
                visit(whens[:middle])

            @pl.when(turn >= whens[middle])
            def _():
                visit(whens[middle:])

    visit(sorted(events))


def schedule(tasks, turns, last):
    events, tail = {}, []
    for task, when in zip(tasks, turns):
        for turn in when:
            if turn < last:
                events.setdefault(turn, []).append(task)
            else:
                tail.append(task)
    return events, tail


def lanes_of(h):
    lane = lax.broadcasted_iota(jnp.int32, (1, PAIR), 1) < HEAD_DIM
    return lane if h == 0 else ~lane


def attend(dims, number, tokens, weight, bias, block, weights, chunks):
    big_y, big_x, big_z, share = dims
    rows, width = tokens.shape
    pairs = width // PAIR
    others = share - 1
    blocks = 4
    n = len(weights)
    last = LEAD + 4 * pairs
    parts = [
        (j, columns, GATHER_TURNS[group])
        for j, w in enumerate(weights)
        for group, columns in enumerate(pieces(w.shape[1], GATHER_SHARES))
    ]
    copies = len(parts) * gather_copies(dims) + others * 2 * pairs + chunks.shape[0] - 1

    def body(*refs):
        x_ref, w_ref, bias_ref, chunks_in = refs[:4]
        blocks_in, refs = refs[4 : 4 + n], refs[4 + n :]
        o_ref, l_ref, kv_out, chunks_out, project_ref, gains_ref, refs = refs[:6] + (refs[6:],)
        gathered, (kv_held, send, recv, local) = refs[:n], refs[n:]
        h = pl.program_id(0)
        net = Net(dims, send, recv, local)

        def move_keys(j):
            moves = []
            for slot, (_, target) in enumerate(net.line("share")):
                source = Part(project_ref)[:, pl.ds(width + PAIR * j, PAIR)]
                moves.append(net.plan(source, Part(kv_held)[others - 1 - slot, j], target))
            return moves

        key_moves = [move_keys(j) for j in range(2 * pairs)]
        keep = Move(Part(kv_held), Part(kv_out), None, local, len(parts) + 1, None)
        tasks = [gather(net, blocks_in[j], gathered[j], columns) for j, columns, _ in parts]
        tasks.append(exchange_images(net, chunks_in, chunks_out))
        turns = [turn for _, _, turn in parts] + [CHUNK_TURNS]
        events, tail = schedule(tasks, turns, last)

        @pl.when(h == 0)
        def _():
            net.greet(["z", "x", "y", "c", "image"] + (["share"] if share > 2 else []))
            gains_ref[...] = jnp.transpose(w_ref[:, 3 * width :].astype(F32))[:8]

        @pl.when(h == 0)
        def _():
            def row_step(i, _):
                at_turn(i, {t: e for t, e in events.items() if t < LEAD})
                at = pl.ds(pl.multiple_of(i * block, block), block)
                x = x_ref[at, :].astype(F32)
                normed = (x * inverse_rms(x) * gains_ref[0:1, :]).astype(BF)
                project_ref[at, :] = mm(normed, w_ref[:, : 3 * width], 1, 0).astype(BF)
                return 0

            lax.fori_loop(0, blocks, row_step, 0)
            for j in range(pairs):
                for move in key_moves[j] + key_moves[j + pairs]:
                    move.start()

        for j in range(pairs):

            @pl.when(h == j)
            def _(j=j):
                for move in key_moves[j] + key_moves[j + pairs]:
                    move.wait_recv()
                if j == pairs - 1:
                    keep.start()

        def own(first):
            return pl.ds(pl.multiple_of((h + first) * PAIR, PAIR), PAIR)

        def step(i, _):
            at_turn(LEAD + h * 4 + i, {t: e for t, e in events.items() if t >= LEAD})
            at = pl.ds(pl.multiple_of(i * block, block), block)
            k = jnp.concatenate([project_ref[:, own(pairs)]] + [kv_held[s, h] for s in range(others)], 0)
            v = jnp.concatenate(
                [project_ref[:, own(2 * pairs)]] + [kv_held[s, h + pairs] for s in range(others)], 0
            )
            q = project_ref[at, own(0)] * jnp.asarray(SCALE, BF)
            mixed, logs = [], []
            for half in range(2):
                scores = mm(jnp.where(lanes_of(half), q, jnp.zeros_like(q)), k, 1, 1) + bias_ref[...]
                highest = jnp.max(scores, -1, keepdims=True)
                powers = jnp.exp(scores - highest)
                total = jnp.sum(powers, -1, keepdims=True)
                mixed.append(mm(powers.astype(BF), v, 1, 0) / total)
                logs.append(highest + jnp.log(total))
            o_ref[at, :] = jnp.where(lanes_of(0), mixed[0], mixed[1]).astype(BF)
            l_ref[at, :] = jnp.where(lanes_of(0), logs[0], logs[1])
            return 0

        lax.fori_loop(0, blocks, step, 0)

        @pl.when(h == pairs - 1)
        def _():
            for task in tail:
                next(task, None)
            for moves in key_moves:
                for move in moves:
                    move.wait_send()
            keep.wait()

    column = lambda first: pl.BlockSpec((rows, PAIR), lambda h: (0, h + first))
    keys = rows * share
    shapes = [
        jax.ShapeDtypeStruct((rows, width), BF),
        jax.ShapeDtypeStruct((rows, width), F32),
        jax.ShapeDtypeStruct((others, 2 * pairs, rows, PAIR), BF),
        jax.ShapeDtypeStruct(chunks.shape, chunks.dtype),
        jax.ShapeDtypeStruct((rows, 3 * width), BF),
        jax.ShapeDtypeStruct((8, width), F32),
    ] + [jax.ShapeDtypeStruct((big_y, big_x, big_z, 2) + w.shape, w.dtype) for w in weights]
    return pl.pallas_call(
        body,
        grid=(pairs,),
        in_specs=[kept(tokens.shape), kept(weight.shape), kept((1, keys))] + [ANY] * (1 + n),
        out_specs=[column(0), column(0), ANY, ANY, kept((rows, 3 * width)), kept((8, width))] + [ANY] * n,
        out_shape=shapes,
        scratch_shapes=[
            pltpu.VMEM((others, 2 * pairs, rows, PAIR), BF),
            sems(copies),
            sems(copies),
            sems(len(parts) + 2),
        ],
        compiler_params=pltpu.CompilerParams(
            collective_id=number, has_side_effects=True, vmem_limit_bytes=60 * MIB
        ),
        cost_estimate=pl.CostEstimate(
            flops=16 * rows * keys * width, bytes_accessed=8 * keys * width, transcendentals=rows * keys * HEADS
        ),
        name="attend",
    )(tokens, weight, bias, chunks, *weights)


LEAD = 4
GATHER_SHARES = (1, 2, 2, 2, 2, 1)
GATHER_TURNS = (
    (0, 4, 7, 12, 14),
    (0, 7, 12, 16, 20),
    (1, 10, 16, 21, 24),
    (2, 14, 21, 25, 28),
    (3, 17, 24, 28, 28),
    (5, 20, 27, 28, 28),
)
CHUNK_TURNS = (14, 28)
SCATTER_TURNS = (
    ((2, 5, 13, 20, 24),),
    ((0, 2, 8, 15, 21), (0, 3, 10, 17, 23)),
    ((1, 4, 12, 19, 24),),
)
RESULT_TURNS = (0, 24)


def attend_back(dims, number, project, kv, bias, mixed, logs, back, block, grads, chunks):
    big_y, big_x, big_z, share = dims
    rows, width = mixed.shape
    pairs = width // PAIR
    others = share - 1
    blocks = 4
    keys = rows * share
    n = len(grads)
    parts = [
        (j, (low + first, wide), order, SCATTER_TURNS[j][group])
        for j, g in enumerate(grads)
        for group, (first, width_of) in enumerate(pieces(g.shape[5], (1,) * len(SCATTER_TURNS[j])))
        for (low, wide), order in halves(width_of)
    ]
    copies = len(parts) * scatter_copies(dims) + others * 2 * pairs + chunks.shape[0] - 1

    def body(*refs):
        q_ref, k_ref, v_ref, k_other, v_other, bias_ref, mixed_ref, logs_ref, back_ref = refs[:9]
        grads_in, chunks_in, refs = refs[9 : 9 + n], refs[9 + n], refs[10 + n :]
        out_ref, sums, squares, chunks_out, refs = refs[0], refs[1 : 1 + n], refs[1 + n], refs[2 + n], refs[3 + n :]
        dk_sums, dv_sums, parted, arrived, bias_column = refs[:5]
        send, recv, local = refs[5:8]
        buffers = refs[8:]
        h = pl.program_id(0)
        net = Net(dims, send, recv, local)

        def move_keys(j):
            moves = []
            for slot, (_, target) in enumerate(net.line("share")):
                moves.append(net.plan(Part(parted)[slot, j], Part(arrived)[others - 1 - slot, j], target))
            return moves

        key_moves = [move_keys(j) for j in range(2 * pairs)]
        tasks = [
            scatter(net, grads_in[j], *buffers[5 * k : 5 * k + 5], sums[j], squares, columns, order)
            for k, (j, columns, order, _) in enumerate(parts)
        ]
        tasks.append(exchange_images(net, chunks_in, chunks_out))
        turns = [turn for _, _, _, turn in parts] + [RESULT_TURNS]
        events, tail = schedule(tasks, turns, 4 * pairs)

        @pl.when(h == 0)
        def _():
            net.greet(["z", "x", "y", "c", "image"] + (["share"] if share > 2 else []))
            squares[...] = jnp.zeros_like(squares)
            bias_column[...] = jnp.transpose(jnp.broadcast_to(bias_ref[...], (PAIR, keys)))

        turn = lax.rem(h, 2)
        dk_sums[turn] = jnp.zeros((keys, PAIR), F32)
        dv_sums[turn] = jnp.zeros((keys, PAIR), F32)

        def step(i, _):
            at_turn(h * 4 + i, events)
            at = pl.ds(pl.multiple_of(i * block, block), block)
            k = jnp.concatenate([k_ref[...]] + [k_other[s, 0] for s in range(others)], 0)
            v = jnp.concatenate([v_ref[...]] + [v_other[s, 0] for s in range(others)], 0)
            q, do = q_ref[at, :] * jnp.asarray(SCALE, BF), back_ref[at, :]
            lse = jnp.transpose(logs_ref[at, :])
            products = jnp.transpose(do.astype(F32) * mixed_ref[at, :].astype(F32))
            dqs, dks, dvs = [], [], []
            mask = jnp.concatenate([bias_column[...]] * (block // PAIR), 1)
            for half in range(2):
                low, high = half * HEAD_DIM, (half + 1) * HEAD_DIM
                q_h = jnp.where(lanes_of(half), q, jnp.zeros_like(q))
                do_h = jnp.where(lanes_of(half), do, jnp.zeros_like(do))
                row_dots = jnp.sum(products[low:high, :], 0, keepdims=True)
                chances = jnp.exp(mm(k, q_h, 1, 1) + mask - lse[low : low + 1, :])
                slopes = mm(v, do_h, 1, 1)
                scores = (chances * (slopes - row_dots)).astype(BF)
                dqs.append(mm(scores, k, 0, 0))
                dks.append(mm(scores, q_h, 1, 0))
                dvs.append(mm(chances.astype(BF), do_h, 1, 0))
            dq = (jnp.where(lanes_of(0), dqs[0], dqs[1]) * SCALE).astype(BF)
            out_ref[at, pl.ds(pl.multiple_of(h * PAIR, PAIR), PAIR)] = dq
            dk_sums[turn] += dks[0] + dks[1]
            dv_sums[turn] += dvs[0] + dvs[1]
            return 0

        lax.fori_loop(0, blocks, step, 0)

        def finish(j):
            for move in key_moves[j] + key_moves[j + pairs]:
                move.wait_recv()
            for kept, sums_of in ((j, dk_sums), (j + pairs, dv_sums)):
                value = sums_of[j % 2, 0:rows, :]
                for slot in range(others):
                    value = value + arrived[slot, kept].astype(F32)
                out_ref[:, width + PAIR * kept : width + PAIR * (kept + 1)] = value.astype(BF)

        for j in range(pairs):

            @pl.when(h == j)
            def _(j=j):
                if j > 0:
                    finish(j - 1)
                for slot in range(others):
                    away = slice(rows * (slot + 1), rows * (slot + 2))
                    parted[slot, j] = dk_sums[j % 2, away, :].astype(BF)
                    parted[slot, j + pairs] = dv_sums[j % 2, away, :].astype(BF)
                for move in key_moves[j] + key_moves[j + pairs]:
                    move.start()
                if j == pairs - 1:
                    for task in tail:
                        next(task, None)
                    finish(j)
                    for moves in key_moves:
                        for move in moves:
                            move.wait_send()

    column = lambda first: pl.BlockSpec((rows, PAIR), lambda h: (0, h + first))
    other = lambda first: pl.BlockSpec((others, 1, rows, PAIR), lambda h: (0, h + first, 0, 0))
    whole = lambda shape: pl.BlockSpec(shape, lambda h: (0,) * len(shape))
    shard = grads[0].shape[4] if n else 0
    shapes = (
        [jax.ShapeDtypeStruct((rows, 3 * width), BF)]
        + [jax.ShapeDtypeStruct((shard, g.shape[5]), F32) for g in grads]
        + [jax.ShapeDtypeStruct((8, 128), F32)]
    )
    moved = jax.ShapeDtypeStruct(chunks.shape, chunks.dtype)
    scratch = [
        pltpu.VMEM((2, keys, PAIR), F32),
        pltpu.VMEM((2, keys, PAIR), F32),
        pltpu.VMEM((others, 2 * pairs, rows, PAIR), BF),
        pltpu.VMEM((others, 2 * pairs, rows, PAIR), BF),
        pltpu.VMEM((keys, PAIR), F32),
        sems(copies),
        sems(copies),
        sems(len(parts) + 1),
    ]
    for _, columns, order, _ in parts:
        scratch += scatter_scratch(dims, shard, columns, order)
    return pl.pallas_call(
        body,
        grid=(pairs,),
        in_specs=[
            column(0),
            column(pairs),
            column(2 * pairs),
            other(0),
            other(pairs),
            whole((1, keys)),
            column(0),
            column(0),
            column(0),
        ]
        + [ANY] * (n + 1),
        out_specs=[whole(s.shape) for s in shapes] + [ANY],
        out_shape=shapes + [moved],
        scratch_shapes=scratch,
        compiler_params=pltpu.CompilerParams(
            collective_id=number, has_side_effects=True, vmem_limit_bytes=60 * MIB
        ),
        cost_estimate=pl.CostEstimate(
            flops=40 * rows * keys * width, bytes_accessed=16 * keys * width, transcendentals=rows * keys * HEADS
        ),
        name="attend_back",
    )(project, project, project, kv, kv, bias, mixed, logs, back, *grads, chunks)


def norm_back(back, value, scale, gain):
    scaled = back * gain
    inner = jnp.mean(scaled * value, -1, keepdims=True)
    return scale * scaled - value * (scale * scale * scale * inner), back * (value * scale)


GELU_A = 0.7978845608028654
GELU_B = 0.044715


def mlp_call(tokens, attended, cotangent, keep, weights, gains, block):
    rows, width = tokens.shape
    hidden_units = (weights.shape[1] - width) // 3
    steps = rows // block
    tile = 1024
    in_tiles, down_tiles = 2 * hidden_units // tile, hidden_units // tile
    part = 512

    def body(
        x_ref, a_ref, c_ref, keep_ref, w_ref, g_ref,
        result_ref, middle_ref, back_ref, gain_ref, g_out_ref, g_in_ref, g_down_ref,
        normed_t, low_t, branch_t, mixed, hidden, back_gu,
    ):
        i = pl.program_id(0)
        wo_ref = w_ref.at[:, :width]
        wi_ref = w_ref.at[:, width : width + 2 * hidden_units]
        wd_ref = w_ref.at[:, width + 2 * hidden_units :]

        @pl.when(i == 0)
        def _():
            gain_ref[...] = jnp.zeros_like(gain_ref)

        @pl.when(i < steps)
        def _():
            at = pl.ds(pl.multiple_of(i * block, block), block)
            gain = g_ref[1:2, :]
            a = a_ref[...]
            mixed[at, :] = a
            middle = x_ref[...].astype(F32) + mm(a, wo_ref[...], 1, 1)
            scale = inverse_rms(middle)
            normed = (middle * scale * gain).astype(BF)
            normed_t[:, at] = jnp.transpose(normed)
            back_result = keep_ref[...] * c_ref[...].astype(F32)
            low = back_result.astype(BF)
            low_t[:, at] = jnp.transpose(low)
            result, back = middle, jnp.zeros_like(middle)
            for p in range(hidden_units // part):
                one = slice(p * part, (p + 1) * part)
                two = slice(hidden_units + p * part, hidden_units + (p + 1) * part)
                gate = mm(normed, wi_ref[:, one], 1, 0)
                up = mm(normed, wi_ref[:, two], 1, 0)
                back_hidden = mm(low, wd_ref[:, one], 1, 0)
                square = gate * gate
                bend = jnp.tanh(GELU_A * (gate + GELU_B * (gate * square)))
                half = 0.5 + 0.5 * bend
                curve = gate * half
                slope = half + (0.5 * GELU_A) * gate * (1.0 - bend * bend) * (1.0 + (3.0 * GELU_B) * square)
                hid = (curve * up).astype(BF)
                back_gate = (back_hidden * up * slope).astype(BF)
                back_up = (back_hidden * curve).astype(BF)
                hidden[at, one] = hid
                back_gu[at, one] = back_gate
                back_gu[at, two] = back_up
                result = result + mm(hid, wd_ref[:, one], 1, 1)
                back = back + mm(back_gate, wi_ref[:, one], 1, 1) + mm(back_up, wi_ref[:, two], 1, 1)
            result_ref[...] = (keep_ref[...] * result).astype(BF)
            into, gain_rows = norm_back(back, middle, scale, gain)
            gain_ref[0:1, :] += jnp.sum(gain_rows, 0, keepdims=True)
            back_middle = back_result + into
            middle_ref[...] = back_middle
            branch = back_middle.astype(BF)
            branch_t[:, at] = jnp.transpose(branch)
            back_ref[...] = mm(branch, wo_ref[...], 1, 0).astype(BF)

        @pl.when(i == steps)
        def _():
            g_out_ref[...] = mm(branch_t[...], mixed[...], 1, 0).astype(BF)

        for t in range(in_tiles):

            @pl.when(i == steps + 1 + t)
            def _(t=t):
                g_in_ref[...] = mm(normed_t[...], back_gu[:, t * tile : (t + 1) * tile], 1, 0).astype(BF)

        for t in range(down_tiles):

            @pl.when(i == steps + 1 + in_tiles + t)
            def _(t=t):
                g_down_ref[...] = mm(low_t[...], hidden[:, t * tile : (t + 1) * tile], 1, 0).astype(BF)

    row = lambda last: pl.BlockSpec((block, last), lambda i: (jnp.minimum(i, steps - 1), 0))
    return pl.pallas_call(
        body,
        grid=(steps + 1 + in_tiles + down_tiles,),
        in_specs=[
            row(width),
            row(width),
            row(width),
            row(1),
            kept(weights.shape),
            kept(gains.shape),
        ],
        out_specs=[
            row(width),
            row(width),
            row(width),
            whole((8, width)),
            whole((width, width)),
            pl.BlockSpec((width, tile), lambda i: (0, jnp.clip(i - steps - 1, 0, in_tiles - 1))),
            pl.BlockSpec((width, tile), lambda i: (0, jnp.clip(i - steps - 1 - in_tiles, 0, down_tiles - 1))),
        ],
        out_shape=[
            jax.ShapeDtypeStruct((rows, width), BF),
            jax.ShapeDtypeStruct((rows, width), F32),
            jax.ShapeDtypeStruct((rows, width), BF),
            jax.ShapeDtypeStruct((8, width), F32),
            jax.ShapeDtypeStruct((width, width), BF),
            jax.ShapeDtypeStruct((width, 2 * hidden_units), BF),
            jax.ShapeDtypeStruct((width, hidden_units), BF),
        ],
        scratch_shapes=[
            pltpu.VMEM((width, rows), BF),
            pltpu.VMEM((width, rows), BF),
            pltpu.VMEM((width, rows), BF),
            pltpu.VMEM((rows, width), BF),
            pltpu.VMEM((rows, hidden_units), BF),
            pltpu.VMEM((rows, 2 * hidden_units), BF),
        ],
        compiler_params=pltpu.CompilerParams(vmem_limit_bytes=61 * MIB),
        cost_estimate=pl.CostEstimate(
            flops=6 * rows * width * (width + 3 * hidden_units),
            bytes_accessed=8 * width * (width + 3 * hidden_units),
            transcendentals=rows * hidden_units,
        ),
        name="mlp",
    )(tokens, attended, cotangent, keep, weights, gains)


def finish_call(tokens, back_project, weight, back_middle, gains, gain_two_grad, block):
    rows, width = tokens.shape
    steps = rows // block
    tiles, tile = 3, width

    def body(x_ref, b_ref, w_ref, m_ref, g_ref, two_ref, out_ref, grad_ref, gain_ref, normed_t, held, gain_rows):
        i = pl.program_id(0)

        @pl.when(i == 0)
        def _():
            gain_rows[...] = jnp.zeros_like(gain_rows)
            gain_rows[1:2, :] = two_ref[0:1, :]

        @pl.when(i < steps)
        def _():
            at = pl.ds(pl.multiple_of(i * block, block), block)
            gain = g_ref[0:1, :]
            x = x_ref[...].astype(F32)
            scale = inverse_rms(x)
            normed_t[:, at] = jnp.transpose((x * scale * gain).astype(BF))
            back = b_ref[...]
            held[at, :] = back
            into, rows_of_gain = norm_back(mm(back, w_ref[:, : 3 * width], 1, 1), x, scale, gain)
            out_ref[...] = (m_ref[...] + into).astype(BF)
            gain_rows[0:1, :] += jnp.sum(rows_of_gain, 0, keepdims=True)

        for t in range(tiles):

            @pl.when(i == steps + t)
            def _(t=t):
                grad_ref[...] = mm(normed_t[...], held[:, t * tile : (t + 1) * tile], 1, 0).astype(BF)

        @pl.when(i == steps)
        def _():
            gain_ref[...] = jnp.transpose(gain_rows[...]).astype(BF)

    row = lambda last: pl.BlockSpec((block, last), lambda i: (jnp.minimum(i, steps - 1), 0))
    return pl.pallas_call(
        body,
        grid=(steps + tiles,),
        in_specs=[row(width), row(3 * width), kept(weight.shape), row(width), kept(gains.shape), kept((8, width))],
        out_specs=[
            row(width),
            pl.BlockSpec((width, tile), lambda i: (0, jnp.clip(i - steps, 0, tiles - 1))),
            whole((width, 128)),
        ],
        out_shape=[
            jax.ShapeDtypeStruct((rows, width), BF),
            jax.ShapeDtypeStruct((width, 3 * width), BF),
            jax.ShapeDtypeStruct((width, 128), BF),
        ],
        scratch_shapes=[
            pltpu.VMEM((width, rows), BF),
            pltpu.VMEM((rows, 3 * width), BF),
            pltpu.VMEM((128, width), F32),
        ],
        compiler_params=pltpu.CompilerParams(vmem_limit_bytes=48 * MIB),
        cost_estimate=pl.CostEstimate(
            flops=12 * rows * width * width, bytes_accessed=28 * width * width, transcendentals=rows
        ),
        name="finish",
    )(tokens, back_project, weight, back_middle, gains, gain_two_grad)


def adam_step(master, grad, first, second, factor, rate, decay):
    clipped = factor * grad
    first_new = BETA_ONE * first + (1.0 - BETA_ONE) * clipped
    second_new = BETA_TWO * second + (1.0 - BETA_TWO) * clipped * clipped
    corrected = first_new / (1.0 - BETA_ONE**STEP)
    spread = jnp.sqrt(second_new / (1.0 - BETA_TWO**STEP)) + ADAM_EPS
    master_new = master - rate * (corrected / spread + decay * master)
    return (master_new, first_new, second_new)


def adam_call(squares, grads, masters, firsts, seconds):
    shard, width = grads[0].shape[0], grads[0].shape[1] - 128

    def body(*refs):
        squares_ref, refs = refs[0], refs[1:]
        ins, norm_ref, outs = refs[:19], refs[19], refs[20:]
        norm = jnp.sqrt(squares_ref[0:1, :])
        norm_ref[0, 0] = norm[0, 0]
        factor = jnp.minimum(1.0, CLIP / norm[:, 0:1])
        for j in range(5):
            grad = ins[0][:, :width] if j == 0 else ins[0][:, width:] if j == 4 else ins[j][...]
            if j == 4:
                filled = jnp.concatenate([grad, jnp.zeros((128 - shard, 128), F32)], 0)
                grad = jnp.transpose(filled)[:2, :shard]
            made = adam_step(
                ins[4 + j][...], grad, ins[9 + j][...], ins[14 + j][...], factor, RATES[j], DECAYS[j]
            )
            for kind in range(3):
                outs[5 * kind + j][...] = made[kind]
            outs[15 + j][...] = made[0].astype(BF)

    shapes = [jax.ShapeDtypeStruct((1, 1), F32)]
    shapes += [jax.ShapeDtypeStruct(m.shape, F32) for _ in range(3) for m in masters]
    shapes += [jax.ShapeDtypeStruct(m.shape, BF) for m in masters]
    vmem = pl.BlockSpec(memory_space=pltpu.VMEM)
    return pl.pallas_call(
        body,
        out_shape=shapes,
        out_specs=[pl.BlockSpec(memory_space=pltpu.SMEM)] + [vmem] * 20,
        compiler_params=pltpu.CompilerParams(vmem_limit_bytes=60 * MIB),
        name="adam",
    )(squares, *grads, *masters, *firsts, *seconds)


def prepare_call(dims, counts, qkv, out_t, in_up, down_t, gains, rows, band_rows):
    share = dims[3]
    images = rows // band_rows
    shard, width = qkv.shape[0], out_t.shape[1]
    wide = in_up.shape[1]

    def body(counts_ref, qkv_ref, out_ref, in_ref, down_ref, gain_ref, early_ref, late_ref, keep_ref, bias_ref):
        early_ref[:, : 3 * width] = qkv_ref[...].astype(BF)
        filled = jnp.concatenate([gain_ref[...], jnp.zeros((2, 128 - shard), F32)], 1)
        filled = jnp.concatenate([filled, jnp.zeros((126, 128), F32)], 0)
        early_ref[:, 3 * width :] = jnp.transpose(filled)[:shard].astype(BF)
        late_ref[:, :width] = out_ref[...].astype(BF)
        late_ref[:, width : width + wide] = in_ref[...].astype(BF)
        late_ref[:, width + wide :] = down_ref[...].astype(BF)
        band = lax.axis_index("band")
        image, part = band // share, lax.rem(band, share)
        count = counts_ref[image]
        down = lax.broadcasted_iota(jnp.int32, (band_rows, 1), 0)
        along = lax.broadcasted_iota(jnp.int32, (1, band_rows), 1)
        for s in range(images):
            first = (s * share + part) * band_rows
            keep_ref[s * band_rows : (s + 1) * band_rows, :] = jnp.where(down + first < count, 1.0, 0.0)
            for other in range(share):
                first = (s * share + lax.rem(part + other, share)) * band_rows
                at = (other * images + s) * band_rows
                bias_ref[:, at : at + band_rows] = jnp.where(along + first < count, 0.0, NEG)

    vmem = pl.BlockSpec(memory_space=pltpu.VMEM)
    return pl.pallas_call(
        body,
        out_shape=[
            jax.ShapeDtypeStruct((shard, 3 * width + 128), BF),
            jax.ShapeDtypeStruct((shard, width + wide + down_t.shape[1]), BF),
            jax.ShapeDtypeStruct((rows, 1), F32),
            jax.ShapeDtypeStruct((1, share * rows), F32),
        ],
        in_specs=[pl.BlockSpec(memory_space=pltpu.SMEM)] + [vmem] * 5,
        out_specs=[vmem] * 4,
        compiler_params=pltpu.CompilerParams(vmem_limit_bytes=60 * MIB),
        name="prepare",
    )(counts, qkv, out_t, in_up, down_t, gains)


def grid_of(n_img):
    big_y = max(d for d in range(1, n_img + 1) if n_img % d == 0 and d * d <= n_img)
    return big_y, n_img // big_y


def on_device(
    patches,
    cotangent,
    valid_counts,
    qkv_master,
    out_master,
    in_master,
    down_master,
    gain_master,
    qkv_first,
    out_first,
    in_first,
    down_first,
    gain_first,
    qkv_second,
    out_second,
    in_second,
    down_second,
    gain_second,
):
    images, band_rows, width = patches.shape
    n_img, n_band = lax.axis_size("img"), lax.axis_size("band")
    share = n_band // images
    big_y, big_x = grid_of(n_img)
    dims = (big_y, big_x, n_band // 2, share)
    rows = images * band_rows
    shard = qkv_master.shape[0]
    own_comm = shard % 8 == 0 and big_y == big_x == 2
    both = ("img", "band")

    places = [[s * share + r for s in range(images)] for r in range(share)]

    def exchange(chunks):
        return lax.all_to_all(chunks, "band", 0, 0, axis_index_groups=places, tiled=True)

    def blocks_of(grads):
        return [g.reshape(dims[:3] + (2, shard, g.shape[1])) for g in grads]

    early, late, row_keep, bias = prepare_call(
        dims,
        valid_counts,
        qkv_master,
        jnp.transpose(out_master),
        in_master,
        jnp.transpose(down_master),
        gain_master,
        rows,
        band_rows,
    )
    if own_comm:
        w_early, tokens_low = gather_call(dims, "gather", 0, [early], patches)
        w_early = w_early.reshape(width, early.shape[1])
    else:
        w_early = lax.all_gather(early, both, axis=0, tiled=True)
        tokens_low = exchange(patches)
    tokens = tokens_low.reshape(rows, width)
    attended, log_sums, kv, cotangent_low, project, gain_rows, *late_all = attend(
        dims, 1, tokens, w_early, bias, rows // 4, [late] if own_comm else [], cotangent
    )
    if own_comm:
        w_late = late_all[0].reshape(width, late.shape[1])
    else:
        w_late = lax.all_gather(late, both, axis=0, tiled=True)

    result_low, back_middle, back_attended, gain_two_grad, *late_grads = mlp_call(
        tokens,
        attended,
        cotangent_low.reshape(rows, width),
        row_keep,
        w_late,
        gain_rows,
        min(256, rows),
    )
    result_low = result_low.reshape(images, band_rows, width)
    back_project, *late_sums, squares, output = attend_back(
        dims,
        2,
        project,
        kv,
        bias,
        attended,
        log_sums,
        back_attended,
        rows // 4,
        blocks_of(late_grads) if own_comm else [],
        result_low,
    )
    if not own_comm:
        late_sums = [lax.psum_scatter(g.astype(F32), both, scatter_dimension=0, tiled=True) for g in late_grads]
    if own_comm:
        qkv_sum, back_input, total = finale_call(
            dims, 3, tokens, back_project, w_early, back_middle, gain_rows, gain_two_grad, squares, images
        )
    else:
        back_rows, *early_grads = finish_call(
            tokens, back_project, w_early, back_middle, gain_rows, gain_two_grad, min(256, rows)
        )
        grad = jnp.concatenate([g.astype(F32) for g in early_grads], 1)
        qkv_sum = lax.psum_scatter(grad, both, scatter_dimension=0, tiled=True)
        back_input = exchange(back_rows.reshape(images, band_rows, width))
        squares = sum(jnp.sum(g * g) for g in late_sums + [qkv_sum])
        total = lax.psum(jnp.broadcast_to(squares, (8, 128)), both)
    out_sum, in_sum, down_sum = late_sums

    def turned(arrays):
        return [jnp.transpose(a) if j in (1, 3) else a for j, a in enumerate(arrays)]

    norm, *updated = adam_call(
        total,
        [qkv_sum, out_sum, in_sum, down_sum],
        turned([qkv_master, out_master, in_master, down_master, gain_master]),
        turned([qkv_first, out_first, in_first, down_first, gain_first]),
        turned([qkv_second, out_second, in_second, down_second, gain_second]),
    )
    updated = [a for kind in range(4) for a in turned(updated[5 * kind : 5 * kind + 5])]
    return (output, back_input, norm.reshape(())) + tuple(updated)


def solution(mesh):
    rows_split, columns_split = P(("img", "band"), None), P(None, ("img", "band"))
    weights = (rows_split, columns_split, rows_split, columns_split, columns_split)
    tokens = P("img", "band", None)
    return jax.shard_map(
        on_device,
        mesh=mesh,
        in_specs=(tokens, tokens, P("img")) + weights * 3,
        out_specs=(tokens, tokens, P()) + weights * 4,
        check_vma=False,
    )
```

```python
import functools

import jax
import jax.numpy as jnp
from jax import lax
from jax.experimental import pallas as pl
from jax.experimental.pallas import tpu as pltpu
from jax.sharding import PartitionSpec as P

HEADS = 12
HEAD_DIM = 64
PAIR = 2 * HEAD_DIM
STEP = 10
EPS = 1e-06
NEG = -1000000000.0
SCALE = 0.125
CLIP = 1.0
BETA_ONE = 0.9
BETA_TWO = 0.999
ADAM_EPS = 1e-08
RATES = (0.06, 0.5, 0.06, 0.04, 0.5)
DECAYS = (0.1, 0.1, 0.1, 0.1, 0.0)
BF = jnp.bfloat16
F32 = jnp.float32
MESH = pl.DeviceIdType.MESH
ANY = pl.BlockSpec(memory_space=pl.ANY)
MIB = 2**20


class Net:
    def __init__(self, dims, send, recv, local):
        self.dims = dims
        big_y, big_x, big_z, share = dims
        img, band = lax.axis_index("img"), lax.axis_index("band")
        self.y, self.x = img // big_x, img % big_x
        self.z, self.c = band // 2, band % 2
        self.twin = 1 - self.c
        image, self.part = band // share, band % share
        self.image, self.images = image, 2 * big_z // share
        self.send, self.recv, self.local = send, recv, local
        self.used, self.used_local = 0, 0
        self.lines = {}
        for name, size in zip("yxzc", (big_y, big_x, big_z, 2)):
            places = []
            for d in range(1, size):
                at = dict(y=self.y, x=self.x, z=self.z, c=self.c)
                at[name] = lax.rem(at[name] + d, size)
                places.append((at[name], (at["y"] * big_x + at["x"], at["z"] * 2 + at["c"])))
            self.lines[name] = places
        self.band, self.img = band, img
        self.lines["band"], self.lines["img"] = [], []
        for d in range(1, 2 * big_z):
            other = lax.rem(band + d, 2 * big_z)
            self.lines["band"].append((other, (img, other)))
        for d in range(1, big_y * big_x):
            other = lax.rem(img + d, big_y * big_x)
            self.lines["img"].append((other, (other, band)))
        across, along = lax.rem(self.x + 1, big_x), lax.rem(self.y + 1, big_y)
        one = self.c
        self.near = (jnp.where(one == 0, self.y, along), jnp.where(one == 0, across, self.x))
        self.next = (jnp.where(one == 0, along, self.y), jnp.where(one == 0, self.x, across))
        self.far = (along, across)
        self.near_device = (self.near[0] * big_x + self.near[1], band)
        self.next_device = (self.next[0] * big_x + self.next[1], band)
        self.lines["image"] = []
        for d in range(1, self.images):
            other = lax.rem(image + d, self.images)
            self.lines["image"].append((other, (img, other * share + self.part)))
        self.lines["share"] = []
        for d in range(1, share):
            other = lax.rem(self.part + d, share)
            self.lines["share"].append((other, (img, image * share + other)))

    def line(self, name):
        return self.lines[name]

    def greet(self, kinds):
        barrier = pltpu.get_barrier_semaphore()
        count = 0
        for kind in kinds:
            for _, target in self.lines[kind]:
                pl.semaphore_signal(barrier, inc=1, device_id=target, device_id_type=MESH)
            count += len(self.lines[kind])
        pl.semaphore_wait(barrier, count)

    def copy(self, source, target_ref, target):
        made = self.plan(source, target_ref, target)
        made.start()
        return made

    def plan(self, source, target_ref, target):
        self.used += 1
        return Move(source, target_ref, self.send, self.recv, self.used - 1, target)

    def local_copy(self, source, target_ref):
        self.used_local += 1
        made = Move(source, target_ref, None, self.local, self.used_local - 1, None)
        made.start()
        return made


class Part:
    def __init__(self, ref, index=None):
        self.ref, self.index = ref, index

    def __getitem__(self, index):
        return Part(self.ref, index)

    def view(self):
        return self.ref if self.index is None else self.ref.at[self.index]


class Move:
    def __init__(self, source, target_ref, send, recv, at, target):
        self.source, self.target_ref = source, target_ref
        self.send, self.recv, self.at, self.target = send, recv, at, target

    def build(self):
        if self.target is None:
            return pltpu.make_async_copy(self.source.view(), self.target_ref.view(), self.recv.at[self.at])
        return pltpu.make_async_remote_copy(
            src_ref=self.source.view(),
            dst_ref=self.target_ref.view(),
            send_sem=self.send.at[self.at],
            recv_sem=self.recv.at[self.at],
            device_id=self.target,
            device_id_type=MESH,
        )

    def start(self):
        self.build().start()

    def wait(self):
        self.build().wait()

    def wait_recv(self):
        self.build().wait_recv()

    def wait_send(self):
        self.build().wait_send()


def drive(tasks):
    waiting = list(tasks)
    turn = 0
    while waiting:
        left = []
        for start, task in waiting:
            if start <= turn:
                try:
                    next(task)
                except StopIteration:
                    continue
            left.append((start, task))
        waiting = left
        turn += 1


def exchange_images(net, source, target, idle=1):
    moves = [net.copy(Part(source)[other], Part(target)[net.image], dev) for other, dev in net.line("image")]
    own = net.local_copy(Part(source)[net.image], Part(target)[net.image])
    for _ in range(idle):
        yield
    for move in moves:
        move.wait_recv()
    own.wait()
    for move in moves:
        move.wait_send()


def gather(net, source, target, columns):
    cols = pl.ds(*columns)
    y, x, c = net.y, net.x, net.c
    (_, twin), = net.line("c")

    def blocks(place):
        return Part(target)[place[0], place[1], :, c, :, cols]

    here = Part(target)[y, x, net.z, c, :, cols]
    own = net.local_copy(Part(source)[:, cols], here)
    from_z = [net.copy(Part(source)[:, cols], here, dev) for _, dev in net.line("z")]
    yield
    own.wait()
    for move in from_z:
        move.wait_recv()
    mine = blocks((y, x))
    first = net.copy(mine, mine, net.near_device)
    second = net.copy(mine, mine, net.next_device)
    twins = [net.copy(mine, mine, twin)]
    yield
    first.wait_recv()
    near = blocks(net.near)
    third = net.copy(near, near, net.next_device)
    twins.append(net.copy(near, near, twin))
    yield
    second.wait_recv()
    third.wait_recv()
    for place in (net.next, net.far):
        twins.append(net.copy(blocks(place), blocks(place), twin))
    yield
    for move in twins:
        move.wait_recv()
    for move in from_z + [first, second, third] + twins:
        move.wait_send()


def gather_copies(dims):
    return dims[2] - 1 + 3 + 4


def scatter_copies(dims):
    return dims[0] + dims[1] + dims[2] - 3 + 1


def add_up(own, others):
    if len(others) == 1:
        return own + others[0]
    total = own.astype(F32)
    for other in others:
        total = total + other.astype(F32)
    return total.astype(own.dtype)


def scatter(net, grad, held, from_core, from_first, from_second, from_z, out, squares, columns, order, offset=0):
    big_y, big_x, big_z, _ = net.dims
    cols = pl.ds(*columns)
    y, x, z, c = net.y, net.x, net.z, net.c
    sent = []
    (_, twin), = net.line("c")
    moves = [net.copy(Part(grad)[:, :, :, net.twin, :, cols], Part(from_core), twin)]
    sent += moves
    own = net.local_copy(Part(grad)[:, :, :, c, :, cols], Part(held))
    yield
    own.wait()
    moves[0].wait_recv()

    def first_add(at, _):
        a, b, d = at // (big_x * big_z), (at // big_z) % big_x, at % big_z
        held[a, b, d] = held[a, b, d] + from_core[a, b, d]
        return 0

    lax.fori_loop(0, big_y * big_x * big_z, first_add, 0)
    moves = []
    for slot, (other, dev) in enumerate(net.line(order[0])):
        part = Part(held)[:, other] if order[0] == "x" else Part(held)[other]
        moves.append(net.copy(part, Part(from_first)[slot], dev))
    sent += moves
    yield
    for move in moves:
        move.wait_recv()
    left = big_y if order[0] == "x" else big_x

    def second_add(at, _):
        a, d = at // big_z, at % big_z
        place = (a, x, d) if order[0] == "x" else (y, a, d)
        held[place] = add_up(held[place], [from_first[slot, a, d] for slot in range(len(moves))])
        return 0

    lax.fori_loop(0, left * big_z, second_add, 0)
    moves = []
    for slot, (other, dev) in enumerate(net.line(order[1])):
        part = Part(held)[other, x] if order[1] == "y" else Part(held)[y, other]
        moves.append(net.copy(part, Part(from_second)[slot], dev))
    sent += moves
    yield
    for move in moves:
        move.wait_recv()

    def third_add(d, _):
        held[y, x, d] = add_up(held[y, x, d], [from_second[slot, d] for slot in range(len(moves))])
        return 0

    lax.fori_loop(0, big_z, third_add, 0)
    moves = []
    for slot, (other, dev) in enumerate(net.line("z")):
        moves.append(net.copy(Part(held)[y, x, other], Part(from_z)[slot], dev))
    sent += moves
    yield
    for move in moves:
        move.wait_recv()
    total = held[y, x, z].astype(F32)
    for slot in range(len(moves)):
        total = total + from_z[slot].astype(F32)
    out[:, offset + columns[0] : offset + columns[0] + columns[1]] = total
    tile = squares[...]
    for a in range(total.shape[0] // 8):
        for b in range(columns[1] // 128):
            piece = total[8 * a : 8 * a + 8, 128 * b : 128 * b + 128]
            tile = tile + piece * piece
    squares[...] = tile
    for move in sent:
        move.wait_send()


def scatter_scratch(dims, rows, columns, order):
    big_y, big_x, big_z, _ = dims
    width = columns[1]
    ahead, left = (big_x, big_y) if order[0] == "x" else (big_y, big_x)
    return [
        pltpu.VMEM((big_y, big_x, big_z, rows, width), BF),
        pltpu.VMEM((big_y, big_x, big_z, rows, width), BF),
        pltpu.VMEM((ahead - 1, left, big_z, rows, width), BF),
        pltpu.VMEM((left - 1, big_z, rows, width), BF),
        pltpu.VMEM((big_z - 1, rows, width), BF),
    ]


def sum_tiles(net, tile, slots):
    first = 0
    for name, me in (("band", net.band), ("img", net.img)):
        places = net.line(name)
        slots[first + me] = tile[...]
        moves = [net.copy(Part(tile), Part(slots)[first + me], dev) for _, dev in places]
        for move in moves:
            move.wait_recv()
        for move in moves:
            move.wait_send()
        total = slots[first]
        for d in range(1, len(places) + 1):
            total = total + slots[first + d]
        tile[...] = total
        first += len(places) + 1


def sems(count):
    return pltpu.SemaphoreType.DMA((max(count, 1),))


def halves(width):
    units = width // 128
    low = (units + 1) // 2 * 128
    if low == width:
        return [((0, width), "xy")]
    return [((0, low), "xy"), ((low, width - low), "yx")]


def pieces(width, shares):
    units, found, start = width // 128, [], 0
    for group in range(len(shares)):
        stop = units * sum(shares[: group + 1]) // sum(shares) * 128
        found.append((start, stop - start))
        start = stop
    return found


def gather_call(dims, name, number, blocks, images=None):
    big_y, big_x, big_z, share = dims
    parts = [[(0, block.shape[1])] for block in blocks]
    copies = sum(len(p) for p in parts) * gather_copies(dims)
    local = sum(len(p) for p in parts)
    n = len(blocks)
    with_images = images is not None
    if with_images:
        copies += images.shape[0] - 1
        local += 1

    def body(*refs):
        ins, rest = refs[: n + with_images], refs[n + with_images :]
        outs, (send, recv, local_sem) = rest[: n + with_images], rest[n + with_images :]
        net = Net(dims, send, recv, local_sem)
        net.greet("zxyc" if not with_images else ["z", "x", "y", "c", "image"])
        tasks = []
        for j in range(n):
            for columns in parts[j]:
                tasks.append((0, gather(net, ins[j], outs[j], columns)))
        if with_images:
            tasks.append((1, exchange_images(net, ins[n], outs[n], 3)))
        drive(tasks)

    args = list(blocks) + ([images] if with_images else [])
    shapes = [jax.ShapeDtypeStruct((big_y, big_x, big_z, 2) + b.shape, b.dtype) for b in blocks]
    if with_images:
        shapes.append(jax.ShapeDtypeStruct(images.shape, images.dtype))
    return pl.pallas_call(
        body,
        out_shape=shapes,
        in_specs=[ANY] * len(args),
        out_specs=[ANY] * len(shapes),
        scratch_shapes=[sems(copies), sems(copies), sems(local)],
        compiler_params=pltpu.CompilerParams(collective_id=number, has_side_effects=True),
        name=name,
    )(*args)


def finale_call(dims, number, tokens, back_project, weight, back_middle, gains, gain_two_grad, squares, images):
    big_y, big_x, big_z, _ = dims
    rows, width = tokens.shape
    block = rows // images
    devices = 2 * big_x * big_y * big_z
    shard = width // devices
    parts = halves(3 * width + 128)
    tile = 256
    band_size, img_size = 2 * big_z, big_x * big_y
    copies = len(parts) * scatter_copies(dims) + images - 1 + band_size + img_size - 2
    local = len(parts) + 5 + 2 * images
    scratch = [sems(copies), sems(copies), sems(local)]
    for columns, order in parts:
        scratch += scatter_scratch(dims, shard, columns, order)
    n_fixed = 3 + 5 * len(parts)
    scratch += [
        pltpu.VMEM((8, 128), F32),
        pltpu.VMEM((band_size + img_size, 8, 128), F32),
        pltpu.VMEM(tokens.shape, BF),
        pltpu.VMEM(back_project.shape, BF),
        pltpu.VMEM(weight.shape, BF),
        pltpu.VMEM(back_middle.shape, F32),
        pltpu.VMEM((images, block, width), BF),
        pltpu.VMEM((width, rows), BF),
        pltpu.VMEM((128, width), F32),
    ]
    scratch += [pltpu.VMEM((big_y, big_x, big_z, 2, shard, columns[1]), BF) for columns, _ in parts]

    def body(*refs):
        x_hbm, b_hbm, w_hbm, m_hbm, g_ref, two_ref, squares_ref = refs[:7]
        sum_ref, moved, total_ref, rest = refs[7], refs[8], refs[9], refs[10:]
        tally, slots, x_all, b_all, w_all, m_all, sent, normed_t, gain_rows = rest[n_fixed : n_fixed + 9]
        grads = rest[n_fixed + 9 :]
        net = Net(dims, *rest[:3])
        order = [other for other, _ in net.line("image")] + [net.image]
        load_w = net.local_copy(Part(w_hbm), Part(w_all))
        loads = []
        for chunk in order:
            at = pl.ds(pl.multiple_of(chunk * block, block), block)
            loads.append([net.local_copy(Part(a)[at, :], Part(b)[at, :]) for a, b in ((b_hbm, b_all), (x_hbm, x_all))])
            if len(loads) == 1:
                load_m = net.local_copy(Part(m_hbm), Part(m_all))
        net.greet(["z", "x", "y", "c", "image", "band", "img"])
        tally[...] = squares_ref[...]
        gain_rows[...] = jnp.zeros_like(gain_rows)
        gain_rows[1:2, :] = two_ref[0:1, :]
        load_w.wait()
        moves = []
        for place, chunk in enumerate(order):
            for load in loads[place]:
                load.wait()
            if place == 0:
                load_m.wait()
            at = pl.ds(pl.multiple_of(chunk * block, block), block)
            gain = g_ref[0:1, :]
            x = x_all[at, :].astype(F32)
            scale = inverse_rms(x)
            normed_t[:, place * block : (place + 1) * block] = jnp.transpose((x * scale * gain).astype(BF))
            into, rows_of_gain = norm_back(mm(b_all[at, :], w_all[:, : 3 * width], 1, 1), x, scale, gain)
            sent[chunk] = (m_all[at, :] + into).astype(BF)
            gain_rows[0:1, :] += jnp.sum(rows_of_gain, 0, keepdims=True)
            if place < images - 1:
                moves.append(net.copy(Part(sent)[chunk], Part(moved)[net.image], net.line("image")[place][1]))
            else:
                own = net.local_copy(Part(sent)[chunk], Part(moved)[net.image])
        tasks = []
        for k, (columns, turn) in enumerate(parts):
            buffers = rest[3 + 5 * k : 8 + 5 * k]
            for low in range(columns[0], min(columns[0] + columns[1], 3 * width), tile):
                total = jnp.zeros((width, tile), F32)
                for place, chunk in enumerate(order):
                    at = pl.ds(pl.multiple_of(chunk * block, block), block)
                    inner = slice(place * block, (place + 1) * block)
                    total = total + mm(normed_t[:, inner], b_all[at, low : low + tile], 1, 0)
                into = slice(low - columns[0], low - columns[0] + tile)
                grads[k][..., into] = total.astype(BF).reshape(grads[k].shape[:5] + (tile,))
            if k == len(parts) - 1:
                turned = jnp.transpose(gain_rows[...]).astype(BF)
                grads[k][..., columns[1] - 128 :] = turned.reshape(grads[k].shape[:5] + (128,))
            task = scatter(net, grads[k], *buffers, sum_ref, tally, (0, columns[1]), turn, columns[0])
            next(task)
            tasks.append((0, task))
        drive(tasks)
        sum_tiles(net, tally, slots)
        total_ref[...] = jnp.broadcast_to(jnp.sum(tally[...], keepdims=True), (8, 128))
        for move in moves:
            move.wait_recv()
        own.wait()
        for move in moves:
            move.wait_send()

    vmem = pl.BlockSpec(memory_space=pltpu.VMEM)
    shapes = [
        jax.ShapeDtypeStruct((shard, 3 * width + 128), F32),
        jax.ShapeDtypeStruct((images, block, width), BF),
        jax.ShapeDtypeStruct((8, 128), F32),
    ]
    return pl.pallas_call(
        body,
        out_shape=shapes,
        in_specs=[ANY] * 4 + [vmem] * 3,
        out_specs=[vmem, ANY, vmem],
        scratch_shapes=scratch,
        compiler_params=pltpu.CompilerParams(
            collective_id=number, has_side_effects=True, vmem_limit_bytes=61 * MIB
        ),
        name="finale",
    )(tokens, back_project, weight, back_middle, gains, gain_two_grad, squares)


def whole(shape):
    return pl.BlockSpec(shape, lambda i: (0,) * len(shape))


def kept(shape):
    return pl.BlockSpec(shape, lambda i: (0,) * len(shape), pipeline_mode=pl.Buffered(1))


def inverse_rms(value):
    return lax.rsqrt(jnp.mean(value * value, -1, keepdims=True) + EPS)


def mm(a, b, ca, cb):
    return lax.dot_general(a, b, (((ca,), (cb,)), ((), ())), preferred_element_type=F32)


def at_turn(turn, events):
    def visit(whens):
        if len(whens) == 1:

            @pl.when(turn == whens[0])
            def _():
                for task in events[whens[0]]:
                    next(task, None)

        elif whens:
            middle = len(whens) // 2

            @pl.when(turn < whens[middle])
            def _():
                visit(whens[:middle])

            @pl.when(turn >= whens[middle])
            def _():
                visit(whens[middle:])

    visit(sorted(events))


def schedule(tasks, turns, last):
    events, tail = {}, []
    for task, when in zip(tasks, turns):
        for turn in when:
            if turn < last:
                events.setdefault(turn, []).append(task)
            else:
                tail.append(task)
    return events, tail


def lanes_of(h):
    lane = lax.broadcasted_iota(jnp.int32, (1, PAIR), 1) < HEAD_DIM
    return lane if h == 0 else ~lane


def attend(dims, number, tokens, weight, bias, block, weights, chunks):
    big_y, big_x, big_z, share = dims
    rows, width = tokens.shape
    pairs = width // PAIR
    others = share - 1
    blocks = 4
    n = len(weights)
    last = LEAD + 4 * pairs
    parts = [
        (j, columns, GATHER_TURNS[group])
        for j, w in enumerate(weights)
        for group, columns in enumerate(pieces(w.shape[1], GATHER_SHARES))
    ]
    copies = len(parts) * gather_copies(dims) + others * 2 * pairs + chunks.shape[0] - 1

    def body(*refs):
        x_ref, w_ref, bias_ref, chunks_in = refs[:4]
        blocks_in, refs = refs[4 : 4 + n], refs[4 + n :]
        o_ref, l_ref, kv_out, chunks_out, project_ref, gains_ref, refs = refs[:6] + (refs[6:],)
        gathered, (kv_held, send, recv, local) = refs[:n], refs[n:]
        h = pl.program_id(0)
        net = Net(dims, send, recv, local)

        def move_keys(j):
            moves = []
            for slot, (_, target) in enumerate(net.line("share")):
                source = Part(project_ref)[:, pl.ds(width + PAIR * j, PAIR)]
                moves.append(net.plan(source, Part(kv_held)[others - 1 - slot, j], target))
            return moves

        key_moves = [move_keys(j) for j in range(2 * pairs)]
        keep = Move(Part(kv_held), Part(kv_out), None, local, len(parts) + 1, None)
        tasks = [gather(net, blocks_in[j], gathered[j], columns) for j, columns, _ in parts]
        tasks.append(exchange_images(net, chunks_in, chunks_out))
        turns = [turn for _, _, turn in parts] + [CHUNK_TURNS]
        events, tail = schedule(tasks, turns, last)

        @pl.when(h == 0)
        def _():
            net.greet(["z", "x", "y", "c", "image"] + (["share"] if share > 2 else []))
            gains_ref[...] = jnp.transpose(w_ref[:, 3 * width :].astype(F32))[:8]

        @pl.when(h == 0)
        def _():
            def row_step(i, _):
                at_turn(i, {t: e for t, e in events.items() if t < LEAD})
                at = pl.ds(pl.multiple_of(i * block, block), block)
                x = x_ref[at, :].astype(F32)
                normed = (x * inverse_rms(x) * gains_ref[0:1, :]).astype(BF)
                project_ref[at, :] = mm(normed, w_ref[:, : 3 * width], 1, 0).astype(BF)
                return 0

            lax.fori_loop(0, blocks, row_step, 0)
            for j in range(pairs):
                for move in key_moves[j] + key_moves[j + pairs]:
                    move.start()

        for j in range(pairs):

            @pl.when(h == j)
            def _(j=j):
                for move in key_moves[j] + key_moves[j + pairs]:
                    move.wait_recv()
                if j == pairs - 1:
                    keep.start()

        def own(first):
            return pl.ds(pl.multiple_of((h + first) * PAIR, PAIR), PAIR)

        def step(i, _):
            at_turn(LEAD + h * 4 + i, {t: e for t, e in events.items() if t >= LEAD})
            at = pl.ds(pl.multiple_of(i * block, block), block)
            k = jnp.concatenate([project_ref[:, own(pairs)]] + [kv_held[s, h] for s in range(others)], 0)
            v = jnp.concatenate(
                [project_ref[:, own(2 * pairs)]] + [kv_held[s, h + pairs] for s in range(others)], 0
            )
            q = project_ref[at, own(0)] * jnp.asarray(SCALE, BF)
            mixed, logs = [], []
            for half in range(2):
                scores = mm(jnp.where(lanes_of(half), q, jnp.zeros_like(q)), k, 1, 1) + bias_ref[...]
                highest = jnp.max(scores, -1, keepdims=True)
                powers = jnp.exp(scores - highest)
                total = jnp.sum(powers, -1, keepdims=True)
                mixed.append(mm(powers.astype(BF), v, 1, 0) / total)
                logs.append(highest + jnp.log(total))
            o_ref[at, :] = jnp.where(lanes_of(0), mixed[0], mixed[1]).astype(BF)
            l_ref[at, :] = jnp.where(lanes_of(0), logs[0], logs[1])
            return 0

        lax.fori_loop(0, blocks, step, 0)

        @pl.when(h == pairs - 1)
        def _():
            for task in tail:
                next(task, None)
            for moves in key_moves:
                for move in moves:
                    move.wait_send()
            keep.wait()

    column = lambda first: pl.BlockSpec((rows, PAIR), lambda h: (0, h + first))
    keys = rows * share
    shapes = [
        jax.ShapeDtypeStruct((rows, width), BF),
        jax.ShapeDtypeStruct((rows, width), F32),
        jax.ShapeDtypeStruct((others, 2 * pairs, rows, PAIR), BF),
        jax.ShapeDtypeStruct(chunks.shape, chunks.dtype),
        jax.ShapeDtypeStruct((rows, 3 * width), BF),
        jax.ShapeDtypeStruct((8, width), F32),
    ] + [jax.ShapeDtypeStruct((big_y, big_x, big_z, 2) + w.shape, w.dtype) for w in weights]
    return pl.pallas_call(
        body,
        grid=(pairs,),
        in_specs=[kept(tokens.shape), kept(weight.shape), kept((1, keys))] + [ANY] * (1 + n),
        out_specs=[column(0), column(0), ANY, ANY, kept((rows, 3 * width)), kept((8, width))] + [ANY] * n,
        out_shape=shapes,
        scratch_shapes=[
            pltpu.VMEM((others, 2 * pairs, rows, PAIR), BF),
            sems(copies),
            sems(copies),
            sems(len(parts) + 2),
        ],
        compiler_params=pltpu.CompilerParams(
            collective_id=number, has_side_effects=True, vmem_limit_bytes=60 * MIB
        ),
        cost_estimate=pl.CostEstimate(
            flops=16 * rows * keys * width, bytes_accessed=8 * keys * width, transcendentals=rows * keys * HEADS
        ),
        name="attend",
    )(tokens, weight, bias, chunks, *weights)


LEAD = 4
GATHER_SHARES = (1, 2, 2, 2, 2, 1)
GATHER_TURNS = (
    (0, 4, 7, 12, 14),
    (0, 7, 12, 16, 20),
    (1, 10, 16, 21, 24),
    (2, 14, 21, 25, 28),
    (3, 17, 24, 28, 28),
    (5, 20, 27, 28, 28),
)
CHUNK_TURNS = (14, 28)
SCATTER_TURNS = (
    ((2, 5, 13, 20, 24),),
    ((0, 2, 8, 15, 21), (0, 3, 10, 17, 23)),
    ((1, 4, 12, 19, 24),),
)
RESULT_TURNS = (0, 24)


def attend_back(dims, number, project, kv, bias, mixed, logs, back, block, grads, chunks):
    big_y, big_x, big_z, share = dims
    rows, width = mixed.shape
    pairs = width // PAIR
    others = share - 1
    blocks = 4
    keys = rows * share
    n = len(grads)
    parts = [
        (j, (low + first, wide), order, SCATTER_TURNS[j][group])
        for j, g in enumerate(grads)
        for group, (first, width_of) in enumerate(pieces(g.shape[5], (1,) * len(SCATTER_TURNS[j])))
        for (low, wide), order in halves(width_of)
    ]
    copies = len(parts) * scatter_copies(dims) + others * 2 * pairs + chunks.shape[0] - 1

    def body(*refs):
        q_ref, k_ref, v_ref, k_other, v_other, bias_ref, mixed_ref, logs_ref, back_ref = refs[:9]
        grads_in, chunks_in, refs = refs[9 : 9 + n], refs[9 + n], refs[10 + n :]
        out_ref, sums, squares, chunks_out, refs = refs[0], refs[1 : 1 + n], refs[1 + n], refs[2 + n], refs[3 + n :]
        dk_sums, dv_sums, parted, arrived, bias_column = refs[:5]
        send, recv, local = refs[5:8]
        buffers = refs[8:]
        h = pl.program_id(0)
        net = Net(dims, send, recv, local)

        def move_keys(j):
            moves = []
            for slot, (_, target) in enumerate(net.line("share")):
                moves.append(net.plan(Part(parted)[slot, j], Part(arrived)[others - 1 - slot, j], target))
            return moves

        key_moves = [move_keys(j) for j in range(2 * pairs)]
        tasks = [
            scatter(net, grads_in[j], *buffers[5 * k : 5 * k + 5], sums[j], squares, columns, order)
            for k, (j, columns, order, _) in enumerate(parts)
        ]
        tasks.append(exchange_images(net, chunks_in, chunks_out))
        turns = [turn for _, _, _, turn in parts] + [RESULT_TURNS]
        events, tail = schedule(tasks, turns, 4 * pairs)

        @pl.when(h == 0)
        def _():
            net.greet(["z", "x", "y", "c", "image"] + (["share"] if share > 2 else []))
            squares[...] = jnp.zeros_like(squares)
            bias_column[...] = jnp.transpose(jnp.broadcast_to(bias_ref[...], (PAIR, keys)))

        turn = lax.rem(h, 2)
        dk_sums[turn] = jnp.zeros((keys, PAIR), F32)
        dv_sums[turn] = jnp.zeros((keys, PAIR), F32)

        def step(i, _):
            at_turn(h * 4 + i, events)
            at = pl.ds(pl.multiple_of(i * block, block), block)
            k = jnp.concatenate([k_ref[...]] + [k_other[s, 0] for s in range(others)], 0)
            v = jnp.concatenate([v_ref[...]] + [v_other[s, 0] for s in range(others)], 0)
            q, do = q_ref[at, :] * jnp.asarray(SCALE, BF), back_ref[at, :]
            lse = jnp.transpose(logs_ref[at, :])
            products = jnp.transpose(do.astype(F32) * mixed_ref[at, :].astype(F32))
            dqs, dks, dvs = [], [], []
            mask = jnp.concatenate([bias_column[...]] * (block // PAIR), 1)
            for half in range(2):
                low, high = half * HEAD_DIM, (half + 1) * HEAD_DIM
                q_h = jnp.where(lanes_of(half), q, jnp.zeros_like(q))
                do_h = jnp.where(lanes_of(half), do, jnp.zeros_like(do))
                row_dots = jnp.sum(products[low:high, :], 0, keepdims=True)
                chances = jnp.exp(mm(k, q_h, 1, 1) + mask - lse[low : low + 1, :])
                slopes = mm(v, do_h, 1, 1)
                scores = (chances * (slopes - row_dots)).astype(BF)
                dqs.append(mm(scores, k, 0, 0))
                dks.append(mm(scores, q_h, 1, 0))
                dvs.append(mm(chances.astype(BF), do_h, 1, 0))
            dq = (jnp.where(lanes_of(0), dqs[0], dqs[1]) * SCALE).astype(BF)
            out_ref[at, pl.ds(pl.multiple_of(h * PAIR, PAIR), PAIR)] = dq
            dk_sums[turn] += dks[0] + dks[1]
            dv_sums[turn] += dvs[0] + dvs[1]
            return 0

        lax.fori_loop(0, blocks, step, 0)

        def finish(j):
            for move in key_moves[j] + key_moves[j + pairs]:
                move.wait_recv()
            for kept, sums_of in ((j, dk_sums), (j + pairs, dv_sums)):
                value = sums_of[j % 2, 0:rows, :]
                for slot in range(others):
                    value = value + arrived[slot, kept].astype(F32)
                out_ref[:, width + PAIR * kept : width + PAIR * (kept + 1)] = value.astype(BF)

        for j in range(pairs):

            @pl.when(h == j)
            def _(j=j):
                if j > 0:
                    finish(j - 1)
                for slot in range(others):
                    away = slice(rows * (slot + 1), rows * (slot + 2))
                    parted[slot, j] = dk_sums[j % 2, away, :].astype(BF)
                    parted[slot, j + pairs] = dv_sums[j % 2, away, :].astype(BF)
                for move in key_moves[j] + key_moves[j + pairs]:
                    move.start()
                if j == pairs - 1:
                    for task in tail:
                        next(task, None)
                    finish(j)
                    for moves in key_moves:
                        for move in moves:
                            move.wait_send()

    column = lambda first: pl.BlockSpec((rows, PAIR), lambda h: (0, h + first))
    other = lambda first: pl.BlockSpec((others, 1, rows, PAIR), lambda h: (0, h + first, 0, 0))
    whole = lambda shape: pl.BlockSpec(shape, lambda h: (0,) * len(shape))
    shard = grads[0].shape[4] if n else 0
    shapes = (
        [jax.ShapeDtypeStruct((rows, 3 * width), BF)]
        + [jax.ShapeDtypeStruct((shard, g.shape[5]), F32) for g in grads]
        + [jax.ShapeDtypeStruct((8, 128), F32)]
    )
    moved = jax.ShapeDtypeStruct(chunks.shape, chunks.dtype)
    scratch = [
        pltpu.VMEM((2, keys, PAIR), F32),
        pltpu.VMEM((2, keys, PAIR), F32),
        pltpu.VMEM((others, 2 * pairs, rows, PAIR), BF),
        pltpu.VMEM((others, 2 * pairs, rows, PAIR), BF),
        pltpu.VMEM((keys, PAIR), F32),
        sems(copies),
        sems(copies),
        sems(len(parts) + 1),
    ]
    for _, columns, order, _ in parts:
        scratch += scatter_scratch(dims, shard, columns, order)
    return pl.pallas_call(
        body,
        grid=(pairs,),
        in_specs=[
            column(0),
            column(pairs),
            column(2 * pairs),
            other(0),
            other(pairs),
            whole((1, keys)),
            column(0),
            column(0),
            column(0),
        ]
        + [ANY] * (n + 1),
        out_specs=[whole(s.shape) for s in shapes] + [ANY],
        out_shape=shapes + [moved],
        scratch_shapes=scratch,
        compiler_params=pltpu.CompilerParams(
            collective_id=number, has_side_effects=True, vmem_limit_bytes=60 * MIB
        ),
        cost_estimate=pl.CostEstimate(
            flops=40 * rows * keys * width, bytes_accessed=16 * keys * width, transcendentals=rows * keys * HEADS
        ),
        name="attend_back",
    )(project, project, project, kv, kv, bias, mixed, logs, back, *grads, chunks)


def norm_back(back, value, scale, gain):
    scaled = back * gain
    inner = jnp.mean(scaled * value, -1, keepdims=True)
    return scale * scaled - value * (scale * scale * scale * inner), back * (value * scale)


GELU_A = 0.7978845608028654
GELU_B = 0.044715


def mlp_call(tokens, attended, cotangent, keep, weights, gains, block):
    rows, width = tokens.shape
    hidden_units = (weights.shape[1] - width) // 3
    steps = rows // block
    tile = 1024
    in_tiles, down_tiles = 2 * hidden_units // tile, hidden_units // tile
    part = 1024

    def body(
        x_ref, a_ref, c_ref, keep_ref, w_ref, g_ref,
        result_ref, middle_ref, back_ref, gain_ref, g_out_ref, g_in_ref, g_down_ref,
        normed_t, low_t, branch_t, mixed, hidden, back_gu,
    ):
        i = pl.program_id(0)
        wo_ref = w_ref.at[:, :width]
        wi_ref = w_ref.at[:, width : width + 2 * hidden_units]
        wd_ref = w_ref.at[:, width + 2 * hidden_units :]

        @pl.when(i == 0)
        def _():
            gain_ref[...] = jnp.zeros_like(gain_ref)

        @pl.when(i < steps)
        def _():
            at = pl.ds(pl.multiple_of(i * block, block), block)
            gain = g_ref[1:2, :]
            a = a_ref[...]
            mixed[at, :] = a
            middle = x_ref[...].astype(F32) + mm(a, wo_ref[...], 1, 1)
            scale = inverse_rms(middle)
            normed = (middle * scale * gain).astype(BF)
            normed_t[:, at] = jnp.transpose(normed)
            back_result = keep_ref[...] * c_ref[...].astype(F32)
            low = back_result.astype(BF)
            low_t[:, at] = jnp.transpose(low)
            result, back = middle, jnp.zeros_like(middle)
            for p in range(hidden_units // part):
                one = slice(p * part, (p + 1) * part)
                two = slice(hidden_units + p * part, hidden_units + (p + 1) * part)
                gate = mm(normed, wi_ref[:, one], 1, 0)
                up = mm(normed, wi_ref[:, two], 1, 0)
                back_hidden = mm(low, wd_ref[:, one], 1, 0)
                square = gate * gate
                bend = jnp.tanh(GELU_A * (gate + GELU_B * (gate * square)))
                half = 0.5 + 0.5 * bend
                curve = gate * half
                slope = half + (0.5 * GELU_A) * gate * (1.0 - bend * bend) * (1.0 + (3.0 * GELU_B) * square)
                hid = (curve * up).astype(BF)
                back_gate = (back_hidden * up * slope).astype(BF)
                back_up = (back_hidden * curve).astype(BF)
                hidden[at, one] = hid
                back_gu[at, one] = back_gate
                back_gu[at, two] = back_up
                result = result + mm(hid, wd_ref[:, one], 1, 1)
                back = back + mm(back_gate, wi_ref[:, one], 1, 1) + mm(back_up, wi_ref[:, two], 1, 1)
            result_ref[...] = (keep_ref[...] * result).astype(BF)
            into, gain_rows = norm_back(back, middle, scale, gain)
            gain_ref[0:1, :] += jnp.sum(gain_rows, 0, keepdims=True)
            back_middle = back_result + into
            middle_ref[...] = back_middle
            branch = back_middle.astype(BF)
            branch_t[:, at] = jnp.transpose(branch)
            back_ref[...] = mm(branch, wo_ref[...], 1, 0).astype(BF)

        @pl.when(i == steps)
        def _():
            g_out_ref[...] = mm(branch_t[...], mixed[...], 1, 0).astype(BF)

        for t in range(in_tiles):

            @pl.when(i == steps + 1 + t)
            def _(t=t):
                g_in_ref[...] = mm(normed_t[...], back_gu[:, t * tile : (t + 1) * tile], 1, 0).astype(BF)

        for t in range(down_tiles):

            @pl.when(i == steps + 1 + in_tiles + t)
            def _(t=t):
                g_down_ref[...] = mm(low_t[...], hidden[:, t * tile : (t + 1) * tile], 1, 0).astype(BF)

    row = lambda last: pl.BlockSpec((block, last), lambda i: (jnp.minimum(i, steps - 1), 0))
    return pl.pallas_call(
        body,
        grid=(steps + 1 + in_tiles + down_tiles,),
        in_specs=[
            row(width),
            row(width),
            row(width),
            row(1),
            kept(weights.shape),
            kept(gains.shape),
        ],
        out_specs=[
            row(width),
            row(width),
            row(width),
            whole((8, width)),
            whole((width, width)),
            pl.BlockSpec((width, tile), lambda i: (0, jnp.clip(i - steps - 1, 0, in_tiles - 1))),
            pl.BlockSpec((width, tile), lambda i: (0, jnp.clip(i - steps - 1 - in_tiles, 0, down_tiles - 1))),
        ],
        out_shape=[
            jax.ShapeDtypeStruct((rows, width), BF),
            jax.ShapeDtypeStruct((rows, width), F32),
            jax.ShapeDtypeStruct((rows, width), BF),
            jax.ShapeDtypeStruct((8, width), F32),
            jax.ShapeDtypeStruct((width, width), BF),
            jax.ShapeDtypeStruct((width, 2 * hidden_units), BF),
            jax.ShapeDtypeStruct((width, hidden_units), BF),
        ],
        scratch_shapes=[
            pltpu.VMEM((width, rows), BF),
            pltpu.VMEM((width, rows), BF),
            pltpu.VMEM((width, rows), BF),
            pltpu.VMEM((rows, width), BF),
            pltpu.VMEM((rows, hidden_units), BF),
            pltpu.VMEM((rows, 2 * hidden_units), BF),
        ],
        compiler_params=pltpu.CompilerParams(vmem_limit_bytes=61 * MIB),
        cost_estimate=pl.CostEstimate(
            flops=6 * rows * width * (width + 3 * hidden_units),
            bytes_accessed=8 * width * (width + 3 * hidden_units),
            transcendentals=rows * hidden_units,
        ),
        name="mlp",
    )(tokens, attended, cotangent, keep, weights, gains)


def finish_call(tokens, back_project, weight, back_middle, gains, gain_two_grad, block):
    rows, width = tokens.shape
    steps = rows // block
    tiles, tile = 3, width

    def body(x_ref, b_ref, w_ref, m_ref, g_ref, two_ref, out_ref, grad_ref, gain_ref, normed_t, held, gain_rows):
        i = pl.program_id(0)

        @pl.when(i == 0)
        def _():
            gain_rows[...] = jnp.zeros_like(gain_rows)
            gain_rows[1:2, :] = two_ref[0:1, :]

        @pl.when(i < steps)
        def _():
            at = pl.ds(pl.multiple_of(i * block, block), block)
            gain = g_ref[0:1, :]
            x = x_ref[...].astype(F32)
            scale = inverse_rms(x)
            normed_t[:, at] = jnp.transpose((x * scale * gain).astype(BF))
            back = b_ref[...]
            held[at, :] = back
            into, rows_of_gain = norm_back(mm(back, w_ref[:, : 3 * width], 1, 1), x, scale, gain)
            out_ref[...] = (m_ref[...] + into).astype(BF)
            gain_rows[0:1, :] += jnp.sum(rows_of_gain, 0, keepdims=True)

        for t in range(tiles):

            @pl.when(i == steps + t)
            def _(t=t):
                grad_ref[...] = mm(normed_t[...], held[:, t * tile : (t + 1) * tile], 1, 0).astype(BF)

        @pl.when(i == steps)
        def _():
            gain_ref[...] = jnp.transpose(gain_rows[...]).astype(BF)

    row = lambda last: pl.BlockSpec((block, last), lambda i: (jnp.minimum(i, steps - 1), 0))
    return pl.pallas_call(
        body,
        grid=(steps + tiles,),
        in_specs=[row(width), row(3 * width), kept(weight.shape), row(width), kept(gains.shape), kept((8, width))],
        out_specs=[
            row(width),
            pl.BlockSpec((width, tile), lambda i: (0, jnp.clip(i - steps, 0, tiles - 1))),
            whole((width, 128)),
        ],
        out_shape=[
            jax.ShapeDtypeStruct((rows, width), BF),
            jax.ShapeDtypeStruct((width, 3 * width), BF),
            jax.ShapeDtypeStruct((width, 128), BF),
        ],
        scratch_shapes=[
            pltpu.VMEM((width, rows), BF),
            pltpu.VMEM((rows, 3 * width), BF),
            pltpu.VMEM((128, width), F32),
        ],
        compiler_params=pltpu.CompilerParams(vmem_limit_bytes=48 * MIB),
        cost_estimate=pl.CostEstimate(
            flops=12 * rows * width * width, bytes_accessed=28 * width * width, transcendentals=rows
        ),
        name="finish",
    )(tokens, back_project, weight, back_middle, gains, gain_two_grad)


def adam_step(master, grad, first, second, factor, rate, decay):
    clipped = factor * grad
    first_new = BETA_ONE * first + (1.0 - BETA_ONE) * clipped
    second_new = BETA_TWO * second + (1.0 - BETA_TWO) * clipped * clipped
    corrected = first_new / (1.0 - BETA_ONE**STEP)
    spread = jnp.sqrt(second_new / (1.0 - BETA_TWO**STEP)) + ADAM_EPS
    master_new = master - rate * (corrected / spread + decay * master)
    return (master_new, first_new, second_new)


def adam_call(squares, grads, masters, firsts, seconds):
    shard, width = grads[0].shape[0], grads[0].shape[1] - 128

    def body(*refs):
        squares_ref, refs = refs[0], refs[1:]
        ins, norm_ref, outs = refs[:19], refs[19], refs[20:]
        norm = jnp.sqrt(squares_ref[0:1, :])
        norm_ref[0, 0] = norm[0, 0]
        factor = jnp.minimum(1.0, CLIP / norm[:, 0:1])
        for j in range(5):
            grad = ins[0][:, :width] if j == 0 else ins[0][:, width:] if j == 4 else ins[j][...]
            if j == 4:
                filled = jnp.concatenate([grad, jnp.zeros((128 - shard, 128), F32)], 0)
                grad = jnp.transpose(filled)[:2, :shard]
            made = adam_step(
                ins[4 + j][...], grad, ins[9 + j][...], ins[14 + j][...], factor, RATES[j], DECAYS[j]
            )
            for kind in range(3):
                outs[5 * kind + j][...] = made[kind]
            outs[15 + j][...] = made[0].astype(BF)

    shapes = [jax.ShapeDtypeStruct((1, 1), F32)]
    shapes += [jax.ShapeDtypeStruct(m.shape, F32) for _ in range(3) for m in masters]
    shapes += [jax.ShapeDtypeStruct(m.shape, BF) for m in masters]
    vmem = pl.BlockSpec(memory_space=pltpu.VMEM)
    return pl.pallas_call(
        body,
        out_shape=shapes,
        out_specs=[pl.BlockSpec(memory_space=pltpu.SMEM)] + [vmem] * 20,
        compiler_params=pltpu.CompilerParams(vmem_limit_bytes=60 * MIB),
        name="adam",
    )(squares, *grads, *masters, *firsts, *seconds)


def prepare_call(dims, counts, qkv, out_t, in_up, down_t, gains, rows, band_rows):
    share = dims[3]
    images = rows // band_rows
    shard, width = qkv.shape[0], out_t.shape[1]
    wide = in_up.shape[1]

    def body(counts_ref, qkv_ref, out_ref, in_ref, down_ref, gain_ref, early_ref, late_ref, keep_ref, bias_ref):
        early_ref[:, : 3 * width] = qkv_ref[...].astype(BF)
        filled = jnp.concatenate([gain_ref[...], jnp.zeros((2, 128 - shard), F32)], 1)
        filled = jnp.concatenate([filled, jnp.zeros((126, 128), F32)], 0)
        early_ref[:, 3 * width :] = jnp.transpose(filled)[:shard].astype(BF)
        late_ref[:, :width] = out_ref[...].astype(BF)
        late_ref[:, width : width + wide] = in_ref[...].astype(BF)
        late_ref[:, width + wide :] = down_ref[...].astype(BF)
        band = lax.axis_index("band")
        image, part = band // share, lax.rem(band, share)
        count = counts_ref[image]
        down = lax.broadcasted_iota(jnp.int32, (band_rows, 1), 0)
        along = lax.broadcasted_iota(jnp.int32, (1, band_rows), 1)
        for s in range(images):
            first = (s * share + part) * band_rows
            keep_ref[s * band_rows : (s + 1) * band_rows, :] = jnp.where(down + first < count, 1.0, 0.0)
            for other in range(share):
                first = (s * share + lax.rem(part + other, share)) * band_rows
                at = (other * images + s) * band_rows
                bias_ref[:, at : at + band_rows] = jnp.where(along + first < count, 0.0, NEG)

    vmem = pl.BlockSpec(memory_space=pltpu.VMEM)
    return pl.pallas_call(
        body,
        out_shape=[
            jax.ShapeDtypeStruct((shard, 3 * width + 128), BF),
            jax.ShapeDtypeStruct((shard, width + wide + down_t.shape[1]), BF),
            jax.ShapeDtypeStruct((rows, 1), F32),
            jax.ShapeDtypeStruct((1, share * rows), F32),
        ],
        in_specs=[pl.BlockSpec(memory_space=pltpu.SMEM)] + [vmem] * 5,
        out_specs=[vmem] * 4,
        compiler_params=pltpu.CompilerParams(vmem_limit_bytes=60 * MIB),
        name="prepare",
    )(counts, qkv, out_t, in_up, down_t, gains)


def grid_of(n_img):
    big_y = max(d for d in range(1, n_img + 1) if n_img % d == 0 and d * d <= n_img)
    return big_y, n_img // big_y


def on_device(
    patches,
    cotangent,
    valid_counts,
    qkv_master,
    out_master,
    in_master,
    down_master,
    gain_master,
    qkv_first,
    out_first,
    in_first,
    down_first,
    gain_first,
    qkv_second,
    out_second,
    in_second,
    down_second,
    gain_second,
):
    images, band_rows, width = patches.shape
    n_img, n_band = lax.axis_size("img"), lax.axis_size("band")
    share = n_band // images
    big_y, big_x = grid_of(n_img)
    dims = (big_y, big_x, n_band // 2, share)
    rows = images * band_rows
    shard = qkv_master.shape[0]
    own_comm = shard % 8 == 0 and big_y == big_x == 2
    both = ("img", "band")

    places = [[s * share + r for s in range(images)] for r in range(share)]

    def exchange(chunks):
        return lax.all_to_all(chunks, "band", 0, 0, axis_index_groups=places, tiled=True)

    def blocks_of(grads):
        return [g.reshape(dims[:3] + (2, shard, g.shape[1])) for g in grads]

    early, late, row_keep, bias = prepare_call(
        dims,
        valid_counts,
        qkv_master,
        jnp.transpose(out_master),
        in_master,
        jnp.transpose(down_master),
        gain_master,
        rows,
        band_rows,
    )
    if own_comm:
        w_early, tokens_low = gather_call(dims, "gather", 0, [early], patches)
        w_early = w_early.reshape(width, early.shape[1])
    else:
        w_early = lax.all_gather(early, both, axis=0, tiled=True)
        tokens_low = exchange(patches)
    tokens = tokens_low.reshape(rows, width)
    attended, log_sums, kv, cotangent_low, project, gain_rows, *late_all = attend(
        dims, 1, tokens, w_early, bias, rows // 4, [late] if own_comm else [], cotangent
    )
    if own_comm:
        w_late = late_all[0].reshape(width, late.shape[1])
    else:
        w_late = lax.all_gather(late, both, axis=0, tiled=True)

    result_low, back_middle, back_attended, gain_two_grad, *late_grads = mlp_call(
        tokens,
        attended,
        cotangent_low.reshape(rows, width),
        row_keep,
        w_late,
        gain_rows,
        min(256, rows),
    )
    result_low = result_low.reshape(images, band_rows, width)
    back_project, *late_sums, squares, output = attend_back(
        dims,
        2,
        project,
        kv,
        bias,
        attended,
        log_sums,
        back_attended,
        rows // 4,
        blocks_of(late_grads) if own_comm else [],
        result_low,
    )
    if not own_comm:
        late_sums = [lax.psum_scatter(g.astype(F32), both, scatter_dimension=0, tiled=True) for g in late_grads]
    if own_comm:
        qkv_sum, back_input, total = finale_call(
            dims, 3, tokens, back_project, w_early, back_middle, gain_rows, gain_two_grad, squares, images
        )
    else:
        back_rows, *early_grads = finish_call(
            tokens, back_project, w_early, back_middle, gain_rows, gain_two_grad, min(256, rows)
        )
        grad = jnp.concatenate([g.astype(F32) for g in early_grads], 1)
        qkv_sum = lax.psum_scatter(grad, both, scatter_dimension=0, tiled=True)
        back_input = exchange(back_rows.reshape(images, band_rows, width))
        squares = sum(jnp.sum(g * g) for g in late_sums + [qkv_sum])
        total = lax.psum(jnp.broadcast_to(squares, (8, 128)), both)
    out_sum, in_sum, down_sum = late_sums

    def turned(arrays):
        return [jnp.transpose(a) if j in (1, 3) else a for j, a in enumerate(arrays)]

    norm, *updated = adam_call(
        total,
        [qkv_sum, out_sum, in_sum, down_sum],
        turned([qkv_master, out_master, in_master, down_master, gain_master]),
        turned([qkv_first, out_first, in_first, down_first, gain_first]),
        turned([qkv_second, out_second, in_second, down_second, gain_second]),
    )
    updated = [a for kind in range(4) for a in turned(updated[5 * kind : 5 * kind + 5])]
    return (output, back_input, norm.reshape(())) + tuple(updated)


def solution(mesh):
    rows_split, columns_split = P(("img", "band"), None), P(None, ("img", "band"))
    weights = (rows_split, columns_split, rows_split, columns_split, columns_split)
    tokens = P("img", "band", None)
    return jax.shard_map(
        on_device,
        mesh=mesh,
        in_specs=(tokens, tokens, P("img")) + weights * 3,
        out_specs=(tokens, tokens, P()) + weights * 4,
        check_vma=False,
    )
```
